128 devices in a mesh: dp: 4 (over y), expert: 32 (over z, x, core).
Axes of the slice: x: 4, y: 4, z: 4, core: 2. Of those that a mesh axis runs over, the one named last changes fastest.
Arguments:
- tokens: bfloat16 [3072, 7168], P(('dp', 'expert')), may hold values from -6 to 6
- grad_out: bfloat16 [3072, 7168], P(('dp', 'expert')), may hold values from -6 to 6
- route_ids: int32 [3072, 8], P(('dp', 'expert')), may hold values from 0 to 127, all different within a row; in each aligned block of 24 rows (0 to 23, 24 to 47, ...) at most 2 rows name the same one
- route_weight: bfloat16 [3072, 8], P(('dp', 'expert')), may hold values from 0.049804688 to 1
- cluster_of: int32 [128], replicated, may hold values from 0 to 7, as said below
- gate_basis: bfloat16 [8, 512, 7168], P(None, 'expert', 'dp'), may hold values from -0.0625 to 0.0625
- up_basis: bfloat16 [8, 512, 7168], P(None, 'expert', 'dp'), may hold values from -0.0625 to 0.0625
- down_basis: bfloat16 [8, 512, 7168], P(None, 'expert', 'dp'), may hold values from -0.25 to 0.25
- gate_factor: bfloat16 [128, 512, 2048], P('expert', None, 'dp'), may hold values from -0.25 to 0.25
- up_factor: bfloat16 [128, 512, 2048], P('expert', None, 'dp'), may hold values from -0.25 to 0.25
- down_factor: bfloat16 [128, 2048, 512], P('expert', 'dp'), may hold values from -0.125 to 0.125
Outputs:
- grad_tokens: bfloat16 [3072, 7168], P(('dp', 'expert'))
- grad_route: float32 [3072, 8], P(('dp', 'expert'))
- grad_gate_basis: float32 [8, 512, 7168], P(None, 'expert', 'dp')
- grad_up_basis: float32 [8, 512, 7168], P(None, 'expert', 'dp')
- grad_down_basis: float32 [8, 512, 7168], P(None, 'expert', 'dp')
- grad_gate_factor: float32 [128, 512, 2048], P('expert', None, 'dp')
- grad_up_factor: float32 [128, 512, 2048], P('expert', None, 'dp')
- grad_down_factor: float32 [128, 2048, 512], P('expert', 'dp')
The draws below stay inside these ranges and needn't reach their ends.
Inputs may be any that keep to these rules, and one draw needn't show every extreme that they name: `route_ids`: each token names 8 different experts. Among the 24 tokens of one block no expert is named more than 2 times, and in every draw some expert is named exactly 2 times in some block. `cluster_of`: never falls from one expert to the next; all 4 experts of each group of 4 consecutive experts share one cluster; every cluster holds 1 to 13 such groups, and one holds exactly 13.
All inputs are finite; a program needn't handle non-finite values.
Results may differ from the reference program's by a relative error of at most 0.013.
Values may be sent and summed in bfloat16 or wider, within the bound.
A program may use at most 128 MiB of HBM per device.

```python
import math
import jax
import jax.numpy as jnp
import numpy as np
from jax import lax

D = 7168
F = 2048
K = 8
R = 512
EXP_DEV = 4
TOK_DEV = 24
EXPERTS = 128
CLUSTERS = 8
CLUSTER_MOST = 13
CAP = 2
TOKENS = 3072


def draw_cluster_of(key, part):
    key = jax.random.fold_in(key, 7)
    first_key, second_key = jax.random.split(key)
    groups = EXPERTS // EXP_DEV
    largest = jax.random.randint(first_key, (), 0, CLUSTERS)
    spare = groups - CLUSTER_MOST - (CLUSTERS - 1)
    picks = jax.random.randint(second_key, (spare,), 0, CLUSTERS - 1)
    picks = picks + (picks >= largest).astype(jnp.int32)
    counts = 1 + jnp.sum((picks[:, None] == jnp.arange(CLUSTERS, dtype=jnp.int32)[None, :]).astype(jnp.int32), axis=0)
    counts = jnp.where(jnp.arange(CLUSTERS, dtype=jnp.int32) == largest, CLUSTER_MOST, counts)
    ends = jnp.cumsum(counts)
    group_cluster = jnp.sum((jnp.arange(groups, dtype=jnp.int32)[:, None] >= ends[None, :]).astype(jnp.int32), axis=1)
    return jnp.repeat(group_cluster, EXP_DEV).astype(jnp.int32)


def levels(stream_key, dims, cuts, low, high):
    def one(axis_at, blocks):
        heights = jax.random.uniform(jax.random.fold_in(jax.random.fold_in(stream_key, 6), axis_at), (blocks,), jnp.float32, low / len(cuts), high / len(cuts))
        return jnp.repeat(jnp.exp(heights), dims[axis_at] // blocks).reshape((-1,) + (1,) * (len(dims) - axis_at - 1))

    gain = one(*cuts[0])
    for cut in cuts[1:]:
        gain = gain * one(*cut)
    return gain


def routed_block(key, own, number, rows, number_of, top, most, skew):
    ranking = jax.random.permutation(key, number_of)
    heavy_load, common = portions_of(number_of, rows * top, most, skew, True), portions_of(number_of, rows * top, most, skew, False)
    places = jnp.arange(number_of)

    def named(tallies, offset_by):
        used = int((tallies > 0).sum())
        fixed = max(1, used // 4)
        shifted = fixed + (places - fixed + offset_by * (used - fixed)) % max(1, number_of - fixed)
        return jnp.zeros((number_of,), jnp.int32).at[ranking[jnp.where(places < fixed, places, shifted)]].set(jnp.asarray(tallies, jnp.int32))

    tallies = jnp.where(number % 4 == 0, named(heavy_load, number // 4), named(common, number - number // 4 - 1))
    mixed = jax.random.permutation(jax.random.fold_in(own, 3), number_of)
    giver, receiver = mixed[0:number_of // 2 * 2:2], mixed[1:number_of // 2 * 2:2]
    room = jnp.minimum(tallies[giver] - 1, most - tallies[receiver]) // 2
    room = jnp.where((giver == ranking[0]) | (receiver == ranking[0]) | (tallies[receiver] == 0), 0, jnp.maximum(room, 0))
    shifted = jax.random.randint(jax.random.fold_in(own, 4), (number_of // 2,), 0, 1 << 20) % (room + 1)
    tallies = tallies.at[giver].add(-shifted).at[receiver].add(shifted)
    labels = jnp.searchsorted(jnp.cumsum(tallies), jnp.arange(rows * top), side="right").astype(jnp.int32)
    grid = labels.reshape(top, rows).T
    grid = grid[jax.random.permutation(jax.random.fold_in(own, 1), rows)]
    offset_by = jax.random.randint(jax.random.fold_in(own, 2), (rows, 1), 0, top)
    return jnp.take_along_axis(grid, (jnp.arange(top)[None, :] + offset_by) % top, axis=1)


def portions_of(amount, total, reach, lean, full):
    loads = [(1 << 20) // math.isqrt(standing ** lean) + 1 for standing in range(1, amount + 1)]
    largest = reach if full else min(reach, max(-(-total // amount), total * loads[0] // sum(loads)))
    least = 1 if total - largest >= amount - 1 else 0
    given, surplus = [largest] + [least] * (amount - 1), total - largest - least * (amount - 1)
    while surplus > 0:
        candidates = [i for i in range(1, amount) if given[i] < largest] or [i for i in range(1, amount) if given[i] < reach]
        pool, left = sum([loads[i] for i in candidates]), surplus
        for i in candidates:
            more = min(reach - given[i], max(1, left * loads[i] // pool), surplus)
            given[i] = given[i] + more
            surplus = surplus - more
    return np.array(given)


def noise(rng, shape, width, reach, shards=(), held_as=jnp.bfloat16):
    array = width * jax.random.normal(rng, shape, jnp.float32)
    if shards:
        array = array * levels(rng, shape, shards, -0.22, 0.18)
    return jnp.clip(array, -reach, reach).astype(held_as)


def setup_inputs(seed: int = 0) -> dict:
    keys = jax.random.split(jax.random.key(seed), 12)
    tokens = noise(keys[0], (TOKENS, D), 1.0, 6.0, ((0, 128),))
    grad_out = noise(keys[1], (TOKENS, D), 1.0, 6.0, ((0, 128),))
    route_ids_keys = jax.random.split(jax.random.fold_in(keys[2], 1), TOKENS // TOK_DEV)
    route_ids_turns = jax.random.permutation(jax.random.fold_in(keys[2], 3), TOKENS // TOK_DEV)
    route_ids = jax.vmap(lambda own, number: routed_block(jax.random.fold_in(keys[2], 2), own, number, TOK_DEV, EXPERTS, K, CAP, 2))(route_ids_keys, route_ids_turns).reshape((TOKENS, K))
    route_weight = jnp.clip(jnp.exp(math.log(1.0) - 2.9996462 * jax.random.uniform(keys[3], (TOKENS, K), jnp.float32) ** levels(keys[3], (TOKENS, K), ((0, 128),), -0.2, 0.2)), 0.049804688, 1.0).astype(jnp.bfloat16)
    cluster_of = draw_cluster_of(jax.random.fold_in(keys[11], 71), 0)
    gate_basis = noise(keys[5], (CLUSTERS, R, D), D ** -0.5, 0.0625, ((1, 32), (2, 4)))
    up_basis = noise(keys[6], (CLUSTERS, R, D), D ** -0.5, 0.0625, ((1, 32), (2, 4)))
    down_basis = noise(keys[7], (CLUSTERS, R, D), R ** -0.5, 0.25, ((1, 32), (2, 4)))
    gate_factor = noise(keys[8], (EXPERTS, R, F), R ** -0.5, 0.25, ((0, 32), (2, 4)))
    up_factor = noise(keys[9], (EXPERTS, R, F), R ** -0.5, 0.25, ((0, 32), (2, 4)))
    down_factor = noise(keys[10], (EXPERTS, F, R), F ** -0.5, 0.125, ((0, 32), (1, 4)))
    return {"tokens": tokens, "grad_out": grad_out, "route_ids": route_ids, "route_weight": route_weight, "cluster_of": cluster_of, "gate_basis": gate_basis, "up_basis": up_basis, "down_basis": down_basis, "gate_factor": gate_factor, "up_factor": up_factor, "down_factor": down_factor}


def rounded(value):
    return lax.optimization_barrier(value.astype(jnp.bfloat16))


def silu_pair(pre):
    sig = jax.nn.sigmoid(pre)
    return pre * sig, sig * (1.0 + pre * (1.0 - sig))


def reference(tokens, grad_out, route_ids, route_weight, cluster_of, gate_basis, up_basis, down_basis, gate_factor, up_factor, down_factor):
    blocks = TOKENS // TOK_DEV
    pairs = TOK_DEV * K
    block_ids = route_ids.reshape(blocks, pairs).astype(jnp.int32)
    matches = (block_ids[:, :, None] == jnp.arange(EXPERTS, dtype=jnp.int32)[None, None, :]).astype(jnp.int32)
    slot_rank = (jnp.sum(matches * jnp.cumsum(matches, axis=1), axis=2) - 1).astype(jnp.int32)
    block_index = jnp.broadcast_to(jnp.arange(blocks, dtype=jnp.int32)[:, None], (blocks, pairs))
    pair_index = jnp.arange(pairs, dtype=jnp.int32)[None, :]
    token_of = (block_index * TOK_DEV + pair_index // K).astype(jnp.int32)
    choice_of = jnp.broadcast_to(pair_index % K, (blocks, pairs)).astype(jnp.int32)
    table = jnp.full((EXPERTS, blocks, CAP), TOKENS, jnp.int32).at[block_ids, block_index, slot_rank].set(token_of)
    which = jnp.zeros((EXPERTS, blocks, CAP), jnp.int32).at[block_ids, block_index, slot_rank].set(choice_of)
    weights = jnp.zeros((EXPERTS, blocks, CAP), jnp.float32).at[block_ids, block_index, slot_rank].set(
        route_weight.reshape(blocks, pairs).astype(jnp.float32))
    tokens_pad = jnp.concatenate([tokens, jnp.zeros((1, D), tokens.dtype)], axis=0)
    grads_pad = jnp.concatenate([grad_out, jnp.zeros((1, D), grad_out.dtype)], axis=0)
    groups = EXPERTS // EXP_DEV
    fl = jnp.float32

    def group_step(carry, device):
        grad_tok, grad_rt, grad_bases = carry
        first = (device * EXP_DEV).astype(jnp.int32)
        token_index = lax.dynamic_slice_in_dim(table, first, EXP_DEV, 0).reshape(EXP_DEV, blocks * CAP)
        k_index = lax.dynamic_slice_in_dim(which, first, EXP_DEV, 0).reshape(EXP_DEV, blocks * CAP)
        slot_weight = lax.dynamic_slice_in_dim(weights, first, EXP_DEV, 0).reshape(EXP_DEV, blocks * CAP)
        cluster = cluster_of[first]
        x_rows = tokens_pad[token_index].astype(fl)
        dy_rows = grads_pad[token_index].astype(fl)
        gate_rows = gate_basis[cluster].astype(fl)
        up_rows = up_basis[cluster].astype(fl)
        down_rows = down_basis[cluster].astype(fl)
        gate_own = lax.dynamic_slice_in_dim(gate_factor, first, EXP_DEV, 0).astype(fl)
        up_own = lax.dynamic_slice_in_dim(up_factor, first, EXP_DEV, 0).astype(fl)
        down_own = lax.dynamic_slice_in_dim(down_factor, first, EXP_DEV, 0).astype(fl)
        rank_gate = rounded(jnp.einsum('emd,rd->emr', x_rows, gate_rows)).astype(fl)
        rank_up = rounded(jnp.einsum('emd,rd->emr', x_rows, up_rows)).astype(fl)
        gate_pre = jnp.einsum('emr,erf->emf', rank_gate, gate_own)
        up_pre = jnp.einsum('emr,erf->emf', rank_up, up_own)
        act, slope = silu_pair(gate_pre)
        hidden = rounded(act * up_pre).astype(fl)
        mixed = rounded(jnp.einsum('emf,efr->emr', hidden, down_own)).astype(fl)
        y_rows = jnp.einsum('emr,rd->emd', mixed, down_rows)
        dots = jnp.sum(y_rows * dy_rows, axis=2)
        upstream = rounded(slot_weight[:, :, None] * dy_rows).astype(fl)
        term_down = jnp.einsum('emr,emd->rd', mixed, upstream)
        grad_mixed = rounded(jnp.einsum('emd,rd->emr', upstream, down_rows)).astype(fl)
        grad_down_own = jnp.einsum('emf,emr->efr', hidden, grad_mixed)
        grad_hidden = jnp.einsum('emr,efr->emf', grad_mixed, down_own)
        grad_gate_pre = rounded(grad_hidden * up_pre * slope).astype(fl)
        grad_up_pre = rounded(grad_hidden * act).astype(fl)
        grad_gate_own = jnp.einsum('emr,emf->erf', rank_gate, grad_gate_pre)
        grad_up_own = jnp.einsum('emr,emf->erf', rank_up, grad_up_pre)
        grad_hg = rounded(jnp.einsum('emf,erf->emr', grad_gate_pre, gate_own)).astype(fl)
        grad_hu = rounded(jnp.einsum('emf,erf->emr', grad_up_pre, up_own)).astype(fl)
        term_gate = jnp.einsum('emr,emd->rd', grad_hg, x_rows)
        term_up = jnp.einsum('emr,emd->rd', grad_hu, x_rows)
        grad_x = rounded(jnp.einsum('emr,rd->emd', grad_hg, gate_rows) + jnp.einsum('emr,rd->emd', grad_hu, up_rows)).astype(fl)
        terms = rounded(jnp.stack([term_gate, term_up, term_down])).astype(fl)
        grad_bases = grad_bases.at[cluster].add(terms)
        flat_index = token_index.reshape(-1)
        grad_tok = grad_tok.at[flat_index].add(grad_x.reshape(-1, D))
        grad_rt = grad_rt.at[flat_index, k_index.reshape(-1)].add(dots.reshape(-1))
        return (grad_tok, grad_rt, grad_bases), (grad_gate_own, grad_up_own, grad_down_own)

    start = (jnp.zeros((TOKENS + 1, D), jnp.float32), jnp.zeros((TOKENS + 1, K), jnp.float32),
             jnp.zeros((CLUSTERS, 3, R, D), jnp.float32))
    carry, owned = lax.scan(group_step, start, jnp.arange(groups, dtype=jnp.int32))
    grad_tok, grad_rt, grad_bases = carry
    grad_gate_factor = owned[0].reshape(EXPERTS, R, F)
    grad_up_factor = owned[1].reshape(EXPERTS, R, F)
    grad_down_factor = owned[2].reshape(EXPERTS, F, R)
    return (grad_tok[:TOKENS].astype(jnp.bfloat16), grad_rt[:TOKENS], grad_bases[:, 0], grad_bases[:, 1],
            grad_bases[:, 2], grad_gate_factor, grad_up_factor, grad_down_factor)
```

```python
import jax
import jax.numpy as jnp
from jax import lax
from jax.experimental import pallas as pl
from jax.experimental.pallas import tpu as pltpu
from jax.sharding import PartitionSpec as P

FL = jnp.float32
BF = jnp.bfloat16
MIB = 1024 * 1024


def dot(a, b, ca, cb):
    return lax.dot_general(a, b, (((ca,), (cb,)), ((), ())), preferred_element_type=FL)


def one_hot(slot_ref, j, tokens):
    row = slot_ref[pl.ds(j, 1), :]
    lanes = row.shape[1]
    grid = lax.broadcasted_iota(jnp.int32, (tokens, lanes), 0)
    return jnp.where(grid == row, 1.0, 0.0).astype(BF)


def pick_kernel(cluster, rows, slots, weights, out):
    groups, tokens, rank = out.shape[0], rows.shape[2], out.shape[3]

    def step(j, carry):
        c = cluster[j]
        own = rows[:, pl.ds(pl.multiple_of(c * rank, rank), rank), :].reshape(3 * rank, tokens)
        got = dot(own, one_hot(slots, j, tokens), 1, 0).reshape(3, rank, -1)
        got = jnp.concatenate([got[:2], got[2:] * weights[pl.ds(j, 1), :]], axis=0).astype(BF)
        half = got.shape[2] // 2
        out[j, 0] = got[:, :, :half]
        out[j, 1] = got[:, :, half:]
        return carry

    lax.fori_loop(0, groups, step, 0)


def pick(cluster, rows, slots, weights, rank):
    groups, lanes = slots.shape
    vmem = pl.BlockSpec(memory_space=pltpu.VMEM)
    return pl.pallas_call(
        pick_kernel,
        out_shape=jax.ShapeDtypeStruct((groups, 2, 3, rank, lanes // 2), BF),
        in_specs=[pl.BlockSpec(memory_space=pltpu.SMEM), vmem, vmem, vmem],
        out_specs=vmem,
        name="pick",
        compiler_params=pltpu.CompilerParams(vmem_limit_bytes=40 * MIB),
    )(cluster, rows, slots, weights)


def combine_kernel(cluster, parts, slots, weights, out, total):
    groups, rank, tokens = parts.shape[1], parts.shape[4], out.shape[2]
    total[...] = jnp.zeros_like(total)

    def step(j, carry):
        c = cluster[j]
        got = parts[0, j].astype(FL)
        for i in range(1, parts.shape[0]):
            got = got + parts[i, j].astype(FL)
        got = jnp.concatenate([got[0], got[1]], axis=2)
        got = jnp.concatenate([got[:2], got[2:] * weights[pl.ds(j, 1), :]], axis=0)
        got = got.astype(BF).reshape(3 * rank, -1)
        add = dot(got, one_hot(slots, j, tokens), 1, 1).reshape(3, rank, tokens)
        total[:, pl.ds(pl.multiple_of(c * rank, rank), rank), :] += add
        return carry

    lax.fori_loop(0, groups, step, 0)
    out[...] = total[...].astype(BF)


def combine(cluster, parts, slots, weights, clusters, tokens):
    rank = parts.shape[4]
    vmem = pl.BlockSpec(memory_space=pltpu.VMEM)
    shape = (3, clusters * rank, tokens)
    return pl.pallas_call(
        combine_kernel,
        out_shape=jax.ShapeDtypeStruct(shape, BF),
        in_specs=[pl.BlockSpec(memory_space=pltpu.SMEM), vmem, vmem, vmem],
        out_specs=vmem,
        scratch_shapes=[pltpu.VMEM(shape, FL)],
        name="combine",
        compiler_params=pltpu.CompilerParams(vmem_limit_bytes=40 * MIB),
    )(cluster, parts, slots, weights)


def mix(tiles):
    first, second = [], []
    for k in range(0, len(tiles), 2):
        a, b = tiles[k], tiles[k + 1]
        h = a.shape[-1] // 2
        first.append(jnp.concatenate([a[:, :h], b[:, :h]], axis=1))
        second.append(jnp.concatenate([a[:, h:], b[:, h:]], axis=1))
    return jnp.concatenate(first, axis=1), jnp.concatenate(second, axis=1)


def split_tiles(a):
    return [a[:, k : k + 128] for k in range(0, a.shape[1], 128)]


def expert_kernel(slots, gate, up, down, part, route, d_gate, d_up, d_down):
    rows = [mix(split_tiles(slots[0, k])) for k in range(3)]
    results = []
    for e in range(2):
        hg, hu, gm = rows[0][e], rows[1][e], rows[2][e]
        gf, uf, df = gate[e], up[e], down[e]
        gate_pre = dot(gf, hg, 0, 0)
        up_pre = dot(uf, hu, 0, 0)
        sig = 1.0 / (1.0 + jnp.exp(-gate_pre))
        act = gate_pre * sig
        slope = sig * (1.0 + gate_pre * (1.0 - sig))
        hidden = (act * up_pre).astype(BF)
        mixed = dot(df, hidden, 0, 0)
        grad_hidden = dot(df, gm, 1, 0)
        grad_gate_pre = (grad_hidden * up_pre * slope).astype(BF)
        grad_up_pre = (grad_hidden * act).astype(BF)
        route[0, e : e + 1] = jnp.sum(mixed * gm.astype(FL), axis=0, keepdims=True)
        d_down[e] = dot(hidden, gm, 1, 1)
        d_gate[e] = dot(hg, grad_gate_pre, 1, 1)
        d_up[e] = dot(hu, grad_up_pre, 1, 1)
        grad_hg = dot(gf, grad_gate_pre, 1, 0)
        grad_hu = dot(uf, grad_up_pre, 1, 0)
        results.append((grad_hg.astype(BF), grad_hu.astype(BF), mixed.astype(BF)))
    for k in range(3):
        tiles = []
        for a, b in zip(split_tiles(results[0][k]), split_tiles(results[1][k])):
            h = a.shape[-1] // 2
            tiles.append(jnp.concatenate([a[:, :h], b[:, :h]], axis=1))
            tiles.append(jnp.concatenate([a[:, h:], b[:, h:]], axis=1))
        part[0, k] = jnp.concatenate(tiles, axis=1)


def experts_step(slots, gate, up, down):
    count, rank, units = gate.shape
    lanes = slots.shape[3]

    def block(shape):
        return pl.BlockSpec((shape[0] // 2,) + shape[1:], lambda g: (g,) + (0,) * (len(shape) - 1))

    outs = [
        (slots.shape, BF),
        ((2, 2, lanes // 2), FL),
        (gate.shape, FL),
        (up.shape, FL),
        (down.shape, FL),
    ]
    return pl.pallas_call(
        expert_kernel,
        grid=(2,),
        out_shape=[jax.ShapeDtypeStruct(s, d) for s, d in outs],
        in_specs=[block(a.shape) for a in (slots, gate, up, down)],
        out_specs=[block(s) for s, _ in outs],
        name="experts_step",
        compiler_params=pltpu.CompilerParams(vmem_limit_bytes=56 * MIB),
    )(slots, gate, up, down)


def slot_tables(route_ids, route_weight, cells):
    flat = route_ids.reshape(-1)
    pairs = flat.shape[0]
    at = jnp.arange(pairs, dtype=jnp.int32)
    earlier = (flat[:, None] == flat[None, :]) & (at[None, :] < at[:, None])
    slot = jnp.sum(earlier.astype(jnp.int32), axis=1)
    placed = (flat * 2 + slot)[:, None] == jnp.arange(cells, dtype=jnp.int32)[None, :]
    token = at // route_ids.shape[1] + 1
    cell_token = jnp.sum(jnp.where(placed, token[:, None], 0), axis=0)
    cell_weight = jnp.sum(
        jnp.where(placed, route_weight.reshape(-1)[:, None].astype(FL), 0.0), axis=0
    )
    return placed, cell_token, cell_weight


def body(
    tokens,
    grad_out,
    route_ids,
    route_weight,
    cluster_of,
    gate_basis,
    up_basis,
    down_basis,
    gate_factor,
    up_factor,
    down_factor,
):
    n_dp = lax.axis_size("dp")
    n_ex = lax.axis_size("expert")
    tok_rows, width = tokens.shape
    local = gate_factor.shape[0]
    lane_rows = local * 2
    cells = n_ex * lane_rows
    clusters, rank, part_width = gate_basis.shape
    plane_tokens = n_ex * tok_rows
    all_rank = n_ex * rank

    placed, cell_token, cell_weight = slot_tables(route_ids, route_weight, cells)
    table = jnp.concatenate([cell_token.astype(FL), cell_weight]).reshape(4, 128)
    tables = lax.all_gather(table, "expert").reshape(n_ex, 2, n_ex, local, 2)
    tables = tables.transpose(1, 2, 3, 0, 4).reshape(2, n_ex, n_ex * lane_rows)
    block = (jnp.arange(n_ex * lane_rows, dtype=jnp.int32) // 2) % n_ex
    named = tables[0].astype(jnp.int32)
    slots = jnp.where(named > 0, named - 1 + tok_rows * block[None, :], -1)
    weights = tables[1]
    cluster = cluster_of.reshape(n_ex, local)[:, 0]

    x_all = lax.all_gather(tokens, "expert", axis=0, tiled=True)
    dy_all = lax.all_gather(grad_out, "expert", axis=0, tiled=True)
    bases = jnp.stack([gate_basis, up_basis, down_basis]).reshape(3, clusters * rank, part_width)
    bases = lax.all_gather(bases, "dp", axis=2, tiled=True)
    gate_up = bases[:2].reshape(2 * clusters * rank, width)
    down = bases[2]
    first = dot(gate_up, x_all, 1, 1).astype(BF).reshape(2, clusters * rank, plane_tokens)
    back = dot(down, dy_all, 1, 1).astype(BF)[None]
    picked = pick(cluster, jnp.concatenate([first, back]), slots, weights, rank)

    sent = jnp.broadcast_to(picked[None], (n_dp,) + picked.shape)
    sent = sent.reshape((n_dp * n_ex,) + picked.shape[1:])
    got = lax.all_to_all(sent, ("dp", "expert"), split_axis=0, concat_axis=0, tiled=True)
    got = got.reshape(n_dp, n_ex, 2, 3, rank, -1).transpose(2, 3, 1, 4, 0, 5)
    got = got.reshape(2, 3, all_rank, -1)
    part, route, d_gate_factor, d_up_factor, d_down_factor = experts_step(
        got, gate_factor, up_factor, down_factor
    )

    home = part.reshape(2, 3, n_ex, rank, n_dp, -1).transpose(4, 2, 0, 1, 3, 5)
    home = home.reshape((n_dp * n_ex,) + picked.shape[1:])
    home = lax.all_to_all(home, ("dp", "expert"), split_axis=0, concat_axis=0, tiled=True)
    home = home.reshape((n_dp, n_ex) + picked.shape[1:])
    summed = combine(cluster, home, slots, weights, clusters, plane_tokens)

    dots = route.reshape(local, n_dp, n_ex, 2).transpose(1, 2, 0, 3).reshape(n_dp * n_ex, lane_rows)
    dots = lax.all_to_all(dots, ("dp", "expert"), split_axis=0, concat_axis=0, tiled=True)
    scores = jnp.sum(dots.reshape(n_dp, cells), axis=0)
    scores = scores / jnp.where(cell_weight > 0.0, cell_weight, 1.0)
    grad_route = jnp.sum(jnp.where(placed, scores[None, :], 0.0), axis=1).reshape(route_ids.shape)

    back_up = summed[:2].reshape(2 * clusters * rank, plane_tokens)
    grad_gate_up = dot(back_up, x_all, 1, 0).astype(BF).reshape(2, clusters * rank, width)
    grad_down = dot(summed[2], dy_all, 1, 0).astype(BF)[None]
    terms = jnp.concatenate([grad_gate_up, grad_down])
    terms = lax.psum_scatter(terms, "dp", scatter_dimension=2, tiled=True).astype(FL)
    grad_x = dot(back_up, gate_up, 0, 0).astype(BF)
    grad_tokens = lax.psum_scatter(grad_x, "expert", scatter_dimension=0, tiled=True)
    shape = gate_basis.shape
    return (
        grad_tokens,
        grad_route,
        terms[0].reshape(shape),
        terms[1].reshape(shape),
        terms[2].reshape(shape),
        d_gate_factor,
        d_up_factor,
        d_down_factor,
    )


def solution(mesh):
    rows = P(("dp", "expert"), None)
    basis = P(None, "expert", "dp")
    factor = P("expert", None, "dp")
    low = P("expert", "dp", None)
    in_specs = (rows, rows, rows, rows, P(), basis, basis, basis, factor, factor, low)
    out_specs = (rows, rows, basis, basis, basis, factor, factor, low)
    return jax.shard_map(body, mesh=mesh, in_specs=in_specs, out_specs=out_specs, check_vma=False)
```

```python
import jax
import jax.numpy as jnp
from jax import lax
from jax.experimental import pallas as pl
from jax.experimental.pallas import tpu as pltpu
from jax.sharding import PartitionSpec as P

FL = jnp.float32
BF = jnp.bfloat16
MIB = 1024 * 1024


def dot(a, b, ca, cb):
    return lax.dot_general(a, b, (((ca,), (cb,)), ((), ())), preferred_element_type=FL)


def one_hot(slot_ref, j, tokens):
    row = slot_ref[pl.ds(j, 1), :]
    lanes = row.shape[1]
    grid = lax.broadcasted_iota(jnp.int32, (tokens, lanes), 0)
    return jnp.where(grid == row, 1.0, 0.0).astype(BF)


def pick_kernel(cluster, rows, slots, weights, out):
    groups, tokens, rank = out.shape[0], rows.shape[2], out.shape[3]

    def step(j, carry):
        c = cluster[j]
        own = rows[:, pl.ds(pl.multiple_of(c * rank, rank), rank), :].reshape(3 * rank, tokens)
        got = dot(own, one_hot(slots, j, tokens), 1, 0).reshape(3, rank, -1)
        got = jnp.concatenate([got[:2], got[2:] * weights[pl.ds(j, 1), :]], axis=0).astype(BF)
        half = got.shape[2] // 2
        out[j, 0] = got[:, :, :half]
        out[j, 1] = got[:, :, half:]
        return carry

    lax.fori_loop(0, groups, step, 0)


def pick(cluster, rows, slots, weights, rank):
    groups, lanes = slots.shape
    vmem = pl.BlockSpec(memory_space=pltpu.VMEM)
    return pl.pallas_call(
        pick_kernel,
        out_shape=jax.ShapeDtypeStruct((groups, 2, 3, rank, lanes // 2), BF),
        in_specs=[pl.BlockSpec(memory_space=pltpu.SMEM), vmem, vmem, vmem],
        out_specs=vmem,
        name="pick",
        compiler_params=pltpu.CompilerParams(vmem_limit_bytes=40 * MIB),
    )(cluster, rows, slots, weights)


def combine_kernel(cluster, parts, slots, weights, out, total):
    groups, rank, tokens = parts.shape[1], parts.shape[4], out.shape[2]
    total[...] = jnp.zeros_like(total)

    def step(j, carry):
        c = cluster[j]
        got = parts[0, j].astype(FL)
        for i in range(1, parts.shape[0]):
            got = got + parts[i, j].astype(FL)
        got = jnp.concatenate([got[0], got[1]], axis=2)
        got = jnp.concatenate([got[:2], got[2:] * weights[pl.ds(j, 1), :]], axis=0)
        got = got.astype(BF).reshape(3 * rank, -1)
        add = dot(got, one_hot(slots, j, tokens), 1, 1).reshape(3, rank, tokens)
        total[:, pl.ds(pl.multiple_of(c * rank, rank), rank), :] += add
        return carry

    lax.fori_loop(0, groups, step, 0)
    out[...] = total[...].astype(BF)


def combine(cluster, parts, slots, weights, clusters, tokens):
    rank = parts.shape[4]
    vmem = pl.BlockSpec(memory_space=pltpu.VMEM)
    shape = (3, clusters * rank, tokens)
    return pl.pallas_call(
        combine_kernel,
        out_shape=jax.ShapeDtypeStruct(shape, BF),
        in_specs=[pl.BlockSpec(memory_space=pltpu.SMEM), vmem, vmem, vmem],
        out_specs=vmem,
        scratch_shapes=[pltpu.VMEM(shape, FL)],
        name="combine",
        compiler_params=pltpu.CompilerParams(vmem_limit_bytes=40 * MIB),
    )(cluster, parts, slots, weights)


def mix(tiles):
    first, second = [], []
    for k in range(0, len(tiles), 2):
        a, b = tiles[k], tiles[k + 1]
        h = a.shape[-1] // 2
        first.append(jnp.concatenate([a[:, :h], b[:, :h]], axis=1))
        second.append(jnp.concatenate([a[:, h:], b[:, h:]], axis=1))
    return jnp.concatenate(first, axis=1), jnp.concatenate(second, axis=1)


def split_tiles(a):
    return [a[:, k : k + 128] for k in range(0, a.shape[1], 128)]


def expert_kernel(slots, gate, up, down, part, route, d_gate, d_up, d_down):
    rows = [mix(split_tiles(slots[0, k])) for k in range(3)]
    results = []
    for e in range(2):
        hg, hu, gm = rows[0][e], rows[1][e], rows[2][e]
        gf, uf, df = gate[e], up[e], down[e]
        gate_pre = dot(gf, hg, 0, 0)
        up_pre = dot(uf, hu, 0, 0)
        sig = 1.0 / (1.0 + jnp.exp(-gate_pre))
        act = gate_pre * sig
        slope = sig * (1.0 + gate_pre * (1.0 - sig))
        hidden = (act * up_pre).astype(BF)
        mixed = dot(df, hidden, 0, 0)
        grad_hidden = dot(df, gm, 1, 0)
        grad_gate_pre = (grad_hidden * up_pre * slope).astype(BF)
        grad_up_pre = (grad_hidden * act).astype(BF)
        route[0, e : e + 1] = jnp.sum(mixed * gm.astype(FL), axis=0, keepdims=True)
        d_down[e] = dot(hidden, gm, 1, 1)
        d_gate[e] = dot(hg, grad_gate_pre, 1, 1)
        d_up[e] = dot(hu, grad_up_pre, 1, 1)
        grad_hg = dot(gf, grad_gate_pre, 1, 0)
        grad_hu = dot(uf, grad_up_pre, 1, 0)
        results.append((grad_hg.astype(BF), grad_hu.astype(BF), mixed.astype(BF)))
    for k in range(3):
        tiles = []
        for a, b in zip(split_tiles(results[0][k]), split_tiles(results[1][k])):
            h = a.shape[-1] // 2
            tiles.append(jnp.concatenate([a[:, :h], b[:, :h]], axis=1))
            tiles.append(jnp.concatenate([a[:, h:], b[:, h:]], axis=1))
        part[0, k] = jnp.concatenate(tiles, axis=1)


def experts_step(slots, gate, up, down):
    count, rank, units = gate.shape
    lanes = slots.shape[3]

    def block(shape):
        return pl.BlockSpec((shape[0] // 2,) + shape[1:], lambda g: (g,) + (0,) * (len(shape) - 1))

    outs = [
        (slots.shape, BF),
        ((2, 2, lanes // 2), FL),
        (gate.shape, FL),
        (up.shape, FL),
        (down.shape, FL),
    ]
    return pl.pallas_call(
        expert_kernel,
        grid=(2,),
        out_shape=[jax.ShapeDtypeStruct(s, d) for s, d in outs],
        in_specs=[block(a.shape) for a in (slots, gate, up, down)],
        out_specs=[block(s) for s, _ in outs],
        name="experts_step",
        compiler_params=pltpu.CompilerParams(vmem_limit_bytes=56 * MIB),
    )(slots, gate, up, down)


def plane_place():
    e = lax.axis_index("expert")
    return e // 8, (e // 2) % 4, e % 2


def slab_of(z, x, core):
    return core * 16 + z * 4 + x


class Copies:
    def __init__(self, send, recv):
        self.send, self.recv, self.count, self.sent = send, recv, 0, []
        self.row = lax.axis_index("dp")
        self.z, self.x, self.core = plane_place()

    def make(self, src, dst, m, target):
        return pltpu.make_async_remote_copy(
            src_ref=src,
            dst_ref=dst,
            send_sem=self.send.at[m],
            recv_sem=self.recv.at[m],
            device_id=target,
            device_id_type=pl.DeviceIdType.MESH,
        )

    def push(self, src, dst, target, land):
        m = self.count
        self.count += 1
        copy = self.make(src, dst, m, target)
        copy.start()
        self.sent.append(copy)
        return self.make(land, land, m, target).wait_recv

    def device(self, dz, dx, flip=False):
        z, x = (self.z + dz + 4) % 4, (self.x + dx + 4) % 4
        core = 1 - self.core if flip else self.core
        return (self.row, (z * 4 + x) * 2 + core)

    def slab(self, dz, dx, flip=False):
        z, x = (self.z + dz + 4) % 4, (self.x + dx + 4) % 4
        core = 1 - self.core if flip else self.core
        return slab_of(z, x, core)

    def row_device(self, dy):
        e = (self.z * 4 + self.x) * 2 + self.core
        return ((self.row + dy + 4) % 4, e)

    def finish(self):
        for copy in self.sent:
            copy.wait_send()


def meet(targets):
    barrier = pltpu.get_barrier_semaphore()
    for target in targets:
        pl.semaphore_signal(
            barrier, inc=1, device_id=target, device_id_type=pl.DeviceIdType.MESH
        )
    pl.semaphore_wait(barrier, len(targets))


OFFSETS = (0, -1, 1, 2)


class SlabGather:
    def __init__(self, copies, own, out, z_first, halves):
        self.c, self.own, self.out, self.z_first, self.halves = copies, own, out, z_first, halves
        self.across, self.done = [], []
        self.cols = own.shape[-1] // 2

    def at(self, p, q):
        return (p, q) if self.z_first else (q, p)

    def ref(self, p, q, flip=False):
        return self.out.at[self.c.slab(*self.at(p, q), flip)]

    def half(self, ref, h):
        return ref.at[:, pl.ds(h * self.cols, self.cols)] if self.halves else ref

    def to(self, p, q, src, dst, land):
        return self.c.push(src, dst, self.c.device(*self.at(p, q)), land)

    def cross(self, p, q, src=None):
        ref = self.ref(p, q)
        target = self.c.device(0, 0, True)
        self.done.append(
            self.c.push(ref if src is None else src, ref, target, self.ref(p, q, True))
        )

    def spread(self, p, src=None):
        ref = self.ref(p, 0)
        src = ref if src is None else src
        ahead = self.to(0, 1, src, ref, self.ref(p, -1))
        behind = self.to(0, -1, src, ref, self.ref(p, 1))
        self.across.append((p, ahead, behind))

    def start(self):
        me = self.ref(0, 0)
        self.from_behind = self.to(1, 0, self.own, me, self.ref(-1, 0))
        self.from_ahead = self.to(-1, 0, self.own, me, self.ref(1, 0))

    def start_own(self):
        self.spread(0, self.own)
        self.cross(0, 0, self.own)

    def first(self):
        self.from_behind()
        ref, far = self.ref(-1, 0), self.ref(2, 0)
        self.far = [self.to(1, 0, self.half(ref, 0), self.half(ref, 0), self.half(far, 0))]
        self.spread(-1)
        self.cross(-1, 0)

    def second(self):
        self.from_ahead()
        if self.halves:
            ref, far = self.ref(1, 0), self.ref(2, 0)
            self.far.append(self.to(-1, 0, self.half(ref, 1), self.half(ref, 1), self.half(far, 1)))
        self.spread(1)
        self.cross(1, 0)

    def third(self):
        for wait in self.far:
            wait()
        self.spread(2)
        self.cross(2, 0)

    def ring(self, k):
        p, ahead, behind = self.across[k]
        if k == 0:
            self.last = []
        ahead()
        if k < 2:
            ref = self.ref(p, -1)
            self.last.append((p, self.to(0, 1, ref, ref, self.ref(p, 2))))
        self.cross(p, -1)
        behind()
        if k >= 2:
            ref = self.ref(p, 1)
            self.last.append((p, self.to(0, -1, ref, ref, self.ref(p, 2))))
        self.cross(p, 1)

    def end(self, k):
        p, wait = self.last[k]
        wait()
        self.cross(p, 2)

    def finish(self):
        for wait in self.done:
            wait()


def gather_kernel(
    x, dy, gate, up, down, table, xs, dys, tables, bases, other, send, recv, local
):
    c = Copies(send, recv)
    width = gate.shape[1]
    mine = c.slab(0, 0)
    sources = (gate, up, down)

    def columns(k, dy_, rows=None):
        at = pl.ds(pl.multiple_of(((c.row + dy_ + 4) % 4) * width, 128), width)
        ref = bases.at[k, :, at] if rows is None else bases.at[k, rows, at]
        return ref

    def other_columns(k, dy_):
        at = pl.ds(pl.multiple_of(((c.row + dy_ + 4) % 4) * width, 128), width)
        return other.at[k, :, at]

    here = [
        pltpu.make_async_copy(x, xs.at[mine], local.at[0]),
        pltpu.make_async_copy(dy, dys.at[mine], local.at[1]),
        pltpu.make_async_copy(table, tables.at[mine], local.at[2]),
    ]
    for k in range(3):
        here.append(pltpu.make_async_copy(sources[k], columns(k, 0), local.at[3 + k]))
    for copy in here:
        copy.start()
    meet(
        [c.device(0, 1), c.device(0, -1), c.device(1, 0), c.device(-1, 0)]
        + [c.device(0, 0, True), c.row_device(1), c.row_device(-1)]
    )
    parts = [
        SlabGather(c, table, tables, True, False),
        SlabGather(c, x, xs, True, True),
        SlabGather(c, dy, dys, False, True),
    ]
    for part in parts:
        part.start()
    basis_waits, basis_done, basis_far = [], [], []

    def basis_cross(k, dy_):
        if k < 2:
            ref = columns(k, dy_)
            src = sources[k] if dy_ == 0 else ref
            land = other_columns(k, dy_)
            basis_done.append(c.push(src, land, c.device(0, 0, True), land))

    for k in range(3):
        ref = columns(k, 0)
        basis_waits.append(
            (
                c.push(sources[k], ref, c.row_device(1), columns(k, -1)),
                c.push(sources[k], ref, c.row_device(-1), columns(k, 1)),
            )
        )
    for part in parts:
        part.start_own()
    for k in range(3):
        basis_cross(k, 0)
    for part in parts:
        part.first()
    for part in parts:
        part.second()
    for part in parts:
        part.third()
    half = gate.shape[0] // 2
    for step in range(4):
        for part in parts:
            part.ring(step)
        if step < 3:
            ahead, behind = basis_waits[step]
            low, high = pl.ds(0, half), pl.ds(half, half)
            ahead()
            ref = columns(step, -1, low)
            far = [c.push(ref, ref, c.row_device(1), columns(step, 2, low))]
            basis_cross(step, -1)
            behind()
            ref = columns(step, 1, high)
            far.append(c.push(ref, ref, c.row_device(-1), columns(step, 2, high)))
            basis_cross(step, 1)
            basis_far.append(far)
    for k in range(3):
        for wait in basis_far[k]:
            wait()
        basis_cross(k, 2)
    for step in range(4):
        for part in parts:
            part.end(step)
    for part in parts:
        part.finish()
    for wait in basis_done:
        wait()
    for copy in here:
        copy.wait()
    c.finish()


GATHER_COPIES = 32 + 32 + 31 + 20


def gather_inputs(x, dy, gate, up, down, table, n_ex):
    rows, width = gate.shape
    slabs = jax.ShapeDtypeStruct((n_ex,) + x.shape, BF)
    anywhere = pl.BlockSpec(memory_space=pl.ANY)
    return pl.pallas_call(
        gather_kernel,
        out_shape=[
            slabs,
            slabs,
            jax.ShapeDtypeStruct((n_ex,) + table.shape, FL),
            jax.ShapeDtypeStruct((3, rows, 4 * width), BF),
            jax.ShapeDtypeStruct((2, rows, 4 * width), BF),
        ],
        in_specs=[anywhere] * 6,
        out_specs=[anywhere] * 5,
        scratch_shapes=[
            pltpu.SemaphoreType.DMA((GATHER_COPIES,)),
            pltpu.SemaphoreType.DMA((GATHER_COPIES,)),
            pltpu.SemaphoreType.DMA((6,)),
        ],
        name="gather_inputs",
        compiler_params=pltpu.CompilerParams(collective_id=0, has_side_effects=True),
    )(x, dy, gate, up, down, table)


def slot_tables(route_ids, route_weight, cells):
    flat = route_ids.reshape(-1)
    pairs = flat.shape[0]
    at = jnp.arange(pairs, dtype=jnp.int32)
    earlier = (flat[:, None] == flat[None, :]) & (at[None, :] < at[:, None])
    slot = jnp.sum(earlier.astype(jnp.int32), axis=1)
    placed = (flat * 2 + slot)[:, None] == jnp.arange(cells, dtype=jnp.int32)[None, :]
    token = at // route_ids.shape[1] + 1
    cell_token = jnp.sum(jnp.where(placed, token[:, None], 0), axis=0)
    cell_weight = jnp.sum(
        jnp.where(placed, route_weight.reshape(-1)[:, None].astype(FL), 0.0), axis=0
    )
    return placed, cell_token, cell_weight


def body(
    tokens,
    grad_out,
    route_ids,
    route_weight,
    cluster_of,
    gate_basis,
    up_basis,
    down_basis,
    gate_factor,
    up_factor,
    down_factor,
):
    n_dp = lax.axis_size("dp")
    n_ex = lax.axis_size("expert")
    tok_rows, width = tokens.shape
    local = gate_factor.shape[0]
    lane_rows = local * 2
    cells = n_ex * lane_rows
    clusters, rank, part_width = gate_basis.shape
    plane_tokens = n_ex * tok_rows
    all_rank = n_ex * rank

    placed, cell_token, cell_weight = slot_tables(route_ids, route_weight, cells)
    table = jnp.concatenate([cell_token.astype(FL), cell_weight]).reshape(4, 128)
    flat = (clusters * rank, part_width)
    x_all, dy_all, tables, bases, other = gather_inputs(
        tokens,
        grad_out,
        gate_basis.reshape(flat),
        up_basis.reshape(flat),
        down_basis.reshape(flat),
        table,
        n_ex,
    )
    x_all = x_all.reshape(plane_tokens, width)
    dy_all = dy_all.reshape(plane_tokens, width)
    tables = tables.reshape(n_ex, 2, n_ex, local, 2)
    tables = tables.transpose(1, 2, 3, 0, 4).reshape(2, n_ex, n_ex * lane_rows)
    block = (jnp.arange(n_ex * lane_rows, dtype=jnp.int32) // 2) % n_ex
    named = tables[0].astype(jnp.int32)
    slots = jnp.where(named > 0, named - 1 + tok_rows * block[None, :], -1)
    weights = tables[1]
    cluster = cluster_of.reshape(n_ex, local)[:, 0]

    gate_up = bases[:2].reshape(2 * clusters * rank, width)
    down = bases[2]
    first = dot(gate_up, x_all, 1, 1).astype(BF).reshape(2, clusters * rank, plane_tokens)
    back = dot(down, dy_all, 1, 1).astype(BF)[None]
    picked = pick(cluster, jnp.concatenate([first, back]), slots, weights, rank)

    sent = jnp.broadcast_to(picked[None], (n_dp,) + picked.shape)
    sent = sent.reshape((n_dp * n_ex,) + picked.shape[1:])
    got = lax.all_to_all(sent, ("dp", "expert"), split_axis=0, concat_axis=0, tiled=True)
    got = got.reshape(n_dp, n_ex, 2, 3, rank, -1).transpose(2, 3, 1, 4, 0, 5)
    got = got.reshape(2, 3, all_rank, -1)
    part, route, d_gate_factor, d_up_factor, d_down_factor = experts_step(
        got, gate_factor, up_factor, down_factor
    )

    home = part.reshape(2, 3, n_ex, rank, n_dp, -1).transpose(4, 2, 0, 1, 3, 5)
    home = home.reshape((n_dp * n_ex,) + picked.shape[1:])
    home = lax.all_to_all(home, ("dp", "expert"), split_axis=0, concat_axis=0, tiled=True)
    home = home.reshape((n_dp, n_ex) + picked.shape[1:])
    summed = combine(cluster, home, slots, weights, clusters, plane_tokens)

    dots = route.reshape(local, n_dp, 2, n_ex // 2, 2).transpose(1, 3, 2, 0, 4)
    dots = dots.reshape(n_dp * n_ex, lane_rows)
    dots = lax.all_to_all(dots, ("dp", "expert"), split_axis=0, concat_axis=0, tiled=True)
    scores = jnp.sum(dots.reshape(n_dp, cells), axis=0)
    scores = scores / jnp.where(cell_weight > 0.0, cell_weight, 1.0)
    grad_route = jnp.sum(jnp.where(placed, scores[None, :], 0.0), axis=1).reshape(route_ids.shape)

    back_up = summed[:2].reshape(2 * clusters * rank, plane_tokens)
    grad_gate_up = dot(back_up, x_all, 1, 0).astype(BF).reshape(2, clusters * rank, width)
    grad_down = dot(summed[2], dy_all, 1, 0).astype(BF)[None]
    terms = jnp.concatenate([grad_gate_up, grad_down])
    terms = lax.psum_scatter(terms, "dp", scatter_dimension=2, tiled=True).astype(FL)
    grad_x = dot(back_up, gate_up, 0, 0).astype(BF)
    grad_x = grad_x.reshape(2, n_ex // 2, tok_rows, width).transpose(1, 0, 2, 3)
    grad_x = grad_x.reshape(plane_tokens, width)
    grad_tokens = lax.psum_scatter(grad_x, "expert", scatter_dimension=0, tiled=True)
    shape = gate_basis.shape
    return (
        grad_tokens,
        grad_route,
        terms[0].reshape(shape),
        terms[1].reshape(shape),
        terms[2].reshape(shape),
        d_gate_factor,
        d_up_factor,
        d_down_factor,
    )


def solution(mesh):
    rows = P(("dp", "expert"), None)
    basis = P(None, "expert", "dp")
    factor = P("expert", None, "dp")
    low = P("expert", "dp", None)
    in_specs = (rows, rows, rows, rows, P(), basis, basis, basis, factor, factor, low)
    out_specs = (rows, rows, basis, basis, basis, factor, factor, low)
    return jax.shard_map(body, mesh=mesh, in_specs=in_specs, out_specs=out_specs, check_vma=False)
```

```python
import jax
import jax.numpy as jnp
from jax import lax
from jax.experimental import pallas as pl
from jax.experimental.pallas import tpu as pltpu
from jax.sharding import PartitionSpec as P

FL = jnp.float32
BF = jnp.bfloat16
MIB = 1024 * 1024


def dot(a, b, ca, cb):
    return lax.dot_general(a, b, (((ca,), (cb,)), ((), ())), preferred_element_type=FL)


def one_hot(slot_ref, j, tokens):
    row = slot_ref[pl.ds(j, 1), :]
    lanes = row.shape[1]
    grid = lax.broadcasted_iota(jnp.int32, (tokens, lanes), 0)
    return jnp.where(grid == row, 1.0, 0.0).astype(BF)


def combine_kernel(cluster, parts, slots, weights, out, total):
    groups, rank, tokens = parts.shape[1], parts.shape[4], out.shape[2]
    total[...] = jnp.zeros_like(total)

    def step(j, carry):
        c = cluster[j]
        got = parts[0, j].astype(FL)
        for i in range(1, parts.shape[0]):
            got = got + parts[i, j].astype(FL)
        got = jnp.concatenate([got[0], got[1]], axis=2)
        got = jnp.concatenate([got[:2], got[2:] * weights[pl.ds(j, 1), :]], axis=0)
        got = got.astype(BF).reshape(3 * rank, -1)
        add = dot(got, one_hot(slots, j, tokens), 1, 1).reshape(3, rank, tokens)
        total[:, pl.ds(pl.multiple_of(c * rank, rank), rank), :] += add
        return carry

    lax.fori_loop(0, groups, step, 0)
    out[...] = total[...].astype(BF)


def combine(cluster, parts, slots, weights, clusters, tokens):
    rank = parts.shape[4]
    vmem = pl.BlockSpec(memory_space=pltpu.VMEM)
    shape = (3, clusters * rank, tokens)
    return pl.pallas_call(
        combine_kernel,
        out_shape=jax.ShapeDtypeStruct(shape, BF),
        in_specs=[pl.BlockSpec(memory_space=pltpu.SMEM), vmem, vmem, vmem],
        out_specs=vmem,
        scratch_shapes=[pltpu.VMEM(shape, FL)],
        name="combine",
        compiler_params=pltpu.CompilerParams(vmem_limit_bytes=40 * MIB),
    )(cluster, parts, slots, weights)


def mix(tiles):
    first, second = [], []
    for k in range(0, len(tiles), 2):
        a, b = tiles[k], tiles[k + 1]
        h = a.shape[-1] // 2
        first.append(jnp.concatenate([a[:, :h], b[:, :h]], axis=1))
        second.append(jnp.concatenate([a[:, h:], b[:, h:]], axis=1))
    return jnp.concatenate(first, axis=1), jnp.concatenate(second, axis=1)


def split_tiles(a):
    return [a[:, k : k + 128] for k in range(0, a.shape[1], 128)]


def middle_kernel(
    member, rows, slots, weights, gate, up, down,
    home, dots, kept_rows, kept_units,
    picked, landed, parts, factors, row_store, unit_store, route,
    out_send, out_recv, back_send, back_recv, dot_send, dot_recv, loads, local,
):
    row, e = lax.axis_index("dp"), lax.axis_index("expert")
    groups, rank, tokens = picked.shape[0], picked.shape[3], rows.shape[2]
    lanes = picked.shape[4]

    def device(d, r):
        return ((row + r) % 4, (e + d) % groups)

    def source(d, r):
        return ((row - r + 4) % 4, (e - d + groups) % groups)

    def everyone(act):
        for r in range(1, 4):
            act(0, r)

        def step(s, carry):
            for r in range(4):
                act((s * 11) % groups, r)
            return carry

        lax.fori_loop(1, groups, step, 0)

    def remote(src, dst, send, recv, target):
        return pltpu.make_async_remote_copy(
            src_ref=src,
            dst_ref=dst,
            send_sem=send,
            recv_sem=recv,
            device_id=target,
            device_id_type=pl.DeviceIdType.MESH,
        )

    def piece(ref, p, at):
        sub = pl.ds(pl.multiple_of(at[1] * rank, rank), rank)
        lane = pl.ds(pl.multiple_of(at[0] * lanes, lanes), lanes)
        return ref.at[p, :, sub, lane]

    def out_copy(p, d, r):
        target = device(d, r)
        n = d * 4 + r
        return remote(
            picked.at[target[1], p],
            piece(landed, p, (row, e)),
            out_send.at[p, n],
            out_recv.at[p, n],
            target,
        )

    def out_wait(p, d, r):
        n = d * 4 + r
        land = piece(landed, p, source(d, r))
        remote(land, land, out_send.at[p, n], out_recv.at[p, n], device(d, r)).wait_recv()

    def back_copy(p, d, r):
        target = device(d, r)
        n = d * 4 + r
        return remote(
            piece(parts, p, target),
            home.at[row, e, p],
            back_send.at[p, n],
            back_recv.at[p, n],
            target,
        )

    def back_wait(p, d, r):
        n = d * 4 + r
        at = source(d, r)
        land = home.at[at[0], at[1], p]
        remote(land, land, back_send.at[p, n], back_recv.at[p, n], device(d, r)).wait_recv()

    def dot_copy(d, r):
        target = device(d, r)
        n = d * 4 + r
        return remote(
            route.at[target[0]], dots.at[row, e], dot_send.at[n], dot_recv.at[n], target
        )

    def dot_wait(d, r):
        n = d * 4 + r
        at = source(d, r)
        land = dots.at[at[0], at[1]]
        remote(land, land, dot_send.at[n], dot_recv.at[n], device(d, r)).wait_recv()

    incoming = [
        pltpu.make_async_copy(ref, factors.at[k], loads.at[k])
        for k, ref in enumerate((gate, up, down))
    ]
    for copy in incoming:
        copy.start()
    barrier = pltpu.get_barrier_semaphore()

    def greet(d, r):
        pl.semaphore_signal(
            barrier, inc=1, device_id=device(d, r), device_id_type=pl.DeviceIdType.MESH
        )

    everyone(greet)

    def pick_for(j):
        own = jnp.zeros((3, rank, tokens), BF)
        for c in range(member.shape[1]):
            share = member[pl.ds(j, 1), c : c + 1].astype(BF)[None]
            own = own + rows[:, c * rank : (c + 1) * rank, :] * share
        got = dot(own.reshape(3 * rank, tokens), one_hot(slots, j, tokens), 1, 0)
        got = got.reshape(3, rank, -1)
        got = jnp.concatenate([got[:2], got[2:] * weights[pl.ds(j, 1), :]], axis=0).astype(BF)
        picked[j, 0] = got[:, :, :lanes]
        picked[j, 1] = got[:, :, lanes:]

    pick_for(e)
    own_copies = [
        pltpu.make_async_copy(picked.at[e, p], piece(landed, p, (row, e)), local.at[p])
        for p in range(2)
    ]
    for copy in own_copies:
        copy.start()
    pl.semaphore_wait(barrier, 4 * groups - 1)
    for r in range(1, 4):
        out_copy(0, 0, r).start()

    def pick_step(s, carry):
        d = (s * 11) % groups
        pick_for((e + d) % groups)
        for r in range(4):
            out_copy(0, d, r).start()
        return carry

    lax.fori_loop(1, groups, pick_step, 0)
    everyone(lambda d, r: out_copy(1, d, r).start())
    for copy in incoming:
        copy.wait()
    for copy in own_copies:
        copy.wait()
    stores = []
    for p in range(2):
        everyone(lambda d, r: out_wait(p, d, r))
        wide = [mix(split_tiles(landed[p, k])) for k in range(3)]
        results = []
        for n in range(2):
            hg, hu, gm = wide[0][n], wide[1][n], wide[2][n]
            ex = 2 * p + n
            row_store[ex, 0] = hg
            row_store[ex, 1] = hu
            row_store[ex, 2] = gm
            gf, uf, df = factors[0, ex], factors[1, ex], factors[2, ex]
            gate_pre = dot(gf, hg, 0, 0)
            up_pre = dot(uf, hu, 0, 0)
            sig = 1.0 / (1.0 + jnp.exp(-gate_pre))
            act = gate_pre * sig
            slope = sig * (1.0 + gate_pre * (1.0 - sig))
            hidden = (act * up_pre).astype(BF)
            mixed = dot(df, hidden, 0, 0)
            grad_hidden = dot(df, gm, 1, 0)
            grad_gate_pre = (grad_hidden * up_pre * slope).astype(BF)
            grad_up_pre = (grad_hidden * act).astype(BF)
            unit_store[ex, 0] = grad_gate_pre
            unit_store[ex, 1] = grad_up_pre
            unit_store[ex, 2] = hidden
            scores = jnp.sum(mixed * gm.astype(FL), axis=0, keepdims=True)
            each = lanes // 2
            for i in range(4):
                route[i, p : p + 1, n * each : (n + 1) * each] = scores[:, i * each : (i + 1) * each]
            grad_hg = dot(gf, grad_gate_pre, 1, 0)
            grad_hu = dot(uf, grad_up_pre, 1, 0)
            results.append((grad_hg.astype(BF), grad_hu.astype(BF), mixed.astype(BF)))
        for k in range(3):
            tiles = []
            for a, b in zip(split_tiles(results[0][k]), split_tiles(results[1][k])):
                h = a.shape[-1] // 2
                tiles.append(jnp.concatenate([a[:, :h], b[:, :h]], axis=1))
                tiles.append(jnp.concatenate([a[:, h:], b[:, h:]], axis=1))
            parts[p, k] = jnp.concatenate(tiles, axis=1)
        everyone(lambda d, r: back_copy(p, d, r).start())
        pair = pl.ds(2 * p, 2)
        here = [
            pltpu.make_async_copy(piece(parts, p, (row, e)), home.at[row, e, p], local.at[2 + p]),
            pltpu.make_async_copy(row_store.at[pair], kept_rows.at[pair], local.at[4 + p]),
            pltpu.make_async_copy(unit_store.at[pair], kept_units.at[pair], local.at[6 + p]),
        ]
        for copy in here:
            copy.start()
        stores += here
    everyone(lambda d, r: dot_copy(d, r).start())
    own_dots = pltpu.make_async_copy(route.at[row], dots.at[row, e], local.at[8])
    own_dots.start()
    stores.append(own_dots)
    for p in range(2):
        everyone(lambda d, r: back_wait(p, d, r))
    everyone(dot_wait)
    for copy in stores:
        copy.wait()
    for p in range(2):
        everyone(lambda d, r: out_copy(p, d, r).wait_send())
        everyone(lambda d, r: back_copy(p, d, r).wait_send())
    everyone(lambda d, r: dot_copy(d, r).wait_send())


def middle(member, rows, slots, weights, gate, up, down, n_dp):
    groups, lanes = slots.shape
    kinds, ranks, _ = rows.shape
    count, all_rank, units = gate.shape
    rank = all_rank // groups
    half = lanes // 2
    anywhere = pl.BlockSpec(memory_space=pl.ANY)
    vmem = pl.BlockSpec(memory_space=pltpu.VMEM)
    kept = jax.ShapeDtypeStruct((count, 3, all_rank, n_dp * half // 2), BF)
    dma = pltpu.SemaphoreType.DMA
    return pl.pallas_call(
        middle_kernel,
        out_shape=[
            jax.ShapeDtypeStruct((n_dp, groups, 2, 3, rank, half), BF),
            jax.ShapeDtypeStruct((n_dp, groups, 2, half), FL),
            kept,
            kept,
        ],
        in_specs=[vmem] * 4 + [anywhere] * 3,
        out_specs=[anywhere] * 4,
        scratch_shapes=[
            pltpu.VMEM((groups, 2, 3, rank, half), BF),
            pltpu.VMEM((2, 3, all_rank, n_dp * half), BF),
            pltpu.VMEM((2, 3, all_rank, n_dp * half), BF),
            pltpu.VMEM((3,) + gate.shape, BF),
            pltpu.VMEM(kept.shape, BF),
            pltpu.VMEM(kept.shape, BF),
            pltpu.VMEM((n_dp, 2, half), FL),
            dma((2, n_dp * groups)),
            dma((2, n_dp * groups)),
            dma((2, n_dp * groups)),
            dma((2, n_dp * groups)),
            dma((n_dp * groups,)),
            dma((n_dp * groups,)),
            dma((3,)),
            dma((9,)),
        ],
        name="middle",
        compiler_params=pltpu.CompilerParams(
            collective_id=2, has_side_effects=True, vmem_limit_bytes=56 * MIB
        ),
    )(member, rows, slots, weights, gate, up, down)


def factor_kernel(rows, units, d_gate, d_up, d_down):
    d_gate[0] = dot(rows[0, 0], units[0, 0], 1, 1)
    d_up[0] = dot(rows[0, 1], units[0, 1], 1, 1)
    d_down[0] = dot(units[0, 2], rows[0, 2], 1, 1)


def factor_grads(rows, units):
    count, _, all_rank, lanes = rows.shape
    held = pl.BlockSpec((1,) + rows.shape[1:], lambda g: (g, 0, 0, 0))
    one = pl.BlockSpec((1, all_rank, units.shape[2]), lambda g: (g, 0, 0))
    return pl.pallas_call(
        factor_kernel,
        grid=(count,),
        out_shape=[jax.ShapeDtypeStruct((count, all_rank, units.shape[2]), FL)] * 3,
        in_specs=[held, held],
        out_specs=[one] * 3,
        name="factor_grads",
        compiler_params=pltpu.CompilerParams(vmem_limit_bytes=40 * MIB),
    )(rows, units)


def plane_place():
    e = lax.axis_index("expert")
    return e // 8, (e // 2) % 4, e % 2


def slab_of(z, x, core):
    return core * 16 + z * 4 + x


class Copies:
    def __init__(self, send, recv):
        self.send, self.recv, self.count, self.sent = send, recv, 0, []
        self.row = lax.axis_index("dp")
        self.z, self.x, self.core = plane_place()

    def make(self, src, dst, m, target):
        return pltpu.make_async_remote_copy(
            src_ref=src,
            dst_ref=dst,
            send_sem=self.send.at[m],
            recv_sem=self.recv.at[m],
            device_id=target,
            device_id_type=pl.DeviceIdType.MESH,
        )

    def push(self, src, dst, target, land):
        m = self.count
        self.count += 1
        copy = self.make(src, dst, m, target)
        copy.start()
        self.sent.append(copy)
        return self.make(land, land, m, target).wait_recv

    def device(self, dz, dx, flip=False):
        z, x = (self.z + dz + 4) % 4, (self.x + dx + 4) % 4
        core = 1 - self.core if flip else self.core
        return (self.row, (z * 4 + x) * 2 + core)

    def slab(self, dz, dx, flip=False):
        z, x = (self.z + dz + 4) % 4, (self.x + dx + 4) % 4
        core = 1 - self.core if flip else self.core
        return slab_of(z, x, core)

    def row_device(self, dy):
        e = (self.z * 4 + self.x) * 2 + self.core
        return ((self.row + dy + 4) % 4, e)

    def finish(self):
        for copy in self.sent:
            copy.wait_send()


def meet(targets):
    barrier = pltpu.get_barrier_semaphore()
    for target in targets:
        pl.semaphore_signal(
            barrier, inc=1, device_id=target, device_id_type=pl.DeviceIdType.MESH
        )
    pl.semaphore_wait(barrier, len(targets))


OFFSETS = (0, -1, 1, 2)


class SlabGather:
    def __init__(self, copies, own, out, z_first, halves):
        self.c, self.own, self.out, self.z_first, self.halves = copies, own, out, z_first, halves
        self.across, self.done = [], []
        self.cols = own.shape[-1] // 2

    def at(self, p, q):
        return (p, q) if self.z_first else (q, p)

    def ref(self, p, q, flip=False):
        return self.out.at[self.c.slab(*self.at(p, q), flip)]

    def half(self, ref, h):
        return ref.at[:, pl.ds(h * self.cols, self.cols)] if self.halves else ref

    def to(self, p, q, src, dst, land):
        return self.c.push(src, dst, self.c.device(*self.at(p, q)), land)

    def cross(self, p, q, src=None):
        ref = self.ref(p, q)
        target = self.c.device(0, 0, True)
        self.done.append(
            self.c.push(ref if src is None else src, ref, target, self.ref(p, q, True))
        )

    def spread(self, p, src=None):
        ref = self.ref(p, 0)
        src = ref if src is None else src
        ahead = self.to(0, 1, src, ref, self.ref(p, -1))
        behind = self.to(0, -1, src, ref, self.ref(p, 1))
        self.across.append((p, ahead, behind))

    def start(self):
        me = self.ref(0, 0)
        self.from_behind = self.to(1, 0, self.own, me, self.ref(-1, 0))
        self.from_ahead = self.to(-1, 0, self.own, me, self.ref(1, 0))

    def start_own(self):
        self.spread(0, self.own)
        self.cross(0, 0, self.own)

    def first(self):
        self.from_behind()
        ref, far = self.ref(-1, 0), self.ref(2, 0)
        self.far = [self.to(1, 0, self.half(ref, 0), self.half(ref, 0), self.half(far, 0))]
        self.spread(-1)
        self.cross(-1, 0)

    def second(self):
        self.from_ahead()
        if self.halves:
            ref, far = self.ref(1, 0), self.ref(2, 0)
            self.far.append(self.to(-1, 0, self.half(ref, 1), self.half(ref, 1), self.half(far, 1)))
        self.spread(1)
        self.cross(1, 0)

    def third(self):
        for wait in self.far:
            wait()
        self.spread(2)
        self.cross(2, 0)

    def ring(self, k):
        p, ahead, behind = self.across[k]
        if k == 0:
            self.last = []
        ahead()
        if k < 2:
            ref = self.ref(p, -1)
            self.last.append((p, self.to(0, 1, ref, ref, self.ref(p, 2))))
        self.cross(p, -1)
        behind()
        if k >= 2:
            ref = self.ref(p, 1)
            self.last.append((p, self.to(0, -1, ref, ref, self.ref(p, 2))))
        self.cross(p, 1)

    def end(self, k):
        p, wait = self.last[k]
        wait()
        self.cross(p, 2)

    def finish(self):
        for wait in self.done:
            wait()


def gather_kernel(
    x, dy, gate, up, down, table, xs, dys, tables, bases, other, send, recv, local
):
    c = Copies(send, recv)
    width = gate.shape[1]
    mine = c.slab(0, 0)
    sources = (gate, up, down)

    def columns(k, dy_, rows=None):
        at = pl.ds(pl.multiple_of(((c.row + dy_ + 4) % 4) * width, 128), width)
        ref = bases.at[k, :, at] if rows is None else bases.at[k, rows, at]
        return ref

    def other_columns(k, dy_):
        at = pl.ds(pl.multiple_of(((c.row + dy_ + 4) % 4) * width, 128), width)
        return other.at[k, :, at]

    here = [
        pltpu.make_async_copy(x, xs.at[mine], local.at[0]),
        pltpu.make_async_copy(dy, dys.at[mine], local.at[1]),
        pltpu.make_async_copy(table, tables.at[mine], local.at[2]),
    ]
    for k in range(3):
        here.append(pltpu.make_async_copy(sources[k], columns(k, 0), local.at[3 + k]))
    for copy in here:
        copy.start()
    meet(
        [c.device(0, 1), c.device(0, -1), c.device(1, 0), c.device(-1, 0)]
        + [c.device(0, 0, True), c.row_device(1), c.row_device(-1)]
    )
    parts = [
        SlabGather(c, table, tables, True, False),
        SlabGather(c, x, xs, True, True),
        SlabGather(c, dy, dys, False, True),
    ]
    for part in parts:
        part.start()
    basis_waits, basis_done, basis_far = [], [], []

    def basis_cross(k, dy_):
        if k < 2:
            ref = columns(k, dy_)
            src = sources[k] if dy_ == 0 else ref
            land = other_columns(k, dy_)
            basis_done.append(c.push(src, land, c.device(0, 0, True), land))

    for k in range(3):
        ref = columns(k, 0)
        basis_waits.append(
            (
                c.push(sources[k], ref, c.row_device(1), columns(k, -1)),
                c.push(sources[k], ref, c.row_device(-1), columns(k, 1)),
            )
        )
    for part in parts:
        part.start_own()
    for k in range(3):
        basis_cross(k, 0)
    for part in parts:
        part.first()
    for part in parts:
        part.second()
    for part in parts:
        part.third()
    half = gate.shape[0] // 2
    for step in range(4):
        for part in parts:
            part.ring(step)
        if step < 3:
            ahead, behind = basis_waits[step]
            low, high = pl.ds(0, half), pl.ds(half, half)
            ahead()
            ref = columns(step, -1, low)
            far = [c.push(ref, ref, c.row_device(1), columns(step, 2, low))]
            basis_cross(step, -1)
            behind()
            ref = columns(step, 1, high)
            far.append(c.push(ref, ref, c.row_device(-1), columns(step, 2, high)))
            basis_cross(step, 1)
            basis_far.append(far)
    for k in range(3):
        for wait in basis_far[k]:
            wait()
        basis_cross(k, 2)
    for step in range(4):
        for part in parts:
            part.end(step)
    for part in parts:
        part.finish()
    for wait in basis_done:
        wait()
    for copy in here:
        copy.wait()
    c.finish()


GATHER_COPIES = 32 + 32 + 31 + 20


def gather_inputs(x, dy, gate, up, down, table, n_ex):
    rows, width = gate.shape
    slabs = jax.ShapeDtypeStruct((n_ex,) + x.shape, BF)
    anywhere = pl.BlockSpec(memory_space=pl.ANY)
    return pl.pallas_call(
        gather_kernel,
        out_shape=[
            slabs,
            slabs,
            jax.ShapeDtypeStruct((n_ex,) + table.shape, FL),
            jax.ShapeDtypeStruct((3, rows, 4 * width), BF),
            jax.ShapeDtypeStruct((2, rows, 4 * width), BF),
        ],
        in_specs=[anywhere] * 6,
        out_specs=[anywhere] * 5,
        scratch_shapes=[
            pltpu.SemaphoreType.DMA((GATHER_COPIES,)),
            pltpu.SemaphoreType.DMA((GATHER_COPIES,)),
            pltpu.SemaphoreType.DMA((6,)),
        ],
        name="gather_inputs",
        compiler_params=pltpu.CompilerParams(collective_id=0, has_side_effects=True),
    )(x, dy, gate, up, down, table)


def home_kernel(
    rows, x, dy, bases, other,
    out, d_gate, d_up, d_down,
    paired, xb, db, bb, terms, far_in, near_in, turned, full, got, passed, kept, last,
    send, recv, loads,
):
    c = Copies(send, recv)
    width = d_gate.shape[1]
    near = (1, -1, 2)
    meet(
        [c.device(0, d) for d in near]
        + [c.device(d, 0) for d in near]
        + [c.device(0, 0, True), c.row_device(1), c.row_device(-1)]
    )
    partner = c.push(rows.at[pl.ds(0, 2)], paired, c.device(0, 0, True), paired)
    order = (2, 1, -1, 0)

    def load_rows(n):
        at = pl.ds(pl.multiple_of(((c.row + order[n] + 4) % 4) * width, 128), width)
        slot = n % 2
        copies = [
            pltpu.make_async_copy(x.at[:, at], xb.at[slot], loads.at[2 * slot]),
            pltpu.make_async_copy(dy.at[:, at], db.at[slot], loads.at[2 * slot + 1]),
        ]
        for copy in copies:
            copy.start()
        return copies

    def load_bases(n):
        at = pl.ds(n * width, width)
        slot = n % 2
        copies = [
            pltpu.make_async_copy(
                bases.at[pl.ds(0, 2), :, at], bb.at[slot, 0], loads.at[4 + 2 * slot]
            ),
            pltpu.make_async_copy(other.at[:, :, at], bb.at[slot, 1], loads.at[5 + 2 * slot]),
        ]
        for copy in copies:
            copy.start()
        return copies

    flying = [load_rows(0), load_rows(1)]
    basis_flying = [load_bases(0), load_bases(1)]
    low, high = pl.ds(0, 64), pl.ds(64, 64)
    near_waits = [[], []]
    far_waits = [[], []]
    for n in range(4):
        for copy in flying[n]:
            copy.wait()
        slot = n % 2

        def columns(k, carry):
            at = pl.ds(pl.multiple_of(k * 256, 256), 256)
            ups = dot(rows[0:2].reshape(256, -1), xb[slot, :, at], 1, 0)
            downs = dot(rows[2], db[slot, :, at], 1, 0)
            if n < 3:
                terms[n, 0, :, at] = ups[:128].astype(BF)
                terms[n, 1, :, at] = ups[128:].astype(BF)
                terms[n, 2, :, at] = downs.astype(BF)
            else:
                d_gate[:, at] = ups[:128]
                d_up[:, at] = ups[128:]
                d_down[:, at] = downs
            return carry

        lax.fori_loop(0, width // 256, columns, 0)
        if n < 2:
            flying.append(load_rows(n + 2))
        for k in range(3):
            if n == 0:
                land = far_in.at[0, k]
                far_waits[0].append(c.push(terms.at[0, k, low], land, c.row_device(1), land))
                land = far_in.at[1, k]
                far_waits[1].append(c.push(terms.at[0, k, high], land, c.row_device(-1), land))
            if n == 1:
                land = near_in.at[0, k, high]
                near_waits[0].append(c.push(terms.at[1, k, high], land, c.row_device(1), land))
            if n == 2:
                land = near_in.at[1, k, low]
                near_waits[1].append(c.push(terms.at[2, k, low], land, c.row_device(-1), land))
    partner()
    half_tokens = turned.shape[0]
    mine = pl.ds(pl.multiple_of(c.core * half_tokens, 128), half_tokens)
    for k in range(2):
        for n, source in enumerate((rows, paired)):
            at = pl.ds((2 * n + k) * 128, 128)
            turned[:, at] = source[k, :, mine].astype(FL).T.astype(BF)
    tok = full.shape[2]
    place = (c.z, c.x)
    got_waits = [[], []]
    for n in range(4):
        for copy in basis_flying[n]:
            copy.wait()
        slot, h = n % 2, n // 2

        def token_columns(k, carry):
            at = pl.ds(pl.multiple_of(k * 256, 256), 256)
            to = pl.ds(pl.multiple_of((n % 2) * width + k * 256, 256), 256)
            both = jnp.concatenate(
                [bb[slot, s, k2, :, at] for s in range(2) for k2 in range(2)], axis=0
            )
            sums = dot(turned[...], both, 1, 0)
            for s in range(16):
                full[h, s, :, to] = sums[s * tok : (s + 1) * tok].astype(BF)
            return carry

        lax.fori_loop(0, width // 256, token_columns, 0)
        if n < 2:
            basis_flying.append(load_bases(n + 2))
        if n % 2 == 1:
            for b in (1, -1, 2, 0):
                waits = []
                for di, d in enumerate(near):
                    if h == 0:
                        slab = ((c.z + b + 4) % 4) * 4 + (c.x + d + 4) % 4
                        target = c.device(0, d)
                    else:
                        slab = ((c.z + d + 4) % 4) * 4 + (c.x + b + 4) % 4
                        target = c.device(d, 0)
                    land = got.at[h, di, b % 4]
                    waits.append(c.push(full.at[h, slab], land, target, land))
                got_waits[h].append((b, waits))
    for k in range(3):
        far_waits[0][k]()
        terms[1, k, low] = (terms[1, k, low].astype(FL) + far_in[0, k].astype(FL)).astype(BF)
        land = near_in.at[0, k, low]
        near_waits[0].append(c.push(terms.at[1, k, low], land, c.row_device(1), land))
        far_waits[1][k]()
        terms[2, k, high] = (terms[2, k, high].astype(FL) + far_in[1, k].astype(FL)).astype(BF)
        land = near_in.at[1, k, high]
        near_waits[1].append(c.push(terms.at[2, k, high], land, c.row_device(-1), land))
    last_waits = [[], []]
    for step in range(4):
        for h in range(2):
            b, waits = got_waits[h][step]
            for wait in waits:
                wait()
            if h == 0:
                slab = ((c.z + b + 4) % 4) * 4 + c.x
                target = c.device(b, 0)
            else:
                slab = c.z * 4 + (c.x + b + 4) % 4
                target = c.device(0, b)
            total = full[h, slab].astype(FL)
            for di in range(3):
                total = total + got[h, di, b % 4].astype(FL)
            if b == 0:
                kept[h] = total
            else:
                passed[h, step] = total.astype(BF)
                land = last.at[h, step]
                last_waits[h].append(c.push(passed.at[h, step], land, target, land))
    for h in range(2):
        for wait in last_waits[h]:
            wait()
        total = kept[h]
        for step in range(3):
            total = total + last[h, step].astype(FL)
        out[:, h * 2 * width : (h + 1) * 2 * width] = total.astype(BF)
    for side in range(2):
        for wait in near_waits[side]:
            wait()
    for k, ref in enumerate((d_gate, d_up, d_down)):
        ref[...] = ref[...] + near_in[0, k].astype(FL) + near_in[1, k].astype(FL)
    c.finish()


HOME_COPIES = 1 + 18 + 24 + 6


def send_home(rows, x, dy, bases, other, tok):
    kinds, ranks, tokens = rows.shape
    full_width = x.shape[1]
    width = full_width // 4
    half = full_width // 2
    anywhere = pl.BlockSpec(memory_space=pl.ANY)
    vmem = pl.BlockSpec(memory_space=pltpu.VMEM)
    basis = jax.ShapeDtypeStruct((ranks, width), FL)
    return pl.pallas_call(
        home_kernel,
        out_shape=[jax.ShapeDtypeStruct((tok, full_width), BF), basis, basis, basis],
        in_specs=[vmem] + [anywhere] * 4,
        out_specs=[vmem] * 4,
        scratch_shapes=[
            pltpu.VMEM((2, ranks, tokens), BF),
            pltpu.VMEM((2, tokens, width), BF),
            pltpu.VMEM((2, tokens, width), BF),
            pltpu.VMEM((2, 2, 2, ranks, width), BF),
            pltpu.VMEM((3, kinds, ranks, width), BF),
            pltpu.VMEM((2, kinds, ranks // 2, width), BF),
            pltpu.VMEM((2, kinds, ranks, width), BF),
            pltpu.VMEM((tokens // 2, 4 * ranks), BF),
            pltpu.VMEM((2, 16, tok, half), BF),
            pltpu.VMEM((2, 3, 4, tok, half), BF),
            pltpu.VMEM((2, 3, tok, half), BF),
            pltpu.VMEM((2, tok, half), FL),
            pltpu.VMEM((2, 3, tok, half), BF),
            pltpu.SemaphoreType.DMA((HOME_COPIES,)),
            pltpu.SemaphoreType.DMA((HOME_COPIES,)),
            pltpu.SemaphoreType.DMA((8,)),
        ],
        name="send_home",
        compiler_params=pltpu.CompilerParams(
            collective_id=1, has_side_effects=True, vmem_limit_bytes=60 * MIB
        ),
    )(rows, x, dy, bases, other)


def slot_tables(route_ids, route_weight, cells):
    flat = route_ids.reshape(-1)
    pairs = flat.shape[0]
    at = jnp.arange(pairs, dtype=jnp.int32)
    earlier = (flat[:, None] == flat[None, :]) & (at[None, :] < at[:, None])
    slot = jnp.sum(earlier.astype(jnp.int32), axis=1)
    placed = (flat * 2 + slot)[:, None] == jnp.arange(cells, dtype=jnp.int32)[None, :]
    token = at // route_ids.shape[1] + 1
    cell_token = jnp.sum(jnp.where(placed, token[:, None], 0), axis=0)
    cell_weight = jnp.sum(
        jnp.where(placed, route_weight.reshape(-1)[:, None].astype(FL), 0.0), axis=0
    )
    return placed, cell_token, cell_weight


def body(
    tokens,
    grad_out,
    route_ids,
    route_weight,
    cluster_of,
    gate_basis,
    up_basis,
    down_basis,
    gate_factor,
    up_factor,
    down_factor,
):
    n_dp = lax.axis_size("dp")
    n_ex = lax.axis_size("expert")
    tok_rows, width = tokens.shape
    local = gate_factor.shape[0]
    lane_rows = local * 2
    cells = n_ex * lane_rows
    clusters, rank, part_width = gate_basis.shape
    plane_tokens = n_ex * tok_rows
    all_rank = n_ex * rank

    placed, cell_token, cell_weight = slot_tables(route_ids, route_weight, cells)
    table = jnp.concatenate([cell_token.astype(FL), cell_weight]).reshape(4, 128)
    flat = (clusters * rank, part_width)
    x_all, dy_all, tables, bases, other = gather_inputs(
        tokens,
        grad_out,
        gate_basis.reshape(flat),
        up_basis.reshape(flat),
        down_basis.reshape(flat),
        table,
        n_ex,
    )
    x_all = x_all.reshape(plane_tokens, width)
    dy_all = dy_all.reshape(plane_tokens, width)
    tables = tables.reshape(n_ex, 2, n_ex, local, 2)
    tables = tables.transpose(1, 2, 3, 0, 4).reshape(2, n_ex, n_ex * lane_rows)
    block = (jnp.arange(n_ex * lane_rows, dtype=jnp.int32) // 2) % n_ex
    named = tables[0].astype(jnp.int32)
    slots = jnp.where(named > 0, named - 1 + tok_rows * block[None, :], -1)
    weights = tables[1]
    cluster = cluster_of.reshape(n_ex, local)[:, 0]

    gate_up = bases[:2].reshape(2 * clusters * rank, width)
    down = bases[2]
    first = dot(gate_up, x_all, 1, 1).astype(BF).reshape(2, clusters * rank, plane_tokens)
    back = dot(down, dy_all, 1, 1).astype(BF)[None]
    rows = jnp.concatenate([first, back])
    member = cluster[:, None] == jnp.arange(clusters, dtype=jnp.int32)[None, :]
    home, dots, kept_rows, kept_units = middle(
        member.astype(FL), rows, slots, weights, gate_factor, up_factor, down_factor, n_dp
    )
    d_gate_factor, d_up_factor, d_down_factor = factor_grads(kept_rows, kept_units)
    summed = combine(cluster, home, slots, weights, clusters, plane_tokens)

    z, x, core = plane_place()
    dots = jnp.sum(dots, axis=0).reshape(n_ex, local, n_ex, 2)
    scores = lax.dynamic_index_in_dim(dots, slab_of(z, x, core), 2, False).reshape(cells)
    scores = scores / jnp.where(cell_weight > 0.0, cell_weight, 1.0)
    grad_route = jnp.sum(jnp.where(placed, scores[None, :], 0.0), axis=1).reshape(route_ids.shape)

    grad_tokens, *terms = send_home(summed, x_all, dy_all, bases, other, tok_rows)
    shape = gate_basis.shape
    return (
        grad_tokens,
        grad_route,
        terms[0].reshape(shape),
        terms[1].reshape(shape),
        terms[2].reshape(shape),
        d_gate_factor,
        d_up_factor,
        d_down_factor,
    )


def solution(mesh):
    rows = P(("dp", "expert"), None)
    basis = P(None, "expert", "dp")
    factor = P("expert", None, "dp")
    low = P("expert", "dp", None)
    in_specs = (rows, rows, rows, rows, P(), basis, basis, basis, factor, factor, low)
    out_specs = (rows, rows, basis, basis, basis, factor, factor, low)
    return jax.shard_map(body, mesh=mesh, in_specs=in_specs, out_specs=out_specs, check_vma=False)
```

```python
import jax
import jax.numpy as jnp
from jax import lax
from jax.experimental import pallas as pl
from jax.experimental.pallas import tpu as pltpu
from jax.sharding import PartitionSpec as P

FL = jnp.float32
BF = jnp.bfloat16
MIB = 1024 * 1024


def dot(a, b, ca, cb):
    return lax.dot_general(a, b, (((ca,), (cb,)), ((), ())), preferred_element_type=FL)


def one_hot(slot_ref, j, tokens):
    row = slot_ref[pl.ds(j, 1), :]
    lanes = row.shape[1]
    grid = lax.broadcasted_iota(jnp.int32, (tokens, lanes), 0)
    return jnp.where(grid == row, 1.0, 0.0).astype(BF)


def combine_kernel(cluster, parts, slots, weights, out, total):
    groups, rank, tokens = parts.shape[0], parts.shape[3], out.shape[2]
    total[...] = jnp.zeros_like(total)

    def step(j, carry):
        c = cluster[j]
        got = parts[j].astype(FL)
        got = jnp.concatenate([got[0], got[1]], axis=2)
        got = jnp.concatenate([got[:2], got[2:] * weights[pl.ds(j, 1), :]], axis=0)
        got = got.astype(BF).reshape(3 * rank, -1)
        add = dot(got, one_hot(slots, j, tokens), 1, 1).reshape(3, rank, tokens)
        total[:, pl.ds(pl.multiple_of(c * rank, rank), rank), :] += add
        return carry

    lax.fori_loop(0, groups, step, 0, unroll=4)
    out[...] = total[...].astype(BF)


def combine(cluster, parts, slots, weights, clusters, tokens):
    rank = parts.shape[3]
    vmem = pl.BlockSpec(memory_space=pltpu.VMEM)
    shape = (3, clusters * rank, tokens)
    return pl.pallas_call(
        combine_kernel,
        out_shape=jax.ShapeDtypeStruct(shape, BF),
        in_specs=[pl.BlockSpec(memory_space=pltpu.SMEM), vmem, vmem, vmem],
        out_specs=vmem,
        scratch_shapes=[pltpu.VMEM(shape, FL)],
        name="combine",
        compiler_params=pltpu.CompilerParams(vmem_limit_bytes=40 * MIB),
    )(cluster, parts, slots, weights)


def mix(tiles):
    first, second = [], []
    for k in range(0, len(tiles), 2):
        a, b = tiles[k], tiles[k + 1]
        h = a.shape[-1] // 2
        first.append(jnp.concatenate([a[:, :h], b[:, :h]], axis=1))
        second.append(jnp.concatenate([a[:, h:], b[:, h:]], axis=1))
    return jnp.concatenate(first, axis=1), jnp.concatenate(second, axis=1)


def split_tiles(a):
    return [a[:, k : k + 128] for k in range(0, a.shape[1], 128)]


def factor_kernel(rows, units, d_gate, d_up, d_down):
    d_gate[0] = dot(rows[0, 0], units[0, 0], 1, 1)
    d_up[0] = dot(rows[0, 1], units[0, 1], 1, 1)
    d_down[0] = dot(units[0, 2], rows[0, 2], 1, 1)


def factor_grads(rows, units):
    count, _, all_rank, lanes = rows.shape
    held = pl.BlockSpec((1,) + rows.shape[1:], lambda g: (g, 0, 0, 0))
    one = pl.BlockSpec((1, all_rank, units.shape[2]), lambda g: (g, 0, 0))
    return pl.pallas_call(
        factor_kernel,
        grid=(count,),
        out_shape=[jax.ShapeDtypeStruct((count, all_rank, units.shape[2]), FL)] * 3,
        in_specs=[held, held],
        out_specs=[one] * 3,
        name="factor_grads",
        compiler_params=pltpu.CompilerParams(vmem_limit_bytes=40 * MIB),
    )(rows, units)


def plane_place():
    e = lax.axis_index("expert")
    return e // 8, (e // 2) % 4, e % 2


def slab_of(z, x, core):
    return core * 16 + z * 4 + x


class Copies:
    def __init__(self, send, recv):
        self.send, self.recv, self.count, self.sent = send, recv, 0, []
        self.row = lax.axis_index("dp")
        self.z, self.x, self.core = plane_place()

    def make(self, src, dst, m, target):
        return pltpu.make_async_remote_copy(
            src_ref=src,
            dst_ref=dst,
            send_sem=self.send.at[m],
            recv_sem=self.recv.at[m],
            device_id=target,
            device_id_type=pl.DeviceIdType.MESH,
        )

    def push(self, src, dst, target, land):
        m = self.count
        self.count += 1
        copy = self.make(src, dst, m, target)
        copy.start()
        self.sent.append(copy)
        return self.make(land, land, m, target).wait_recv

    def device(self, dz, dx, flip=False):
        z, x = (self.z + dz + 4) % 4, (self.x + dx + 4) % 4
        core = 1 - self.core if flip else self.core
        return (self.row, (z * 4 + x) * 2 + core)

    def slab(self, dz, dx, flip=False):
        z, x = (self.z + dz + 4) % 4, (self.x + dx + 4) % 4
        core = 1 - self.core if flip else self.core
        return slab_of(z, x, core)

    def row_device(self, dy):
        e = (self.z * 4 + self.x) * 2 + self.core
        return ((self.row + dy + 4) % 4, e)

    def finish(self):
        for copy in self.sent:
            copy.wait_send()


def meet(targets):
    barrier = pltpu.get_barrier_semaphore()
    for target in targets:
        pl.semaphore_signal(
            barrier, inc=1, device_id=target, device_id_type=pl.DeviceIdType.MESH
        )
    pl.semaphore_wait(barrier, len(targets))


def middle_kernel(
    member, rows, slots, weights, gate, up, down,
    home, dots, kept_rows, kept_units,
    picked, landed, parts, factors, row_store, unit_store, far_in, near_in, summed,
    route, route_in, route_sum,
    out_send, out_recv, back_send, back_recv, dot_send, dot_recv, ring_send, ring_recv,
    loads, local,
):
    c = Copies(ring_send, ring_recv)
    row, e = lax.axis_index("dp"), lax.axis_index("expert")
    groups, rank, tokens = picked.shape[0], picked.shape[3], rows.shape[2]
    lanes = picked.shape[4]
    all_rank = landed.shape[3]

    def everyone(act):
        def step(s, carry):
            act((s * 11) % groups)
            return carry

        lax.fori_loop(1, groups, step, 0)

    def device(d):
        return (row, (e + d) % groups)

    def source(d):
        return (e - d + groups) % groups

    def remote(src, dst, send, recv, target):
        return pltpu.make_async_remote_copy(
            src_ref=src,
            dst_ref=dst,
            send_sem=send,
            recv_sem=recv,
            device_id=target,
            device_id_type=pl.DeviceIdType.MESH,
        )

    def ranks(at):
        return pl.ds(pl.multiple_of(at * rank, rank), rank)

    def out_copy(p, d):
        target = device(d)
        dst = landed.at[p, row, :, ranks(e)]
        return remote(picked.at[target[1], p], dst, out_send.at[p, d], out_recv.at[p, d], target)

    def out_wait(p, d):
        land = landed.at[p, row, :, ranks(source(d))]
        remote(land, land, out_send.at[p, d], out_recv.at[p, d], device(d)).wait_recv()

    def back_copy(p, d):
        target = device(d)
        src = summed.at[p, :, ranks(target[1])]
        return remote(src, home.at[e, p], back_send.at[p, d], back_recv.at[p, d], target)

    def back_wait(p, d):
        land = home.at[source(d), p]
        remote(land, land, back_send.at[p, d], back_recv.at[p, d], device(d)).wait_recv()

    def dot_copy(d):
        return remote(route_sum, dots.at[e], dot_send.at[d], dot_recv.at[d], device(d))

    def dot_wait(d):
        land = dots.at[source(d)]
        remote(land, land, dot_send.at[d], dot_recv.at[d], device(d)).wait_recv()

    def at_row(dy):
        return (row + dy + 4) % 4

    incoming = [
        pltpu.make_async_copy(ref, factors.at[k], loads.at[k])
        for k, ref in enumerate((gate, up, down))
    ]
    for copy in incoming:
        copy.start()
    barrier = pltpu.get_barrier_semaphore()

    def greet(target):
        pl.semaphore_signal(
            barrier, inc=1, device_id=target, device_id_type=pl.DeviceIdType.MESH
        )

    everyone(lambda d: greet(device(d)))
    for dy in (1, -1, 2):
        greet(c.row_device(dy))

    def pick_for(j):
        own = jnp.zeros((3, rank, tokens), BF)
        for k in range(member.shape[1]):
            share = member[pl.ds(j, 1), k : k + 1].astype(BF)[None]
            own = own + rows[:, k * rank : (k + 1) * rank, :] * share
        got = dot(own.reshape(3 * rank, tokens), one_hot(slots, j, tokens), 1, 0)
        got = got.reshape(3, rank, -1)
        got = jnp.concatenate([got[:2], got[2:] * weights[pl.ds(j, 1), :]], axis=0).astype(BF)
        picked[j, 0] = got[:, :, :lanes]
        picked[j, 1] = got[:, :, lanes:]

    pick_for(e)
    own_copies = [
        pltpu.make_async_copy(picked.at[e, p], landed.at[p, row, :, ranks(e)], local.at[p])
        for p in range(2)
    ]
    for copy in own_copies:
        copy.start()
    pl.semaphore_wait(barrier, groups + 2)

    def pick_some(at):
        for s in at:
            pick_for((e + (s * 11) % groups) % groups)
        for s in at:
            out_copy(0, (s * 11) % groups).start()

    pick_some((1, 2, 3))

    def pick_step(n, carry):
        pick_some([4 * n + u for u in range(4)])
        return carry

    lax.fori_loop(1, groups // 4, pick_step, 0)
    everyone(lambda d: out_copy(1, d).start())
    for copy in incoming:
        copy.wait()
    for copy in own_copies:
        copy.wait()
    low, high = pl.ds(0, all_rank // 2), pl.ds(all_rank // 2, all_rank // 2)
    gathers, fars = [], []
    for p in range(2):
        everyone(lambda d: out_wait(p, d))
        own = landed.at[p, row]
        gathers.append(
            (
                c.push(own, own, c.row_device(1), landed.at[p, at_row(-1)]),
                c.push(own, own, c.row_device(-1), landed.at[p, at_row(1)]),
            )
        )
    for p in range(2):
        gathers[p][0]()
        ref = landed.at[p, at_row(-1), :, low]
        far = [c.push(ref, ref, c.row_device(1), landed.at[p, at_row(2), :, low])]
        gathers[p][1]()
        ref = landed.at[p, at_row(1), :, high]
        far.append(c.push(ref, ref, c.row_device(-1), landed.at[p, at_row(2), :, high]))
        fars.append(far)
    stores, far_waits, near_waits = [], [], []
    for p in range(2):
        for wait in fars[p]:
            wait()
        wide = [mix([landed[p, i, k] for i in range(4)]) for k in range(3)]
        results = []
        for n in range(2):
            hg, hu, gm = wide[0][n], wide[1][n], wide[2][n]
            ex = 2 * p + n
            row_store[ex, 0] = hg
            row_store[ex, 1] = hu
            row_store[ex, 2] = gm
            gf, uf, df = factors[0, ex], factors[1, ex], factors[2, ex]
            gate_pre = dot(gf, hg, 0, 0)
            up_pre = dot(uf, hu, 0, 0)
            sig = 1.0 / (1.0 + jnp.exp(-gate_pre))
            act = gate_pre * sig
            slope = sig * (1.0 + gate_pre * (1.0 - sig))
            hidden = (act * up_pre).astype(BF)
            mixed = dot(df, hidden, 0, 0)
            grad_hidden = dot(df, gm, 1, 0)
            grad_gate_pre = (grad_hidden * up_pre * slope).astype(BF)
            grad_up_pre = (grad_hidden * act).astype(BF)
            unit_store[ex, 0] = grad_gate_pre
            unit_store[ex, 1] = grad_up_pre
            unit_store[ex, 2] = hidden
            scores = jnp.sum(mixed * gm.astype(FL), axis=0, keepdims=True)
            each = lanes // 2
            for i in range(4):
                route[i, p : p + 1, n * each : (n + 1) * each] = scores[:, i * each : (i + 1) * each]
            grad_hg = dot(gf, grad_gate_pre, 1, 0)
            grad_hu = dot(uf, grad_up_pre, 1, 0)
            results.append((grad_hg.astype(BF), grad_hu.astype(BF), mixed.astype(BF)))
        for k in range(3):
            tiles = []
            for a, b in zip(split_tiles(results[0][k]), split_tiles(results[1][k])):
                h = a.shape[-1] // 2
                tiles.append(jnp.concatenate([a[:, :h], b[:, :h]], axis=1))
                tiles.append(jnp.concatenate([a[:, h:], b[:, h:]], axis=1))
            for i in range(4):
                parts[p, i, k] = tiles[i]
        ahead, behind = c.row_device(1), c.row_device(-1)
        far = parts.at[p, at_row(2)]
        far_waits.append(
            (
                c.push(far.at[:, low], far_in.at[p, 0], ahead, far_in.at[p, 0]),
                c.push(far.at[:, high], far_in.at[p, 1], behind, far_in.at[p, 1]),
            )
        )
        land = (near_in.at[p, 0, :, high], near_in.at[p, 1, :, low])
        near_waits.append(
            [
                c.push(parts.at[p, at_row(1), :, high], land[0], ahead, land[0]),
                c.push(parts.at[p, at_row(-1), :, low], land[1], behind, land[1]),
            ]
        )
        pair = pl.ds(2 * p, 2)
        here = [
            pltpu.make_async_copy(row_store.at[pair], kept_rows.at[pair], local.at[2 + p]),
            pltpu.make_async_copy(unit_store.at[pair], kept_units.at[pair], local.at[4 + p]),
        ]
        for copy in here:
            copy.start()
        stores += here
    route_waits = []
    for n, dy in enumerate((1, -1, 2)):
        land = route_in.at[n]
        route_waits.append(c.push(route.at[at_row(dy)], land, c.row_device(dy), land))
    for p in range(2):
        for side, dy, half in ((0, 1, low), (1, -1, high)):
            far_waits[p][side]()
            to = at_row(dy)
            more = parts[p, to, :, half].astype(FL) + far_in[p, side].astype(FL)
            parts[p, to, :, half] = more.astype(BF)
            land = near_in.at[p, side, :, half]
            near_waits[p].append(
                c.push(parts.at[p, to, :, half], land, c.row_device(dy), land)
            )
    for wait in route_waits:
        wait()
    route_sum[...] = route[row] + route_in[0] + route_in[1] + route_in[2]
    everyone(lambda d: dot_copy(d).start())
    for p in range(2):
        for wait in near_waits[p]:
            wait()
        total = parts[p, row].astype(FL) + near_in[p, 0].astype(FL) + near_in[p, 1].astype(FL)
        summed[p] = total.astype(BF)
        everyone(lambda d: back_copy(p, d).start())
        own = pltpu.make_async_copy(summed.at[p, :, ranks(e)], home.at[e, p], local.at[6 + p])
        own.start()
        stores.append(own)
    own = pltpu.make_async_copy(route_sum, dots.at[e], local.at[8])
    own.start()
    stores.append(own)
    everyone(dot_wait)
    for p in range(2):
        everyone(lambda d: back_wait(p, d))
    for copy in stores:
        copy.wait()
    for p in range(2):
        everyone(lambda d: out_copy(p, d).wait_send())
        everyone(lambda d: back_copy(p, d).wait_send())
    everyone(lambda d: dot_copy(d).wait_send())
    c.finish()


RING_COPIES = 2 * 4 + 2 * 6 + 3


def middle(member, rows, slots, weights, gate, up, down, n_dp):
    groups, lanes = slots.shape
    kinds, ranks, _ = rows.shape
    count, all_rank, units = gate.shape
    rank = all_rank // groups
    half = lanes // 2
    anywhere = pl.BlockSpec(memory_space=pl.ANY)
    vmem = pl.BlockSpec(memory_space=pltpu.VMEM)
    kept = jax.ShapeDtypeStruct((count, 3, all_rank, n_dp * half // 2), BF)
    dma = pltpu.SemaphoreType.DMA
    return pl.pallas_call(
        middle_kernel,
        out_shape=[
            jax.ShapeDtypeStruct((groups, 2, 3, rank, half), BF),
            jax.ShapeDtypeStruct((groups, 2, half), FL),
            kept,
            kept,
        ],
        in_specs=[vmem] * 4 + [anywhere] * 3,
        out_specs=[anywhere] * 4,
        scratch_shapes=[
            pltpu.VMEM((groups, 2, 3, rank, half), BF),
            pltpu.VMEM((2, n_dp, 3, all_rank, half), BF),
            pltpu.VMEM((2, n_dp, 3, all_rank, half), BF),
            pltpu.VMEM((3,) + gate.shape, BF),
            pltpu.VMEM(kept.shape, BF),
            pltpu.VMEM(kept.shape, BF),
            pltpu.VMEM((2, 2, 3, all_rank // 2, half), BF),
            pltpu.VMEM((2, 2, 3, all_rank, half), BF),
            pltpu.VMEM((2, 3, all_rank, half), BF),
            pltpu.VMEM((n_dp, 2, half), FL),
            pltpu.VMEM((3, 2, half), FL),
            pltpu.VMEM((2, half), FL),
            dma((2, groups)),
            dma((2, groups)),
            dma((2, groups)),
            dma((2, groups)),
            dma((groups,)),
            dma((groups,)),
            dma((RING_COPIES,)),
            dma((RING_COPIES,)),
            dma((3,)),
            dma((9,)),
        ],
        name="middle",
        compiler_params=pltpu.CompilerParams(
            collective_id=2, has_side_effects=True, vmem_limit_bytes=56 * MIB
        ),
    )(member, rows, slots, weights, gate, up, down)


OFFSETS = (0, -1, 1, 2)


class SlabGather:
    def __init__(self, copies, own, out, z_first, halves):
        self.c, self.own, self.out, self.z_first, self.halves = copies, own, out, z_first, halves
        self.across, self.done = [], []
        self.cols = own.shape[-1] // 2

    def at(self, p, q):
        return (p, q) if self.z_first else (q, p)

    def ref(self, p, q, flip=False):
        return self.out.at[self.c.slab(*self.at(p, q), flip)]

    def half(self, ref, h):
        return ref.at[:, pl.ds(h * self.cols, self.cols)] if self.halves else ref

    def to(self, p, q, src, dst, land):
        return self.c.push(src, dst, self.c.device(*self.at(p, q)), land)

    def cross(self, p, q, src=None):
        ref = self.ref(p, q)
        target = self.c.device(0, 0, True)
        self.done.append(
            self.c.push(ref if src is None else src, ref, target, self.ref(p, q, True))
        )

    def spread(self, p, src=None):
        ref = self.ref(p, 0)
        src = ref if src is None else src
        ahead = self.to(0, 1, src, ref, self.ref(p, -1))
        behind = self.to(0, -1, src, ref, self.ref(p, 1))
        self.across.append((p, ahead, behind))

    def start(self):
        me = self.ref(0, 0)
        self.from_behind = self.to(1, 0, self.own, me, self.ref(-1, 0))
        self.from_ahead = self.to(-1, 0, self.own, me, self.ref(1, 0))

    def start_own(self):
        self.spread(0, self.own)
        self.cross(0, 0, self.own)

    def first(self):
        self.from_behind()
        ref, far = self.ref(-1, 0), self.ref(2, 0)
        self.far = [self.to(1, 0, self.half(ref, 0), self.half(ref, 0), self.half(far, 0))]
        self.spread(-1)
        self.cross(-1, 0)

    def second(self):
        self.from_ahead()
        if self.halves:
            ref, far = self.ref(1, 0), self.ref(2, 0)
            self.far.append(self.to(-1, 0, self.half(ref, 1), self.half(ref, 1), self.half(far, 1)))
        self.spread(1)
        self.cross(1, 0)

    def third(self):
        for wait in self.far:
            wait()
        self.spread(2)
        self.cross(2, 0)

    def ring(self, k):
        p, ahead, behind = self.across[k]
        if k == 0:
            self.last = []
        ahead()
        if k < 2:
            ref = self.ref(p, -1)
            self.last.append((p, self.to(0, 1, ref, ref, self.ref(p, 2))))
        self.cross(p, -1)
        behind()
        if k >= 2:
            ref = self.ref(p, 1)
            self.last.append((p, self.to(0, -1, ref, ref, self.ref(p, 2))))
        self.cross(p, 1)

    def end(self, k):
        p, wait = self.last[k]
        wait()
        self.cross(p, 2)

    def finish(self):
        for wait in self.done:
            wait()


def gather_kernel(
    x, dy, gate, up, down, table, xs, dys, tables, bases, other, send, recv, local
):
    c = Copies(send, recv)
    width = gate.shape[1]
    mine = c.slab(0, 0)
    sources = (gate, up, down)

    def columns(k, dy_, rows=None):
        at = pl.ds(pl.multiple_of(((c.row + dy_ + 4) % 4) * width, 128), width)
        ref = bases.at[k, :, at] if rows is None else bases.at[k, rows, at]
        return ref

    def other_columns(k, dy_):
        at = pl.ds(pl.multiple_of(((c.row + dy_ + 4) % 4) * width, 128), width)
        return other.at[k, :, at]

    here = [
        pltpu.make_async_copy(x, xs.at[mine], local.at[0]),
        pltpu.make_async_copy(dy, dys.at[mine], local.at[1]),
        pltpu.make_async_copy(table, tables.at[mine], local.at[2]),
    ]
    for k in range(3):
        here.append(pltpu.make_async_copy(sources[k], columns(k, 0), local.at[3 + k]))
    for copy in here:
        copy.start()
    meet(
        [c.device(0, 1), c.device(0, -1), c.device(1, 0), c.device(-1, 0)]
        + [c.device(0, 0, True), c.row_device(1), c.row_device(-1)]
    )
    parts = [
        SlabGather(c, table, tables, True, False),
        SlabGather(c, x, xs, True, True),
        SlabGather(c, dy, dys, False, True),
    ]
    for part in parts:
        part.start()
    basis_waits, basis_done, basis_far = [], [], []

    def basis_cross(k, dy_):
        if k < 2:
            ref = columns(k, dy_)
            src = sources[k] if dy_ == 0 else ref
            land = other_columns(k, dy_)
            basis_done.append(c.push(src, land, c.device(0, 0, True), land))

    for k in range(3):
        ref = columns(k, 0)
        basis_waits.append(
            (
                c.push(sources[k], ref, c.row_device(1), columns(k, -1)),
                c.push(sources[k], ref, c.row_device(-1), columns(k, 1)),
            )
        )
    for part in parts:
        part.start_own()
    for k in range(3):
        basis_cross(k, 0)
    for part in parts:
        part.first()
    for part in parts:
        part.second()
    for part in parts:
        part.third()
    half = gate.shape[0] // 2
    for step in range(4):
        for part in parts:
            part.ring(step)
        if step < 3:
            ahead, behind = basis_waits[step]
            low, high = pl.ds(0, half), pl.ds(half, half)
            ahead()
            ref = columns(step, -1, low)
            far = [c.push(ref, ref, c.row_device(1), columns(step, 2, low))]
            basis_cross(step, -1)
            behind()
            ref = columns(step, 1, high)
            far.append(c.push(ref, ref, c.row_device(-1), columns(step, 2, high)))
            basis_cross(step, 1)
            basis_far.append(far)
    for k in range(3):
        for wait in basis_far[k]:
            wait()
        basis_cross(k, 2)
    for step in range(4):
        for part in parts:
            part.end(step)
    for part in parts:
        part.finish()
    for wait in basis_done:
        wait()
    for copy in here:
        copy.wait()
    c.finish()


GATHER_COPIES = 32 + 32 + 31 + 20


def gather_inputs(x, dy, gate, up, down, table, n_ex):
    rows, width = gate.shape
    slabs = jax.ShapeDtypeStruct((n_ex,) + x.shape, BF)
    anywhere = pl.BlockSpec(memory_space=pl.ANY)
    return pl.pallas_call(
        gather_kernel,
        out_shape=[
            slabs,
            slabs,
            jax.ShapeDtypeStruct((n_ex,) + table.shape, FL),
            jax.ShapeDtypeStruct((3, rows, 4 * width), BF),
            jax.ShapeDtypeStruct((2, rows, 4 * width), BF),
        ],
        in_specs=[anywhere] * 6,
        out_specs=[anywhere] * 5,
        scratch_shapes=[
            pltpu.SemaphoreType.DMA((GATHER_COPIES,)),
            pltpu.SemaphoreType.DMA((GATHER_COPIES,)),
            pltpu.SemaphoreType.DMA((6,)),
        ],
        name="gather_inputs",
        compiler_params=pltpu.CompilerParams(collective_id=0, has_side_effects=True),
    )(x, dy, gate, up, down, table)


def home_kernel(
    rows, x, dy, bases, other,
    out, d_gate, d_up, d_down,
    paired, xb, db, bb, terms, far_in, near_in, turned, full, got, skipped, passed, kept, last,
    send, recv, loads,
):
    c = Copies(send, recv)
    width = d_gate.shape[1]
    near = (1, -1, 2)
    meet(
        [c.device(0, d) for d in near]
        + [c.device(d, 0) for d in near]
        + [c.device(0, 0, True), c.row_device(1), c.row_device(-1)]
    )
    partner = c.push(rows.at[pl.ds(0, 2)], paired, c.device(0, 0, True), paired)
    order = (2, 1, -1, 0)

    def load_rows(n):
        at = pl.ds(pl.multiple_of(((c.row + order[n] + 4) % 4) * width, 128), width)
        slot = n % 2
        copies = [
            pltpu.make_async_copy(x.at[:, at], xb.at[slot], loads.at[2 * slot]),
            pltpu.make_async_copy(dy.at[:, at], db.at[slot], loads.at[2 * slot + 1]),
        ]
        for copy in copies:
            copy.start()
        return copies

    def load_bases(n):
        at = pl.ds(n * width, width)
        slot = n % 2
        copies = [
            pltpu.make_async_copy(
                bases.at[pl.ds(0, 2), :, at], bb.at[slot, 0], loads.at[4 + 2 * slot]
            ),
            pltpu.make_async_copy(other.at[:, :, at], bb.at[slot, 1], loads.at[5 + 2 * slot]),
        ]
        for copy in copies:
            copy.start()
        return copies

    flying = [load_rows(0), load_rows(1)]
    basis_flying = [load_bases(0), load_bases(1)]
    low, high = pl.ds(0, 64), pl.ds(64, 64)
    near_waits = [[], []]
    far_waits = [[], []]
    for n in range(4):
        for copy in flying[n]:
            copy.wait()
        slot = n % 2

        def columns(k, carry):
            at = pl.ds(pl.multiple_of(k * 256, 256), 256)
            ups = dot(rows[0:2].reshape(256, -1), xb[slot, :, at], 1, 0)
            downs = dot(rows[2], db[slot, :, at], 1, 0)
            if n < 3:
                terms[n, 0, :, at] = ups[:128].astype(BF)
                terms[n, 1, :, at] = ups[128:].astype(BF)
                terms[n, 2, :, at] = downs.astype(BF)
            else:
                d_gate[:, at] = ups[:128]
                d_up[:, at] = ups[128:]
                d_down[:, at] = downs
            return carry

        lax.fori_loop(0, width // 256, columns, 0)
        if n < 2:
            flying.append(load_rows(n + 2))
        for k in range(3):
            if n == 0:
                land = far_in.at[0, k]
                far_waits[0].append(c.push(terms.at[0, k, low], land, c.row_device(1), land))
                land = far_in.at[1, k]
                far_waits[1].append(c.push(terms.at[0, k, high], land, c.row_device(-1), land))
            if n == 1:
                land = near_in.at[0, k, high]
                near_waits[0].append(c.push(terms.at[1, k, high], land, c.row_device(1), land))
            if n == 2:
                land = near_in.at[1, k, low]
                near_waits[1].append(c.push(terms.at[2, k, low], land, c.row_device(-1), land))
    partner()
    half_tokens = turned.shape[0]
    mine = pl.ds(pl.multiple_of(c.core * half_tokens, 128), half_tokens)
    for k in range(2):
        for n, source in enumerate((rows, paired)):
            at = pl.ds((2 * n + k) * 128, 128)
            turned[:, at] = source[k, :, mine].astype(FL).T.astype(BF)
    tok = full.shape[2]
    place = (c.z, c.x)
    got_waits = [{}, {}]
    cross_waits = []
    via_ahead, via_behind = (1, -1), (2, 0)

    def group(h, d, b):
        if h == 0:
            return ((c.z + b + 4) % 4) * 4 + (c.x + d + 4) % 4
        return ((c.z + d + 4) % 4) * 4 + (c.x + b + 4) % 4

    def along(h, d):
        return c.device(0, d) if h == 0 else c.device(d, 0)

    def cross_far(h):
        waits = []
        for d, which in ((1, via_ahead), (-1, via_behind)):
            for k, b in enumerate(which):
                land = skipped.at[h, d % 3 - 1, k]
                waits.append((d, b, k, c.push(full.at[h, group(h, 2, b)], land, along(h, d), land)))
        for d, which in ((1, via_behind), (-1, via_ahead)):
            for b in which:
                cross_push(h, d, b)
        return waits

    def cross_push(h, d, b):
        land = got.at[h, d % 3 - 1, b % 4]
        wait = c.push(full.at[h, group(h, d, b)], land, along(h, d), land)
        got_waits[h].setdefault(b, []).append(wait)

    def cross_near(h):
        for d, b, k, wait in cross_waits[h]:
            wait()
            slab = group(h, d, b)
            more = full[h, slab].astype(FL) + skipped[h, d % 3 - 1, k].astype(FL)
            full[h, slab] = more.astype(BF)
            cross_push(h, d, b)

    for n in range(4):
        for copy in basis_flying[n]:
            copy.wait()
        slot, h = n % 2, n // 2

        def token_columns(k, carry):
            at = pl.ds(pl.multiple_of(k * 256, 256), 256)
            to = pl.ds(pl.multiple_of((n % 2) * width + k * 256, 256), 256)
            both = jnp.concatenate(
                [bb[slot, s, k2, :, at] for s in range(2) for k2 in range(2)], axis=0
            )
            sums = dot(turned[...], both, 1, 0)
            for s in range(16):
                full[h, s, :, to] = sums[s * tok : (s + 1) * tok].astype(BF)
            return carry

        lax.fori_loop(0, width // 256, token_columns, 0)
        if n < 2:
            basis_flying.append(load_bases(n + 2))
        if n % 2 == 1:
            cross_waits.append(cross_far(h))
    for h in range(2):
        cross_near(h)
    for k in range(3):
        far_waits[0][k]()
        terms[1, k, low] = (terms[1, k, low].astype(FL) + far_in[0, k].astype(FL)).astype(BF)
        land = near_in.at[0, k, low]
        near_waits[0].append(c.push(terms.at[1, k, low], land, c.row_device(1), land))
        far_waits[1][k]()
        terms[2, k, high] = (terms[2, k, high].astype(FL) + far_in[1, k].astype(FL)).astype(BF)
        land = near_in.at[1, k, high]
        near_waits[1].append(c.push(terms.at[2, k, high], land, c.row_device(-1), land))
    last_waits = [[], []]
    for step, b in enumerate((1, -1, 2, 0)):
        for h in range(2):
            for wait in got_waits[h][b]:
                wait()
            slab = group(h, 0, b)
            target = c.device(b, 0) if h == 0 else c.device(0, b)
            total = full[h, slab].astype(FL)
            for side in range(2):
                total = total + got[h, side, b % 4].astype(FL)
            if b == 0:
                kept[h] = total
            else:
                passed[h, step] = total.astype(BF)
                land = last.at[h, step]
                last_waits[h].append(c.push(passed.at[h, step], land, target, land))
    for h in range(2):
        for wait in last_waits[h]:
            wait()
        total = kept[h]
        for step in range(3):
            total = total + last[h, step].astype(FL)
        out[:, h * 2 * width : (h + 1) * 2 * width] = total.astype(BF)
    for side in range(2):
        for wait in near_waits[side]:
            wait()
    for k, ref in enumerate((d_gate, d_up, d_down)):
        ref[...] = ref[...] + near_in[0, k].astype(FL) + near_in[1, k].astype(FL)
    c.finish()


HOME_COPIES = 1 + 18 + 24 + 6


def send_home(rows, x, dy, bases, other, tok):
    kinds, ranks, tokens = rows.shape
    full_width = x.shape[1]
    width = full_width // 4
    half = full_width // 2
    anywhere = pl.BlockSpec(memory_space=pl.ANY)
    vmem = pl.BlockSpec(memory_space=pltpu.VMEM)
    basis = jax.ShapeDtypeStruct((ranks, width), FL)
    return pl.pallas_call(
        home_kernel,
        out_shape=[jax.ShapeDtypeStruct((tok, full_width), BF), basis, basis, basis],
        in_specs=[vmem] + [anywhere] * 4,
        out_specs=[vmem] * 4,
        scratch_shapes=[
            pltpu.VMEM((2, ranks, tokens), BF),
            pltpu.VMEM((2, tokens, width), BF),
            pltpu.VMEM((2, tokens, width), BF),
            pltpu.VMEM((2, 2, 2, ranks, width), BF),
            pltpu.VMEM((3, kinds, ranks, width), BF),
            pltpu.VMEM((2, kinds, ranks // 2, width), BF),
            pltpu.VMEM((2, kinds, ranks, width), BF),
            pltpu.VMEM((tokens // 2, 4 * ranks), BF),
            pltpu.VMEM((2, 16, tok, half), BF),
            pltpu.VMEM((2, 2, 4, tok, half), BF),
            pltpu.VMEM((2, 2, 2, tok, half), BF),
            pltpu.VMEM((2, 3, tok, half), BF),
            pltpu.VMEM((2, tok, half), FL),
            pltpu.VMEM((2, 3, tok, half), BF),
            pltpu.SemaphoreType.DMA((HOME_COPIES,)),
            pltpu.SemaphoreType.DMA((HOME_COPIES,)),
            pltpu.SemaphoreType.DMA((8,)),
        ],
        name="send_home",
        compiler_params=pltpu.CompilerParams(
            collective_id=1, has_side_effects=True, vmem_limit_bytes=60 * MIB
        ),
    )(rows, x, dy, bases, other)


def slot_tables(route_ids, route_weight, cells):
    flat = route_ids.reshape(-1)
    pairs = flat.shape[0]
    at = jnp.arange(pairs, dtype=jnp.int32)
    earlier = (flat[:, None] == flat[None, :]) & (at[None, :] < at[:, None])
    slot = jnp.sum(earlier.astype(jnp.int32), axis=1)
    placed = (flat * 2 + slot)[:, None] == jnp.arange(cells, dtype=jnp.int32)[None, :]
    token = at // route_ids.shape[1] + 1
    cell_token = jnp.sum(jnp.where(placed, token[:, None], 0), axis=0)
    cell_weight = jnp.sum(
        jnp.where(placed, route_weight.reshape(-1)[:, None].astype(FL), 0.0), axis=0
    )
    return placed, cell_token, cell_weight


def body(
    tokens,
    grad_out,
    route_ids,
    route_weight,
    cluster_of,
    gate_basis,
    up_basis,
    down_basis,
    gate_factor,
    up_factor,
    down_factor,
):
    n_dp = lax.axis_size("dp")
    n_ex = lax.axis_size("expert")
    tok_rows, width = tokens.shape
    local = gate_factor.shape[0]
    lane_rows = local * 2
    cells = n_ex * lane_rows
    clusters, rank, part_width = gate_basis.shape
    plane_tokens = n_ex * tok_rows
    all_rank = n_ex * rank

    placed, cell_token, cell_weight = slot_tables(route_ids, route_weight, cells)
    table = jnp.concatenate([cell_token.astype(FL), cell_weight]).reshape(4, 128)
    flat = (clusters * rank, part_width)
    x_all, dy_all, tables, bases, other = gather_inputs(
        tokens,
        grad_out,
        gate_basis.reshape(flat),
        up_basis.reshape(flat),
        down_basis.reshape(flat),
        table,
        n_ex,
    )
    x_all = x_all.reshape(plane_tokens, width)
    dy_all = dy_all.reshape(plane_tokens, width)
    tables = tables.reshape(n_ex, 2, n_ex, local, 2)
    tables = tables.transpose(1, 2, 3, 0, 4).reshape(2, n_ex, n_ex * lane_rows)
    block = (jnp.arange(n_ex * lane_rows, dtype=jnp.int32) // 2) % n_ex
    named = tables[0].astype(jnp.int32)
    slots = jnp.where(named > 0, named - 1 + tok_rows * block[None, :], -1)
    weights = tables[1]
    cluster = cluster_of.reshape(n_ex, local)[:, 0]

    gate_up = bases[:2].reshape(2 * clusters * rank, width)
    down = bases[2]
    first = dot(gate_up, x_all, 1, 1).astype(BF).reshape(2, clusters * rank, plane_tokens)
    back = dot(down, dy_all, 1, 1).astype(BF)[None]
    rows = jnp.concatenate([first, back])
    member = cluster[:, None] == jnp.arange(clusters, dtype=jnp.int32)[None, :]
    home, dots, kept_rows, kept_units = middle(
        member.astype(FL), rows, slots, weights, gate_factor, up_factor, down_factor, n_dp
    )
    d_gate_factor, d_up_factor, d_down_factor = factor_grads(kept_rows, kept_units)
    summed = combine(cluster, home, slots, weights, clusters, plane_tokens)

    z, x, core = plane_place()
    dots = dots.reshape(n_ex, local, n_ex, 2)
    scores = lax.dynamic_index_in_dim(dots, slab_of(z, x, core), 2, False).reshape(cells)
    scores = scores / jnp.where(cell_weight > 0.0, cell_weight, 1.0)
    grad_route = jnp.sum(jnp.where(placed, scores[None, :], 0.0), axis=1).reshape(route_ids.shape)

    grad_tokens, *terms = send_home(summed, x_all, dy_all, bases, other, tok_rows)
    shape = gate_basis.shape
    return (
        grad_tokens,
        grad_route,
        terms[0].reshape(shape),
        terms[1].reshape(shape),
        terms[2].reshape(shape),
        d_gate_factor,
        d_up_factor,
        d_down_factor,
    )


def solution(mesh):
    rows = P(("dp", "expert"), None)
    basis = P(None, "expert", "dp")
    factor = P("expert", None, "dp")
    low = P("expert", "dp", None)
    in_specs = (rows, rows, rows, rows, P(), basis, basis, basis, factor, factor, low)
    out_specs = (rows, rows, basis, basis, basis, factor, factor, low)
    return jax.shard_map(body, mesh=mesh, in_specs=in_specs, out_specs=out_specs, check_vma=False)
```

```python
import jax
import jax.numpy as jnp
from jax import lax
from jax.experimental import pallas as pl
from jax.experimental.pallas import tpu as pltpu
from jax.sharding import PartitionSpec as P

FL = jnp.float32
BF = jnp.bfloat16
MIB = 1024 * 1024


def dot(a, b, ca, cb):
    return lax.dot_general(a, b, (((ca,), (cb,)), ((), ())), preferred_element_type=FL)


def one_hot(slot_ref, j, tokens):
    row = slot_ref[pl.ds(j, 1), :]
    lanes = row.shape[1]
    grid = lax.broadcasted_iota(jnp.int32, (tokens, lanes), 0)
    return jnp.where(grid == row, 1.0, 0.0).astype(BF)


def combine_kernel(cluster, parts, slots, weights, out, total):
    groups, rank, tokens = parts.shape[0], parts.shape[3], out.shape[2]
    total[...] = jnp.zeros_like(total)

    def step(j, carry):
        c = cluster[j]
        got = parts[j].astype(FL)
        got = jnp.concatenate([got[0], got[1]], axis=2)
        got = jnp.concatenate([got[:2], got[2:] * weights[pl.ds(j, 1), :]], axis=0)
        got = got.astype(BF).reshape(3 * rank, -1)
        add = dot(got, one_hot(slots, j, tokens), 1, 1).reshape(3, rank, tokens)
        total[:, pl.ds(pl.multiple_of(c * rank, rank), rank), :] += add
        return carry

    lax.fori_loop(0, groups, step, 0, unroll=4)
    out[...] = total[...].astype(BF)


def combine(cluster, parts, slots, weights, clusters, tokens):
    rank = parts.shape[3]
    vmem = pl.BlockSpec(memory_space=pltpu.VMEM)
    shape = (3, clusters * rank, tokens)
    return pl.pallas_call(
        combine_kernel,
        out_shape=jax.ShapeDtypeStruct(shape, BF),
        in_specs=[pl.BlockSpec(memory_space=pltpu.SMEM), vmem, vmem, vmem],
        out_specs=vmem,
        scratch_shapes=[pltpu.VMEM(shape, FL)],
        name="combine",
        compiler_params=pltpu.CompilerParams(vmem_limit_bytes=60 * MIB),
    )(cluster, parts, slots, weights)


def mix(tiles):
    first, second = [], []
    for k in range(0, len(tiles), 2):
        a, b = tiles[k], tiles[k + 1]
        h = a.shape[-1] // 2
        first.append(jnp.concatenate([a[:, :h], b[:, :h]], axis=1))
        second.append(jnp.concatenate([a[:, h:], b[:, h:]], axis=1))
    return jnp.concatenate(first, axis=1), jnp.concatenate(second, axis=1)


def split_tiles(a):
    return [a[:, k : k + 128] for k in range(0, a.shape[1], 128)]


def factor_kernel(rows, units, *refs):
    sources, (d_gate, d_up, d_down), results = refs[:4], refs[4:7], refs[7:]
    d_gate[0] = dot(rows[0, 0], units[0, 0], 1, 1)
    d_up[0] = dot(rows[0, 1], units[0, 1], 1, 1)
    d_down[0] = dot(units[0, 2], rows[0, 2], 1, 1)
    for source, result in zip(sources, results):
        result[...] = source[...]


def factor_grads(rows, units, passing):
    count, _, all_rank, lanes = rows.shape
    held = pl.BlockSpec((1,) + rows.shape[1:], lambda g: (g, 0, 0, 0))
    one = pl.BlockSpec((1, all_rank, units.shape[2]), lambda g: (g, 0, 0))
    tok, width = passing[0].shape
    ranks, part = passing[1].shape
    passed = [pl.BlockSpec((tok, width // count), lambda g: (0, g))]
    passed += [pl.BlockSpec((ranks // count, part), lambda g: (g, 0))] * 3
    factor = jax.ShapeDtypeStruct((count, all_rank, units.shape[2]), FL)
    return pl.pallas_call(
        factor_kernel,
        grid=(count,),
        out_shape=[factor] * 3 + [jax.ShapeDtypeStruct(a.shape, a.dtype) for a in passing],
        in_specs=[held, held] + passed,
        out_specs=[one] * 3 + passed,
        name="factor_grads",
        compiler_params=pltpu.CompilerParams(vmem_limit_bytes=60 * MIB),
    )(rows, units, *passing)


def plane_place():
    e = lax.axis_index("expert")
    return e // 8, (e // 2) % 4, e % 2


def slab_of(z, x, core):
    return core * 16 + z * 4 + x


class Copies:
    def __init__(self, send, recv):
        self.send, self.recv, self.count, self.sent = send, recv, 0, []
        self.row = lax.axis_index("dp")
        self.z, self.x, self.core = plane_place()

    def make(self, src, dst, m, target):
        return pltpu.make_async_remote_copy(
            src_ref=src,
            dst_ref=dst,
            send_sem=self.send.at[m],
            recv_sem=self.recv.at[m],
            device_id=target,
            device_id_type=pl.DeviceIdType.MESH,
        )

    def push(self, src, dst, target, land):
        m = self.count
        self.count += 1
        copy = self.make(src, dst, m, target)
        copy.start()
        self.sent.append(copy)
        return self.make(land, land, m, target).wait_recv

    def device(self, dz, dx, flip=False):
        z, x = (self.z + dz + 4) % 4, (self.x + dx + 4) % 4
        core = 1 - self.core if flip else self.core
        return (self.row, (z * 4 + x) * 2 + core)

    def slab(self, dz, dx, flip=False):
        z, x = (self.z + dz + 4) % 4, (self.x + dx + 4) % 4
        core = 1 - self.core if flip else self.core
        return slab_of(z, x, core)

    def row_device(self, dy):
        e = (self.z * 4 + self.x) * 2 + self.core
        return ((self.row + dy + 4) % 4, e)

    def finish(self):
        for copy in self.sent:
            copy.wait_send()


def meet(targets):
    barrier = pltpu.get_barrier_semaphore()
    for target in targets:
        pl.semaphore_signal(
            barrier, inc=1, device_id=target, device_id_type=pl.DeviceIdType.MESH
        )
    pl.semaphore_wait(barrier, len(targets))


def middle_kernel(
    member, rows, slots, weights, gate, up, down,
    home, dots, kept_rows, kept_units,
    picked, chosen, landed, parts, factors, row_store, unit_store, far_in, near_in, summed,
    route, route_in, route_sum,
    out_send, out_recv, back_send, back_recv, dot_send, dot_recv, ring_send, ring_recv,
    loads, local,
):
    c = Copies(ring_send, ring_recv)
    row, e = lax.axis_index("dp"), lax.axis_index("expert")
    groups, rank, tokens = picked.shape[0], picked.shape[3], rows.shape[2]
    lanes = picked.shape[4]
    all_rank = landed.shape[3]

    def everyone(act):
        def step(s, carry):
            act((s * 11) % groups)
            return carry

        lax.fori_loop(1, groups, step, 0)

    def device(d):
        return (row, (e + d) % groups)

    def source(d):
        return (e - d + groups) % groups

    def remote(src, dst, send, recv, target):
        return pltpu.make_async_remote_copy(
            src_ref=src,
            dst_ref=dst,
            send_sem=send,
            recv_sem=recv,
            device_id=target,
            device_id_type=pl.DeviceIdType.MESH,
        )

    def ranks(at):
        return pl.ds(pl.multiple_of(at * rank, rank), rank)

    def out_copy(p, d):
        target = device(d)
        dst = landed.at[p, row, :, ranks(e)]
        return remote(picked.at[target[1], p], dst, out_send.at[p, d], out_recv.at[p, d], target)

    def out_wait(p, d):
        land = landed.at[p, row, :, ranks(source(d))]
        remote(land, land, out_send.at[p, d], out_recv.at[p, d], device(d)).wait_recv()

    def back_copy(p, d):
        target = device(d)
        src = summed.at[p, :, ranks(target[1])]
        return remote(src, home.at[e, p], back_send.at[p, d], back_recv.at[p, d], target)

    def back_wait(p, d):
        land = home.at[source(d), p]
        remote(land, land, back_send.at[p, d], back_recv.at[p, d], device(d)).wait_recv()

    def dot_copy(d):
        return remote(route_sum, dots.at[e], dot_send.at[d], dot_recv.at[d], device(d))

    def dot_wait(d):
        land = dots.at[source(d)]
        remote(land, land, dot_send.at[d], dot_recv.at[d], device(d)).wait_recv()

    def at_row(dy):
        return (row + dy + 4) % 4

    incoming = [
        pltpu.make_async_copy(ref, factors.at[k], loads.at[k])
        for k, ref in enumerate((gate, up, down))
    ]
    for copy in incoming:
        copy.start()
    barrier = pltpu.get_barrier_semaphore()

    def greet(target):
        pl.semaphore_signal(
            barrier, inc=1, device_id=target, device_id_type=pl.DeviceIdType.MESH
        )

    everyone(lambda d: greet(device(d)))
    for dy in (1, -1, 2):
        greet(c.row_device(dy))

    def own_for(j):
        own = jnp.zeros((3, rank, tokens), BF)
        for k in range(member.shape[1]):
            share = member[pl.ds(j, 1), k : k + 1].astype(BF)[None]
            own = own + rows[:, k * rank : (k + 1) * rank, :] * share
        chosen[j] = own.reshape(3 * rank, tokens)

    def pick_for(j, p):
        at = slice(p * lanes, (p + 1) * lanes)
        grid = lax.broadcasted_iota(jnp.int32, (tokens, lanes), 0)
        hot = jnp.where(grid == slots[pl.ds(j, 1), :][:, at], 1.0, 0.0).astype(BF)
        got = dot(chosen[j], hot, 1, 0).reshape(3, rank, lanes)
        picked[j, p, 0:2] = got[:2].astype(BF)
        picked[j, p, 2] = (got[2] * weights[pl.ds(j, 1), :][:, at]).astype(BF)

    own_for(e)
    for p in range(2):
        pick_for(e, p)
    own_copies = [
        pltpu.make_async_copy(picked.at[e, p], landed.at[p, row, :, ranks(e)], local.at[p])
        for p in range(2)
    ]
    for copy in own_copies:
        copy.start()
    pl.semaphore_wait(barrier, groups + 2)

    def pick_some(p, at):
        for s in at:
            j = (e + (s * 11) % groups) % groups
            if p == 0:
                own_for(j)
            pick_for(j, p)
        for s in at:
            out_copy(p, (s * 11) % groups).start()

    for p in range(2):
        pick_some(p, (1, 2, 3))

        def pick_step(n, carry):
            pick_some(p, [4 * n + u for u in range(4)])
            return carry

        lax.fori_loop(1, groups // 4, pick_step, 0)
    for copy in incoming:
        copy.wait()
    for copy in own_copies:
        copy.wait()
    low, high = pl.ds(0, all_rank // 2), pl.ds(all_rank // 2, all_rank // 2)
    gathers, fars = [], []
    for p in range(2):
        everyone(lambda d: out_wait(p, d))
        own = landed.at[p, row]
        gathers.append(
            (
                c.push(own, own, c.row_device(1), landed.at[p, at_row(-1)]),
                c.push(own, own, c.row_device(-1), landed.at[p, at_row(1)]),
            )
        )
    for p in range(2):
        gathers[p][0]()
        ref = landed.at[p, at_row(-1), :, low]
        far = [c.push(ref, ref, c.row_device(1), landed.at[p, at_row(2), :, low])]
        gathers[p][1]()
        ref = landed.at[p, at_row(1), :, high]
        far.append(c.push(ref, ref, c.row_device(-1), landed.at[p, at_row(2), :, high]))
        fars.append(far)
    stores, far_waits, near_waits = [], [], []
    for p in range(2):
        for wait in fars[p]:
            wait()
        wide = [mix([landed[p, i, k] for i in range(4)]) for k in range(3)]
        results = []
        for n in range(2):
            hg, hu, gm = wide[0][n], wide[1][n], wide[2][n]
            ex = 2 * p + n
            row_store[ex, 0] = hg
            row_store[ex, 1] = hu
            row_store[ex, 2] = gm
            gf, uf, df = factors[0, ex], factors[1, ex], factors[2, ex]
            gate_pre = dot(gf, hg, 0, 0)
            up_pre = dot(uf, hu, 0, 0)
            sig = 1.0 / (1.0 + jnp.exp(-gate_pre))
            act = gate_pre * sig
            slope = sig * (1.0 + gate_pre * (1.0 - sig))
            hidden = (act * up_pre).astype(BF)
            mixed = dot(df, hidden, 0, 0)
            grad_hidden = dot(df, gm, 1, 0)
            grad_gate_pre = (grad_hidden * up_pre * slope).astype(BF)
            grad_up_pre = (grad_hidden * act).astype(BF)
            unit_store[ex, 0] = grad_gate_pre
            unit_store[ex, 1] = grad_up_pre
            unit_store[ex, 2] = hidden
            scores = jnp.sum(mixed * gm.astype(FL), axis=0, keepdims=True)
            each = lanes // 2
            for i in range(4):
                route[i, p : p + 1, n * each : (n + 1) * each] = scores[:, i * each : (i + 1) * each]
            grad_hg = dot(gf, grad_gate_pre, 1, 0)
            grad_hu = dot(uf, grad_up_pre, 1, 0)
            results.append((grad_hg.astype(BF), grad_hu.astype(BF), mixed.astype(BF)))
        for k in range(3):
            tiles = []
            for a, b in zip(split_tiles(results[0][k]), split_tiles(results[1][k])):
                h = a.shape[-1] // 2
                tiles.append(jnp.concatenate([a[:, :h], b[:, :h]], axis=1))
                tiles.append(jnp.concatenate([a[:, h:], b[:, h:]], axis=1))
            for i in range(4):
                parts[p, i, k] = tiles[i]
        ahead, behind = c.row_device(1), c.row_device(-1)
        far = parts.at[p, at_row(2)]
        far_waits.append(
            (
                c.push(far.at[:, low], far_in.at[p, 0], ahead, far_in.at[p, 0]),
                c.push(far.at[:, high], far_in.at[p, 1], behind, far_in.at[p, 1]),
            )
        )
        land = (near_in.at[p, 0, :, high], near_in.at[p, 1, :, low])
        near_waits.append(
            [
                c.push(parts.at[p, at_row(1), :, high], land[0], ahead, land[0]),
                c.push(parts.at[p, at_row(-1), :, low], land[1], behind, land[1]),
            ]
        )
        pair = pl.ds(2 * p, 2)
        here = [
            pltpu.make_async_copy(row_store.at[pair], kept_rows.at[pair], local.at[2 + p]),
            pltpu.make_async_copy(unit_store.at[pair], kept_units.at[pair], local.at[4 + p]),
        ]
        for copy in here:
            copy.start()
        stores += here
    route_waits = []
    for n, dy in enumerate((1, -1, 2)):
        land = route_in.at[n]
        route_waits.append(c.push(route.at[at_row(dy)], land, c.row_device(dy), land))
    for p in range(2):
        for side, dy, half in ((0, 1, low), (1, -1, high)):
            far_waits[p][side]()
            to = at_row(dy)
            more = parts[p, to, :, half].astype(FL) + far_in[p, side].astype(FL)
            parts[p, to, :, half] = more.astype(BF)
            land = near_in.at[p, side, :, half]
            near_waits[p].append(
                c.push(parts.at[p, to, :, half], land, c.row_device(dy), land)
            )
    for wait in route_waits:
        wait()
    route_sum[...] = route[row] + route_in[0] + route_in[1] + route_in[2]
    everyone(lambda d: dot_copy(d).start())
    for p in range(2):
        for wait in near_waits[p]:
            wait()
        total = parts[p, row].astype(FL) + near_in[p, 0].astype(FL) + near_in[p, 1].astype(FL)
        summed[p] = total.astype(BF)
        everyone(lambda d: back_copy(p, d).start())
        own = pltpu.make_async_copy(summed.at[p, :, ranks(e)], home.at[e, p], local.at[6 + p])
        own.start()
        stores.append(own)
    own = pltpu.make_async_copy(route_sum, dots.at[e], local.at[8])
    own.start()
    stores.append(own)
    everyone(dot_wait)
    for p in range(2):
        everyone(lambda d: back_wait(p, d))
    for copy in stores:
        copy.wait()
    for p in range(2):
        everyone(lambda d: out_copy(p, d).wait_send())
        everyone(lambda d: back_copy(p, d).wait_send())
    everyone(lambda d: dot_copy(d).wait_send())
    c.finish()


RING_COPIES = 2 * 4 + 2 * 6 + 3


def middle(member, rows, slots, weights, gate, up, down, n_dp):
    groups, lanes = slots.shape
    kinds, ranks, _ = rows.shape
    count, all_rank, units = gate.shape
    rank = all_rank // groups
    half = lanes // 2
    anywhere = pl.BlockSpec(memory_space=pl.ANY)
    vmem = pl.BlockSpec(memory_space=pltpu.VMEM)
    kept = jax.ShapeDtypeStruct((count, 3, all_rank, n_dp * half // 2), BF)
    dma = pltpu.SemaphoreType.DMA
    return pl.pallas_call(
        middle_kernel,
        out_shape=[
            jax.ShapeDtypeStruct((groups, 2, 3, rank, half), BF),
            jax.ShapeDtypeStruct((groups, 2, half), FL),
            kept,
            kept,
        ],
        in_specs=[vmem] * 4 + [anywhere] * 3,
        out_specs=[anywhere] * 4,
        scratch_shapes=[
            pltpu.VMEM((groups, 2, 3, rank, half), BF),
            pltpu.VMEM((groups, 3 * rank, rows.shape[2]), BF),
            pltpu.VMEM((2, n_dp, 3, all_rank, half), BF),
            pltpu.VMEM((2, n_dp, 3, all_rank, half), BF),
            pltpu.VMEM((3,) + gate.shape, BF),
            pltpu.VMEM(kept.shape, BF),
            pltpu.VMEM(kept.shape, BF),
            pltpu.VMEM((2, 2, 3, all_rank // 2, half), BF),
            pltpu.VMEM((2, 2, 3, all_rank, half), BF),
            pltpu.VMEM((2, 3, all_rank, half), BF),
            pltpu.VMEM((n_dp, 2, half), FL),
            pltpu.VMEM((3, 2, half), FL),
            pltpu.VMEM((2, half), FL),
            dma((2, groups)),
            dma((2, groups)),
            dma((2, groups)),
            dma((2, groups)),
            dma((groups,)),
            dma((groups,)),
            dma((RING_COPIES,)),
            dma((RING_COPIES,)),
            dma((3,)),
            dma((9,)),
        ],
        name="middle",
        compiler_params=pltpu.CompilerParams(
            collective_id=2, has_side_effects=True, vmem_limit_bytes=56 * MIB
        ),
    )(member, rows, slots, weights, gate, up, down)


OFFSETS = (0, -1, 1, 2)


class SlabGather:
    def __init__(self, copies, own, out, z_first, halves):
        self.c, self.own, self.out, self.z_first, self.halves = copies, own, out, z_first, halves
        self.across, self.done = [], []
        self.cols = own.shape[-1] // 2

    def at(self, p, q):
        return (p, q) if self.z_first else (q, p)

    def ref(self, p, q, flip=False):
        return self.out.at[self.c.slab(*self.at(p, q), flip)]

    def half(self, ref, h):
        return ref.at[:, pl.ds(h * self.cols, self.cols)] if self.halves else ref

    def to(self, p, q, src, dst, land):
        return self.c.push(src, dst, self.c.device(*self.at(p, q)), land)

    def cross(self, p, q, src=None):
        ref = self.ref(p, q)
        target = self.c.device(0, 0, True)
        self.done.append(
            self.c.push(ref if src is None else src, ref, target, self.ref(p, q, True))
        )

    def spread(self, p, src=None):
        ref = self.ref(p, 0)
        src = ref if src is None else src
        ahead = self.to(0, 1, src, ref, self.ref(p, -1))
        behind = self.to(0, -1, src, ref, self.ref(p, 1))
        self.across.append((p, ahead, behind))

    def start(self):
        me = self.ref(0, 0)
        self.from_behind = self.to(1, 0, self.own, me, self.ref(-1, 0))
        self.from_ahead = self.to(-1, 0, self.own, me, self.ref(1, 0))

    def start_own(self):
        self.spread(0, self.own)
        self.cross(0, 0, self.own)

    def first(self):
        self.from_behind()
        ref, far = self.ref(-1, 0), self.ref(2, 0)
        self.far = [self.to(1, 0, self.half(ref, 0), self.half(ref, 0), self.half(far, 0))]
        self.spread(-1)
        self.cross(-1, 0)

    def second(self):
        self.from_ahead()
        if self.halves:
            ref, far = self.ref(1, 0), self.ref(2, 0)
            self.far.append(self.to(-1, 0, self.half(ref, 1), self.half(ref, 1), self.half(far, 1)))
        self.spread(1)
        self.cross(1, 0)

    def third(self):
        for wait in self.far:
            wait()
        self.spread(2)
        self.cross(2, 0)

    def ring(self, k):
        p, ahead, behind = self.across[k]
        if k == 0:
            self.last = []
        ahead()
        if k < 2:
            ref = self.ref(p, -1)
            self.last.append((p, self.to(0, 1, ref, ref, self.ref(p, 2))))
        self.cross(p, -1)
        behind()
        if k >= 2:
            ref = self.ref(p, 1)
            self.last.append((p, self.to(0, -1, ref, ref, self.ref(p, 2))))
        self.cross(p, 1)

    def end(self, k):
        p, wait = self.last[k]
        wait()
        self.cross(p, 2)

    def finish(self):
        for wait in self.done:
            wait()


def gather_kernel(
    x, dy, gate, up, down, table, xs, dys, tables, first, last, other, turned,
    basis_held, basis_turned, send, recv, local, basis_sems, turned_sems,
):
    c = Copies(send, recv)
    width = gate.shape[1]
    mine = c.slab(0, 0)
    sources = (gate, up, down)

    def columns(k, dy_, rows=None):
        at = pl.ds(pl.multiple_of(((c.row + dy_ + 4) % 4) * width, 128), width)
        whole = first.at[k] if k < 2 else last
        return whole.at[:, at] if rows is None else whole.at[rows, at]

    def other_columns(k, dy_):
        at = pl.ds(pl.multiple_of(((c.row + dy_ + 4) % 4) * width, 128), width)
        return other.at[k, :, at]

    here = [
        pltpu.make_async_copy(x, xs.at[mine], local.at[0]),
        pltpu.make_async_copy(dy, dys.at[mine], local.at[1]),
        pltpu.make_async_copy(table, tables.at[mine], local.at[2]),
    ]
    for k in range(3):
        here.append(pltpu.make_async_copy(sources[k], columns(k, 0), local.at[3 + k]))
    for copy in here:
        copy.start()
    meet(
        [c.device(0, 1), c.device(0, -1), c.device(1, 0), c.device(-1, 0)]
        + [c.device(0, 0, True), c.row_device(1), c.row_device(-1)]
    )
    parts = [
        SlabGather(c, table, tables, True, False),
        SlabGather(c, x, xs, True, True),
        SlabGather(c, dy, dys, False, True),
    ]
    for part in parts:
        part.start()
    basis_waits, basis_done, basis_far = [], [], []

    def basis_cross(k, dy_):
        if k < 2:
            ref = columns(k, dy_)
            src = sources[k] if dy_ == 0 else ref
            land = other_columns(k, dy_)
            basis_done.append(c.push(src, land, c.device(0, 0, True), land))

    for k in range(3):
        ref = columns(k, 0)
        basis_waits.append(
            (
                c.push(sources[k], ref, c.row_device(1), columns(k, -1)),
                c.push(sources[k], ref, c.row_device(-1), columns(k, 1)),
            )
        )
    for part in parts:
        part.start_own()
    for k in range(3):
        basis_cross(k, 0)
    for part in parts:
        part.first()
    for part in parts:
        part.second()
    for part in parts:
        part.third()
    ranks = gate.shape[0]
    stored = []

    def basis_load(k, dy_):
        at = pl.ds(pl.multiple_of(((c.row + dy_ + 4) % 4) * width, 128), width)
        src = sources[k] if dy_ == 0 else columns(k, dy_)
        copy = pltpu.make_async_copy(src, basis_held.at[k, :, at], basis_sems.at[k, dy_ % 4])
        copy.start()
        return copy

    def turn(k, dy_, load):
        load.wait()
        start = ((c.row + dy_ + 4) % 4) * width
        lanes = pl.ds(k * ranks, ranks)

        def step(i, carry):
            at = pl.ds(pl.multiple_of(start + i * 256, 256), 256)
            basis_turned[at, lanes] = basis_held[k, :, at].T
            return carry

        lax.fori_loop(0, width // 256, step, 0)
        at = pl.ds(pl.multiple_of(start, 256), width)
        copy = pltpu.make_async_copy(
            basis_turned.at[at, lanes], turned.at[at, lanes], turned_sems.at[k, dy_ % 4]
        )
        copy.start()
        stored.append(copy)

    own_loads = [basis_load(k, 0) for k in range(3)]
    for k in range(3):
        turn(k, 0, own_loads[k])
    half = ranks // 2
    waiting = []
    for step in range(4):
        for part in parts:
            part.ring(step)
        for args in waiting:
            turn(*args)
        waiting = []
        if step < 3:
            ahead, behind = basis_waits[step]
            low, high = pl.ds(0, half), pl.ds(half, half)
            ahead()
            ref = columns(step, -1, low)
            far = [c.push(ref, ref, c.row_device(1), columns(step, 2, low))]
            basis_cross(step, -1)
            behind()
            ref = columns(step, 1, high)
            far.append(c.push(ref, ref, c.row_device(-1), columns(step, 2, high)))
            basis_cross(step, 1)
            basis_far.append(far)
            waiting = [(step, d, basis_load(step, d)) for d in (-1, 1)]
    far_loads = []
    for k in range(3):
        for wait in basis_far[k]:
            wait()
        basis_cross(k, 2)
        far_loads.append(basis_load(k, 2))
    for k in (0, 2, 1, 3):
        for part in parts:
            part.end(k)
        if k < 3:
            turn(k, 2, far_loads[k])
    for part in parts:
        part.finish()
    for wait in basis_done:
        wait()
    for copy in here + stored:
        copy.wait()
    c.finish()


GATHER_COPIES = 32 + 32 + 31 + 20


def gather_inputs(x, dy, gate, up, down, table, n_ex):
    rows, width = gate.shape
    slabs = jax.ShapeDtypeStruct((n_ex,) + x.shape, BF)
    anywhere = pl.BlockSpec(memory_space=pl.ANY)
    return pl.pallas_call(
        gather_kernel,
        out_shape=[
            slabs,
            slabs,
            jax.ShapeDtypeStruct((n_ex,) + table.shape, FL),
            jax.ShapeDtypeStruct((2, rows, 4 * width), BF),
            jax.ShapeDtypeStruct((rows, 4 * width), BF),
            jax.ShapeDtypeStruct((2, rows, 4 * width), BF),
            jax.ShapeDtypeStruct((4 * width, 3 * rows), BF),
        ],
        in_specs=[anywhere] * 6,
        out_specs=[anywhere] * 7,
        scratch_shapes=[
            pltpu.VMEM((3, rows, 4 * width), BF),
            pltpu.VMEM((4 * width, 3 * rows), BF),
            pltpu.SemaphoreType.DMA((GATHER_COPIES,)),
            pltpu.SemaphoreType.DMA((GATHER_COPIES,)),
            pltpu.SemaphoreType.DMA((6,)),
            pltpu.SemaphoreType.DMA((3, 4)),
            pltpu.SemaphoreType.DMA((3, 4)),
        ],
        name="gather_inputs",
        compiler_params=pltpu.CompilerParams(
            collective_id=0, has_side_effects=True, vmem_limit_bytes=60 * MIB
        ),
    )(x, dy, gate, up, down, table)


def project_kernel(x, dy, turned, out):
    ranks = out.shape[1]
    ups = dot(x[...], turned[:, : 2 * ranks], 1, 0)
    downs = dot(dy[...], turned[:, 2 * ranks :], 1, 0)
    out[0] = ups[:, :ranks].T.astype(BF)
    out[1] = ups[:, ranks:].T.astype(BF)
    out[2] = downs.T.astype(BF)


def project(x, dy, turned):
    tokens, width = x.shape
    ranks = turned.shape[1] // 3
    step = 256
    some = pl.BlockSpec((step, width), lambda g: (g, 0))
    return pl.pallas_call(
        project_kernel,
        grid=(tokens // step,),
        out_shape=jax.ShapeDtypeStruct((3, ranks, tokens), BF),
        in_specs=[some, some, pl.BlockSpec(turned.shape, lambda g: (0, 0))],
        out_specs=pl.BlockSpec((3, ranks, step), lambda g: (0, 0, g)),
        name="project",
        compiler_params=pltpu.CompilerParams(vmem_limit_bytes=60 * MIB),
    )(x, dy, turned)


def home_kernel(
    rows, x, dy, bases, other,
    out, d_gate, d_up, d_down,
    paired, xb, db, bb, terms, far_in, near_in, turned, full, got, skipped, passed, kept, last,
    send, recv, loads,
):
    c = Copies(send, recv)
    width = d_gate.shape[1]
    near = (1, -1, 2)
    meet(
        [c.device(0, d) for d in near]
        + [c.device(d, 0) for d in near]
        + [c.device(0, 0, True), c.row_device(1), c.row_device(-1)]
    )
    partner = c.push(rows.at[pl.ds(0, 2)], paired, c.device(0, 0, True), paired)
    order = (2, 1, -1, 0)

    def load_rows(n):
        at = pl.ds(pl.multiple_of(((c.row + order[n] + 4) % 4) * width, 128), width)
        slot = n % 2
        copies = [
            pltpu.make_async_copy(x.at[:, at], xb.at[slot], loads.at[2 * slot]),
            pltpu.make_async_copy(dy.at[:, at], db.at[slot], loads.at[2 * slot + 1]),
        ]
        for copy in copies:
            copy.start()
        return copies

    def load_bases(n):
        at = pl.ds(n * width, width)
        slot = n % 2
        copies = [
            pltpu.make_async_copy(
                bases.at[:, :, at], bb.at[slot, 0], loads.at[4 + 2 * slot]
            ),
            pltpu.make_async_copy(other.at[:, :, at], bb.at[slot, 1], loads.at[5 + 2 * slot]),
        ]
        for copy in copies:
            copy.start()
        return copies

    flying = [load_rows(0), load_rows(1)]
    basis_flying = [load_bases(0), load_bases(1)]
    low, high = pl.ds(0, 64), pl.ds(64, 64)
    near_waits = [[], []]
    far_waits = [[], []]
    for n in range(4):
        for copy in flying[n]:
            copy.wait()
        slot = n % 2

        def columns(k, carry):
            at = pl.ds(pl.multiple_of(k * 256, 256), 256)
            ups = dot(rows[0:2].reshape(256, -1), xb[slot, :, at], 1, 0)
            downs = dot(rows[2], db[slot, :, at], 1, 0)
            if n < 3:
                terms[n, 0, :, at] = ups[:128].astype(BF)
                terms[n, 1, :, at] = ups[128:].astype(BF)
                terms[n, 2, :, at] = downs.astype(BF)
            else:
                d_gate[:, at] = ups[:128]
                d_up[:, at] = ups[128:]
                d_down[:, at] = downs
            return carry

        lax.fori_loop(0, width // 256, columns, 0)
        if n < 2:
            flying.append(load_rows(n + 2))
        for k in range(3):
            if n == 0:
                land = far_in.at[0, k]
                far_waits[0].append(c.push(terms.at[0, k, low], land, c.row_device(1), land))
                land = far_in.at[1, k]
                far_waits[1].append(c.push(terms.at[0, k, high], land, c.row_device(-1), land))
            if n == 1:
                land = near_in.at[0, k, high]
                near_waits[0].append(c.push(terms.at[1, k, high], land, c.row_device(1), land))
            if n == 2:
                land = near_in.at[1, k, low]
                near_waits[1].append(c.push(terms.at[2, k, low], land, c.row_device(-1), land))
    partner()
    half_tokens = turned.shape[0]
    mine = pl.ds(pl.multiple_of(c.core * half_tokens, 128), half_tokens)
    for k in range(2):
        for n, source in enumerate((rows, paired)):
            at = pl.ds((2 * n + k) * 128, 128)
            turned[:, at] = source[k, :, mine].astype(FL).T.astype(BF)
    tok = full.shape[2]
    place = (c.z, c.x)
    got_waits = [{}, {}]
    cross_waits = []
    via_ahead, via_behind = (1, -1), (2, 0)

    def group(h, d, b):
        if h == 0:
            return ((c.z + b + 4) % 4) * 4 + (c.x + d + 4) % 4
        return ((c.z + d + 4) % 4) * 4 + (c.x + b + 4) % 4

    def along(h, d):
        return c.device(0, d) if h == 0 else c.device(d, 0)

    def cross_far(h):
        waits = []
        for d, which in ((1, via_ahead), (-1, via_behind)):
            for k, b in enumerate(which):
                land = skipped.at[h, d % 3 - 1, k]
                waits.append((d, b, k, c.push(full.at[h, group(h, 2, b)], land, along(h, d), land)))
        for d, which in ((1, via_behind), (-1, via_ahead)):
            for b in which:
                cross_push(h, d, b)
        return waits

    def cross_push(h, d, b):
        land = got.at[h, d % 3 - 1, b % 4]
        wait = c.push(full.at[h, group(h, d, b)], land, along(h, d), land)
        got_waits[h].setdefault(b, []).append(wait)

    def cross_near(h):
        for d, b, k, wait in cross_waits[h]:
            wait()
            slab = group(h, d, b)
            more = full[h, slab].astype(FL) + skipped[h, d % 3 - 1, k].astype(FL)
            full[h, slab] = more.astype(BF)
            cross_push(h, d, b)

    for n in range(4):
        for copy in basis_flying[n]:
            copy.wait()
        slot, h = n % 2, n // 2

        def token_columns(k, carry):
            at = pl.ds(pl.multiple_of(k * 256, 256), 256)
            to = pl.ds(pl.multiple_of((n % 2) * width + k * 256, 256), 256)
            both = jnp.concatenate(
                [bb[slot, s, k2, :, at] for s in range(2) for k2 in range(2)], axis=0
            )
            sums = dot(turned[...], both, 1, 0)
            for s in range(16):
                full[h, s, :, to] = sums[s * tok : (s + 1) * tok].astype(BF)
            return carry

        lax.fori_loop(0, width // 256, token_columns, 0)
        if n < 2:
            basis_flying.append(load_bases(n + 2))
        if n % 2 == 1:
            cross_waits.append(cross_far(h))
    for h in range(2):
        cross_near(h)
    for k in range(3):
        far_waits[0][k]()
        terms[1, k, low] = (terms[1, k, low].astype(FL) + far_in[0, k].astype(FL)).astype(BF)
        land = near_in.at[0, k, low]
        near_waits[0].append(c.push(terms.at[1, k, low], land, c.row_device(1), land))
        far_waits[1][k]()
        terms[2, k, high] = (terms[2, k, high].astype(FL) + far_in[1, k].astype(FL)).astype(BF)
        land = near_in.at[1, k, high]
        near_waits[1].append(c.push(terms.at[2, k, high], land, c.row_device(-1), land))
    last_waits = [[], []]
    for step, b in enumerate((1, -1, 2, 0)):
        for h in range(2):
            for wait in got_waits[h][b]:
                wait()
            slab = group(h, 0, b)
            target = c.device(b, 0) if h == 0 else c.device(0, b)
            total = full[h, slab].astype(FL)
            for side in range(2):
                total = total + got[h, side, b % 4].astype(FL)
            if b == 0:
                kept[h] = total
            else:
                passed[h, step] = total.astype(BF)
                land = last.at[h, step]
                last_waits[h].append(c.push(passed.at[h, step], land, target, land))
    for h in range(2):
        for wait in last_waits[h]:
            wait()
        total = kept[h]
        for step in range(3):
            total = total + last[h, step].astype(FL)
        out[:, h * 2 * width : (h + 1) * 2 * width] = total.astype(BF)
    for side in range(2):
        for wait in near_waits[side]:
            wait()
    for k, ref in enumerate((d_gate, d_up, d_down)):
        ref[...] = ref[...] + near_in[0, k].astype(FL) + near_in[1, k].astype(FL)
    c.finish()


HOME_COPIES = 1 + 18 + 24 + 6


def send_home(rows, x, dy, bases, other, tok):
    kinds, ranks, tokens = rows.shape
    full_width = x.shape[1]
    width = full_width // 4
    half = full_width // 2
    anywhere = pl.BlockSpec(memory_space=pl.ANY)
    vmem = pl.BlockSpec(memory_space=pltpu.VMEM)
    basis = jax.ShapeDtypeStruct((ranks, width), FL)
    return pl.pallas_call(
        home_kernel,
        out_shape=[jax.ShapeDtypeStruct((tok, full_width), BF), basis, basis, basis],
        in_specs=[vmem] + [anywhere] * 4,
        out_specs=[vmem] * 4,
        scratch_shapes=[
            pltpu.VMEM((2, ranks, tokens), BF),
            pltpu.VMEM((2, tokens, width), BF),
            pltpu.VMEM((2, tokens, width), BF),
            pltpu.VMEM((2, 2, 2, ranks, width), BF),
            pltpu.VMEM((3, kinds, ranks, width), BF),
            pltpu.VMEM((2, kinds, ranks // 2, width), BF),
            pltpu.VMEM((2, kinds, ranks, width), BF),
            pltpu.VMEM((tokens // 2, 4 * ranks), BF),
            pltpu.VMEM((2, 16, tok, half), BF),
            pltpu.VMEM((2, 2, 4, tok, half), BF),
            pltpu.VMEM((2, 2, 2, tok, half), BF),
            pltpu.VMEM((2, 3, tok, half), BF),
            pltpu.VMEM((2, tok, half), FL),
            pltpu.VMEM((2, 3, tok, half), BF),
            pltpu.SemaphoreType.DMA((HOME_COPIES,)),
            pltpu.SemaphoreType.DMA((HOME_COPIES,)),
            pltpu.SemaphoreType.DMA((8,)),
        ],
        name="send_home",
        compiler_params=pltpu.CompilerParams(
            collective_id=1, has_side_effects=True, vmem_limit_bytes=60 * MIB
        ),
    )(rows, x, dy, bases, other)


def slot_tables(route_ids, route_weight, cells):
    flat = route_ids.reshape(-1)
    pairs = flat.shape[0]
    at = jnp.arange(pairs, dtype=jnp.int32)
    earlier = (flat[:, None] == flat[None, :]) & (at[None, :] < at[:, None])
    slot = jnp.sum(earlier.astype(jnp.int32), axis=1)
    placed = (flat * 2 + slot)[:, None] == jnp.arange(cells, dtype=jnp.int32)[None, :]
    token = at // route_ids.shape[1] + 1
    cell_token = jnp.sum(jnp.where(placed, token[:, None], 0), axis=0)
    cell_weight = jnp.sum(
        jnp.where(placed, route_weight.reshape(-1)[:, None].astype(FL), 0.0), axis=0
    )
    return slot, cell_token, cell_weight


def body(
    tokens,
    grad_out,
    route_ids,
    route_weight,
    cluster_of,
    gate_basis,
    up_basis,
    down_basis,
    gate_factor,
    up_factor,
    down_factor,
):
    n_dp = lax.axis_size("dp")
    n_ex = lax.axis_size("expert")
    tok_rows, width = tokens.shape
    local = gate_factor.shape[0]
    lane_rows = local * 2
    cells = n_ex * lane_rows
    clusters, rank, part_width = gate_basis.shape
    plane_tokens = n_ex * tok_rows
    all_rank = n_ex * rank

    slot, cell_token, cell_weight = slot_tables(route_ids, route_weight, cells)
    table = jnp.concatenate([cell_token.astype(FL), cell_weight]).reshape(4, 128)
    flat = (clusters * rank, part_width)
    x_all, dy_all, tables, gate_up, _, other, turned = gather_inputs(
        tokens,
        grad_out,
        gate_basis.reshape(flat),
        up_basis.reshape(flat),
        down_basis.reshape(flat),
        table,
        n_ex,
    )
    x_all = x_all.reshape(plane_tokens, width)
    dy_all = dy_all.reshape(plane_tokens, width)
    tables = tables.reshape(n_ex, 2, n_ex, local, 2)
    tables = tables.transpose(1, 2, 3, 0, 4).reshape(2, n_ex, n_ex * lane_rows)
    block = (jnp.arange(n_ex * lane_rows, dtype=jnp.int32) // 2) % n_ex
    named = tables[0].astype(jnp.int32)
    slots = jnp.where(named > 0, named - 1 + tok_rows * block[None, :], -1)
    weights = tables[1]
    cluster = cluster_of.reshape(n_ex, local)[:, 0]

    rows = project(x_all, dy_all, turned)
    member = cluster[:, None] == jnp.arange(clusters, dtype=jnp.int32)[None, :]
    home, dots, kept_rows, kept_units = middle(
        member.astype(FL), rows, slots, weights, gate_factor, up_factor, down_factor, n_dp
    )
    summed = combine(cluster, home, slots, weights, clusters, plane_tokens)

    z, x, core = plane_place()
    flat = route_ids.reshape(-1)
    lane = jnp.arange(128, dtype=jnp.int32)
    wanted = jnp.arange(4, dtype=jnp.int32)
    wanted = (wanted // 2) * 64 + slab_of(z, x, core) * 2 + wanted % 2
    own = wanted[:, None, None] == lane[None, None, :]
    dots = jnp.sum(jnp.where(own, dots.reshape(1, n_ex * 2, 128), 0.0), axis=2)
    hit = (flat % 2 * 2 + slot)[:, None, None] == jnp.arange(4, dtype=jnp.int32)[None, :, None]
    hit = hit & ((flat // 2)[:, None, None] == jnp.arange(n_ex * 2, dtype=jnp.int32))
    scores = jnp.sum(jnp.where(hit, dots[None], 0.0), axis=(1, 2))
    grad_route = scores.reshape(route_ids.shape) / route_weight.astype(FL)
    passing = send_home(summed, x_all, dy_all, gate_up, other, tok_rows)
    d_gate_factor, d_up_factor, d_down_factor, grad_tokens, *terms = factor_grads(
        kept_rows, kept_units, passing
    )
    shape = gate_basis.shape
    return (
        grad_tokens,
        grad_route,
        terms[0].reshape(shape),
        terms[1].reshape(shape),
        terms[2].reshape(shape),
        d_gate_factor,
        d_up_factor,
        d_down_factor,
    )


def solution(mesh):
    rows = P(("dp", "expert"), None)
    basis = P(None, "expert", "dp")
    factor = P("expert", None, "dp")
    low = P("expert", "dp", None)
    in_specs = (rows, rows, rows, rows, P(), basis, basis, basis, factor, factor, low)
    out_specs = (rows, rows, basis, basis, basis, factor, factor, low)
    return jax.shard_map(body, mesh=mesh, in_specs=in_specs, out_specs=out_specs, check_vma=False)
```

```python
import jax
import jax.numpy as jnp
from jax import lax
from jax.experimental import pallas as pl
from jax.experimental.pallas import tpu as pltpu
from jax.sharding import PartitionSpec as P

FL = jnp.float32
BF = jnp.bfloat16
MIB = 1024 * 1024


def dot(a, b, ca, cb):
    return lax.dot_general(a, b, (((ca,), (cb,)), ((), ())), preferred_element_type=FL)


def one_hot(slot_ref, j, tokens):
    row = slot_ref[pl.ds(j, 1), :]
    lanes = row.shape[1]
    grid = lax.broadcasted_iota(jnp.int32, (tokens, lanes), 0)
    return jnp.where(grid == row, 1.0, 0.0).astype(BF)


def combine_kernel(cluster, parts, slots, weights, out, total):
    groups, rank, tokens = parts.shape[0], parts.shape[3], out.shape[2]
    total[...] = jnp.zeros_like(total)

    def step(j, carry):
        c = cluster[j]
        got = parts[j].astype(FL)
        got = jnp.concatenate([got[0], got[1]], axis=2)
        got = jnp.concatenate([got[:2], got[2:] * weights[pl.ds(j, 1), :]], axis=0)
        got = got.astype(BF).reshape(3 * rank, -1)
        add = dot(got, one_hot(slots, j, tokens), 1, 1).reshape(3, rank, tokens)
        total[:, pl.ds(pl.multiple_of(c * rank, rank), rank), :] += add
        return carry

    lax.fori_loop(0, groups, step, 0, unroll=4)
    out[...] = total[...].astype(BF)


def combine(cluster, parts, slots, weights, clusters, tokens):
    rank = parts.shape[3]
    vmem = pl.BlockSpec(memory_space=pltpu.VMEM)
    shape = (3, clusters * rank, tokens)
    return pl.pallas_call(
        combine_kernel,
        out_shape=jax.ShapeDtypeStruct(shape, BF),
        in_specs=[pl.BlockSpec(memory_space=pltpu.SMEM), vmem, vmem, vmem],
        out_specs=vmem,
        scratch_shapes=[pltpu.VMEM(shape, FL)],
        name="combine",
        compiler_params=pltpu.CompilerParams(vmem_limit_bytes=60 * MIB),
    )(cluster, parts, slots, weights)


def mix(tiles):
    first, second = [], []
    for k in range(0, len(tiles), 2):
        a, b = tiles[k], tiles[k + 1]
        h = a.shape[-1] // 2
        first.append(jnp.concatenate([a[:, :h], b[:, :h]], axis=1))
        second.append(jnp.concatenate([a[:, h:], b[:, h:]], axis=1))
    return jnp.concatenate(first, axis=1), jnp.concatenate(second, axis=1)


def split_tiles(a):
    return [a[:, k : k + 128] for k in range(0, a.shape[1], 128)]


def factor_kernel(rows, units, *refs):
    sources, (d_gate, d_up, d_down), results = refs[:4], refs[4:7], refs[7:]
    d_gate[0] = dot(rows[0, 0], units[0, 0], 1, 1)
    d_up[0] = dot(rows[0, 1], units[0, 1], 1, 1)
    d_down[0] = dot(units[0, 2], rows[0, 2], 1, 1)
    for source, result in zip(sources, results):
        result[...] = source[...]


def factor_grads(rows, units, passing):
    count, _, all_rank, lanes = rows.shape
    held = pl.BlockSpec((1,) + rows.shape[1:], lambda g: (g, 0, 0, 0))
    one = pl.BlockSpec((1, all_rank, units.shape[2]), lambda g: (g, 0, 0))
    tok, width = passing[0].shape
    ranks, part = passing[1].shape
    passed = [pl.BlockSpec((tok, width // count), lambda g: (0, g))]
    passed += [pl.BlockSpec((ranks // count, part), lambda g: (g, 0))] * 3
    factor = jax.ShapeDtypeStruct((count, all_rank, units.shape[2]), FL)
    return pl.pallas_call(
        factor_kernel,
        grid=(count,),
        out_shape=[factor] * 3 + [jax.ShapeDtypeStruct(a.shape, a.dtype) for a in passing],
        in_specs=[held, held] + passed,
        out_specs=[one] * 3 + passed,
        name="factor_grads",
        compiler_params=pltpu.CompilerParams(vmem_limit_bytes=60 * MIB),
    )(rows, units, *passing)


def plane_place():
    e = lax.axis_index("expert")
    return e // 8, (e // 2) % 4, e % 2


def slab_of(z, x, core):
    return core * 16 + z * 4 + x


class Copies:
    def __init__(self, send, recv):
        self.send, self.recv, self.count, self.sent = send, recv, 0, []
        self.row = lax.axis_index("dp")
        self.z, self.x, self.core = plane_place()

    def make(self, src, dst, m, target):
        return pltpu.make_async_remote_copy(
            src_ref=src,
            dst_ref=dst,
            send_sem=self.send.at[m],
            recv_sem=self.recv.at[m],
            device_id=target,
            device_id_type=pl.DeviceIdType.MESH,
        )

    def push(self, src, dst, target, land):
        m = self.count
        self.count += 1
        copy = self.make(src, dst, m, target)
        copy.start()
        self.sent.append(copy)
        return self.make(land, land, m, target).wait_recv

    def device(self, dz, dx, flip=False):
        z, x = (self.z + dz + 4) % 4, (self.x + dx + 4) % 4
        core = 1 - self.core if flip else self.core
        return (self.row, (z * 4 + x) * 2 + core)

    def slab(self, dz, dx, flip=False):
        z, x = (self.z + dz + 4) % 4, (self.x + dx + 4) % 4
        core = 1 - self.core if flip else self.core
        return slab_of(z, x, core)

    def row_device(self, dy):
        e = (self.z * 4 + self.x) * 2 + self.core
        return ((self.row + dy + 4) % 4, e)

    def finish(self):
        for copy in self.sent:
            copy.wait_send()


def greet(targets):
    barrier = pltpu.get_barrier_semaphore()
    for target in targets:
        pl.semaphore_signal(
            barrier, inc=1, device_id=target, device_id_type=pl.DeviceIdType.MESH
        )


def wait_for(targets):
    pl.semaphore_wait(pltpu.get_barrier_semaphore(), len(targets))


def meet(targets):
    greet(targets)
    wait_for(targets)


def middle_kernel(
    member, rows, slots, weights, gate, up, down,
    home, dots, kept_rows, kept_units,
    picked, chosen, landed, parts, factors, row_store, unit_store, far_in, near_in, summed,
    route, route_in, route_sum,
    out_send, out_recv, back_send, back_recv, dot_send, dot_recv, ring_send, ring_recv,
    loads, local,
):
    c = Copies(ring_send, ring_recv)
    row, e = lax.axis_index("dp"), lax.axis_index("expert")
    groups, rank, tokens = picked.shape[0], picked.shape[3], rows.shape[2]
    lanes = picked.shape[4]
    all_rank = landed.shape[3]

    def everyone(act):
        def step(s, carry):
            act((s * 11) % groups)
            return carry

        lax.fori_loop(1, groups, step, 0)

    def device(d):
        return (row, (e + d) % groups)

    def source(d):
        return (e - d + groups) % groups

    def remote(src, dst, send, recv, target):
        return pltpu.make_async_remote_copy(
            src_ref=src,
            dst_ref=dst,
            send_sem=send,
            recv_sem=recv,
            device_id=target,
            device_id_type=pl.DeviceIdType.MESH,
        )

    def ranks(at):
        return pl.ds(pl.multiple_of(at * rank, rank), rank)

    def out_copy(p, d):
        target = device(d)
        dst = landed.at[p, row, :, ranks(e)]
        return remote(picked.at[target[1], p], dst, out_send.at[p, d], out_recv.at[p, d], target)

    def out_wait(p, d):
        land = landed.at[p, row, :, ranks(source(d))]
        remote(land, land, out_send.at[p, d], out_recv.at[p, d], device(d)).wait_recv()

    def back_copy(p, d):
        target = device(d)
        src = summed.at[p, :, ranks(target[1])]
        return remote(src, home.at[e, p], back_send.at[p, d], back_recv.at[p, d], target)

    def back_wait(p, d):
        land = home.at[source(d), p]
        remote(land, land, back_send.at[p, d], back_recv.at[p, d], device(d)).wait_recv()

    def dot_copy(d):
        return remote(route_sum, dots.at[e], dot_send.at[d], dot_recv.at[d], device(d))

    def dot_wait(d):
        land = dots.at[source(d)]
        remote(land, land, dot_send.at[d], dot_recv.at[d], device(d)).wait_recv()

    def at_row(dy):
        return (row + dy + 4) % 4

    incoming = [
        pltpu.make_async_copy(ref, factors.at[k], loads.at[k])
        for k, ref in enumerate((gate, up, down))
    ]
    for copy in incoming:
        copy.start()
    barrier = pltpu.get_barrier_semaphore()

    def greet(target):
        pl.semaphore_signal(
            barrier, inc=1, device_id=target, device_id_type=pl.DeviceIdType.MESH
        )

    everyone(lambda d: greet(device(d)))
    for dy in (1, -1, 2):
        greet(c.row_device(dy))

    def own_for(j):
        own = jnp.zeros((3, rank, tokens), BF)
        for k in range(member.shape[1]):
            share = member[pl.ds(j, 1), k : k + 1].astype(BF)[None]
            own = own + rows[:, k * rank : (k + 1) * rank, :] * share
        chosen[j] = own.reshape(3 * rank, tokens)

    def pick_for(j, p):
        at = slice(p * lanes, (p + 1) * lanes)
        grid = lax.broadcasted_iota(jnp.int32, (tokens, lanes), 0)
        hot = jnp.where(grid == slots[pl.ds(j, 1), :][:, at], 1.0, 0.0).astype(BF)
        got = dot(chosen[j], hot, 1, 0).reshape(3, rank, lanes)
        picked[j, p, 0:2] = got[:2].astype(BF)
        picked[j, p, 2] = (got[2] * weights[pl.ds(j, 1), :][:, at]).astype(BF)

    own_for(e)
    for p in range(2):
        pick_for(e, p)
    own_copies = [
        pltpu.make_async_copy(picked.at[e, p], landed.at[p, row, :, ranks(e)], local.at[p])
        for p in range(2)
    ]
    for copy in own_copies:
        copy.start()
    def pick_some(p, at, first=False):
        for s in at:
            j = (e + (s * 11) % groups) % groups
            if p == 0:
                own_for(j)
            pick_for(j, p)
        if first:
            pl.semaphore_wait(barrier, groups + 2)
        for s in at:
            out_copy(p, (s * 11) % groups).start()

    for p in range(2):
        pick_some(p, (1, 2, 3), p == 0)

        def pick_step(n, carry):
            pick_some(p, [4 * n + u for u in range(4)])
            return carry

        lax.fori_loop(1, groups // 4, pick_step, 0)
    for copy in incoming:
        copy.wait()
    for copy in own_copies:
        copy.wait()
    low, high = pl.ds(0, all_rank // 2), pl.ds(all_rank // 2, all_rank // 2)
    gathers, fars = [], []
    for p in range(2):
        everyone(lambda d: out_wait(p, d))
        own = landed.at[p, row]
        gathers.append(
            (
                c.push(own, own, c.row_device(1), landed.at[p, at_row(-1)]),
                c.push(own, own, c.row_device(-1), landed.at[p, at_row(1)]),
            )
        )
    for p in range(2):
        gathers[p][0]()
        ref = landed.at[p, at_row(-1), :, low]
        far = [c.push(ref, ref, c.row_device(1), landed.at[p, at_row(2), :, low])]
        gathers[p][1]()
        ref = landed.at[p, at_row(1), :, high]
        far.append(c.push(ref, ref, c.row_device(-1), landed.at[p, at_row(2), :, high]))
        fars.append(far)
    stores, far_waits, near_waits = [], [], []
    for p in range(2):
        for wait in fars[p]:
            wait()
        wide = [mix([landed[p, i, k] for i in range(4)]) for k in range(3)]
        results = []
        for n in range(2):
            hg, hu, gm = wide[0][n], wide[1][n], wide[2][n]
            ex = 2 * p + n
            row_store[ex, 0] = hg
            row_store[ex, 1] = hu
            row_store[ex, 2] = gm
            gf, uf, df = factors[0, ex], factors[1, ex], factors[2, ex]
            gate_pre = dot(gf, hg, 0, 0)
            up_pre = dot(uf, hu, 0, 0)
            sig = 1.0 / (1.0 + jnp.exp(-gate_pre))
            act = gate_pre * sig
            slope = sig * (1.0 + gate_pre * (1.0 - sig))
            hidden = (act * up_pre).astype(BF)
            mixed = dot(df, hidden, 0, 0)
            grad_hidden = dot(df, gm, 1, 0)
            grad_gate_pre = (grad_hidden * up_pre * slope).astype(BF)
            grad_up_pre = (grad_hidden * act).astype(BF)
            unit_store[ex, 0] = grad_gate_pre
            unit_store[ex, 1] = grad_up_pre
            unit_store[ex, 2] = hidden
            scores = jnp.sum(mixed * gm.astype(FL), axis=0, keepdims=True)
            each = lanes // 2
            for i in range(4):
                route[i, p : p + 1, n * each : (n + 1) * each] = scores[:, i * each : (i + 1) * each]
            grad_hg = dot(gf, grad_gate_pre, 1, 0)
            grad_hu = dot(uf, grad_up_pre, 1, 0)
            results.append((grad_hg.astype(BF), grad_hu.astype(BF), mixed.astype(BF)))
        for k in range(3):
            tiles = []
            for a, b in zip(split_tiles(results[0][k]), split_tiles(results[1][k])):
                h = a.shape[-1] // 2
                tiles.append(jnp.concatenate([a[:, :h], b[:, :h]], axis=1))
                tiles.append(jnp.concatenate([a[:, h:], b[:, h:]], axis=1))
            for i in range(4):
                parts[p, i, k] = tiles[i]
        ahead, behind = c.row_device(1), c.row_device(-1)
        far = parts.at[p, at_row(2)]
        far_waits.append(
            (
                c.push(far.at[:, low], far_in.at[p, 0], ahead, far_in.at[p, 0]),
                c.push(far.at[:, high], far_in.at[p, 1], behind, far_in.at[p, 1]),
            )
        )
        land = (near_in.at[p, 0, :, high], near_in.at[p, 1, :, low])
        near_waits.append(
            [
                c.push(parts.at[p, at_row(1), :, high], land[0], ahead, land[0]),
                c.push(parts.at[p, at_row(-1), :, low], land[1], behind, land[1]),
            ]
        )
        pair = pl.ds(2 * p, 2)
        here = [
            pltpu.make_async_copy(row_store.at[pair], kept_rows.at[pair], local.at[2 + p]),
            pltpu.make_async_copy(unit_store.at[pair], kept_units.at[pair], local.at[4 + p]),
        ]
        for copy in here:
            copy.start()
        stores += here
    route_waits = []
    for n, dy in enumerate((1, -1, 2)):
        land = route_in.at[n]
        route_waits.append(c.push(route.at[at_row(dy)], land, c.row_device(dy), land))
    for p in range(2):
        for side, dy, half in ((0, 1, low), (1, -1, high)):
            far_waits[p][side]()
            to = at_row(dy)
            more = parts[p, to, :, half].astype(FL) + far_in[p, side].astype(FL)
            parts[p, to, :, half] = more.astype(BF)
            land = near_in.at[p, side, :, half]
            near_waits[p].append(
                c.push(parts.at[p, to, :, half], land, c.row_device(dy), land)
            )
    for wait in route_waits:
        wait()
    route_sum[...] = route[row] + route_in[0] + route_in[1] + route_in[2]
    everyone(lambda d: dot_copy(d).start())
    for p in range(2):
        for wait in near_waits[p]:
            wait()
        total = parts[p, row].astype(FL) + near_in[p, 0].astype(FL) + near_in[p, 1].astype(FL)
        summed[p] = total.astype(BF)
        everyone(lambda d: back_copy(p, d).start())
        own = pltpu.make_async_copy(summed.at[p, :, ranks(e)], home.at[e, p], local.at[6 + p])
        own.start()
        stores.append(own)
    own = pltpu.make_async_copy(route_sum, dots.at[e], local.at[8])
    own.start()
    stores.append(own)
    everyone(dot_wait)
    for p in range(2):
        everyone(lambda d: back_wait(p, d))
    for copy in stores:
        copy.wait()
    for p in range(2):
        everyone(lambda d: out_copy(p, d).wait_send())
        everyone(lambda d: back_copy(p, d).wait_send())
    everyone(lambda d: dot_copy(d).wait_send())
    c.finish()


RING_COPIES = 2 * 4 + 2 * 6 + 3


def middle(member, rows, slots, weights, gate, up, down, n_dp):
    groups, lanes = slots.shape
    kinds, ranks, _ = rows.shape
    count, all_rank, units = gate.shape
    rank = all_rank // groups
    half = lanes // 2
    anywhere = pl.BlockSpec(memory_space=pl.ANY)
    vmem = pl.BlockSpec(memory_space=pltpu.VMEM)
    kept = jax.ShapeDtypeStruct((count, 3, all_rank, n_dp * half // 2), BF)
    dma = pltpu.SemaphoreType.DMA
    return pl.pallas_call(
        middle_kernel,
        out_shape=[
            jax.ShapeDtypeStruct((groups, 2, 3, rank, half), BF),
            jax.ShapeDtypeStruct((groups, 2, half), FL),
            kept,
            kept,
        ],
        in_specs=[vmem] * 4 + [anywhere] * 3,
        out_specs=[anywhere] * 4,
        scratch_shapes=[
            pltpu.VMEM((groups, 2, 3, rank, half), BF),
            pltpu.VMEM((groups, 3 * rank, rows.shape[2]), BF),
            pltpu.VMEM((2, n_dp, 3, all_rank, half), BF),
            pltpu.VMEM((2, n_dp, 3, all_rank, half), BF),
            pltpu.VMEM((3,) + gate.shape, BF),
            pltpu.VMEM(kept.shape, BF),
            pltpu.VMEM(kept.shape, BF),
            pltpu.VMEM((2, 2, 3, all_rank // 2, half), BF),
            pltpu.VMEM((2, 2, 3, all_rank, half), BF),
            pltpu.VMEM((2, 3, all_rank, half), BF),
            pltpu.VMEM((n_dp, 2, half), FL),
            pltpu.VMEM((3, 2, half), FL),
            pltpu.VMEM((2, half), FL),
            dma((2, groups)),
            dma((2, groups)),
            dma((2, groups)),
            dma((2, groups)),
            dma((groups,)),
            dma((groups,)),
            dma((RING_COPIES,)),
            dma((RING_COPIES,)),
            dma((3,)),
            dma((9,)),
        ],
        name="middle",
        compiler_params=pltpu.CompilerParams(
            collective_id=2, has_side_effects=True, vmem_limit_bytes=56 * MIB
        ),
    )(member, rows, slots, weights, gate, up, down)


OFFSETS = (0, -1, 1, 2)


class SlabGather:
    def __init__(self, copies, own, out, z_first, halves):
        self.c, self.own, self.out, self.z_first, self.halves = copies, own, out, z_first, halves
        self.across, self.done = [], []
        self.cols = own.shape[-1] // 2

    def at(self, p, q):
        return (p, q) if self.z_first else (q, p)

    def ref(self, p, q, flip=False):
        return self.out.at[self.c.slab(*self.at(p, q), flip)]

    def half(self, ref, h):
        return ref.at[:, pl.ds(h * self.cols, self.cols)] if self.halves else ref

    def to(self, p, q, src, dst, land):
        return self.c.push(src, dst, self.c.device(*self.at(p, q)), land)

    def cross(self, p, q, src=None):
        ref = self.ref(p, q)
        target = self.c.device(0, 0, True)
        self.done.append(
            self.c.push(ref if src is None else src, ref, target, self.ref(p, q, True))
        )

    def spread(self, p, src=None):
        ref = self.ref(p, 0)
        src = ref if src is None else src
        ahead = self.to(0, 1, src, ref, self.ref(p, -1))
        behind = self.to(0, -1, src, ref, self.ref(p, 1))
        self.across.append((p, ahead, behind))

    def start(self):
        me = self.ref(0, 0)
        self.from_behind = self.to(1, 0, self.own, me, self.ref(-1, 0))
        self.from_ahead = self.to(-1, 0, self.own, me, self.ref(1, 0))

    def start_own(self):
        self.spread(0, self.own)
        self.cross(0, 0, self.own)

    def first(self):
        self.from_behind()
        ref, far = self.ref(-1, 0), self.ref(2, 0)
        self.far = [self.to(1, 0, self.half(ref, 0), self.half(ref, 0), self.half(far, 0))]
        self.spread(-1)
        self.cross(-1, 0)

    def second(self):
        self.from_ahead()
        if self.halves:
            ref, far = self.ref(1, 0), self.ref(2, 0)
            self.far.append(self.to(-1, 0, self.half(ref, 1), self.half(ref, 1), self.half(far, 1)))
        self.spread(1)
        self.cross(1, 0)

    def third(self):
        for wait in self.far:
            wait()
        self.spread(2)
        self.cross(2, 0)

    def ring(self, k):
        p, ahead, behind = self.across[k]
        if k == 0:
            self.last = []
        ahead()
        if k < 2:
            ref = self.ref(p, -1)
            self.last.append((p, self.to(0, 1, ref, ref, self.ref(p, 2))))
        self.cross(p, -1)
        behind()
        if k >= 2:
            ref = self.ref(p, 1)
            self.last.append((p, self.to(0, -1, ref, ref, self.ref(p, 2))))
        self.cross(p, 1)

    def end(self, k):
        p, wait = self.last[k]
        wait()
        self.cross(p, 2)

    def finish(self):
        for wait in self.done:
            wait()


def gather_kernel(
    x, dy, gate, up, down, table, xs, dys, tables, first, last, other, turned,
    basis_held, basis_turned, send, recv, local, basis_sems, turned_sems,
):
    c = Copies(send, recv)
    width = gate.shape[1]
    mine = c.slab(0, 0)
    sources = (gate, up, down)

    def columns(k, dy_, rows=None):
        at = pl.ds(pl.multiple_of(((c.row + dy_ + 4) % 4) * width, 128), width)
        whole = first.at[k] if k < 2 else last
        return whole.at[:, at] if rows is None else whole.at[rows, at]

    def other_columns(k, dy_):
        at = pl.ds(pl.multiple_of(((c.row + dy_ + 4) % 4) * width, 128), width)
        return other.at[k, :, at]

    here = [
        pltpu.make_async_copy(x, xs.at[mine], local.at[0]),
        pltpu.make_async_copy(dy, dys.at[mine], local.at[1]),
        pltpu.make_async_copy(table, tables.at[mine], local.at[2]),
    ]
    for k in range(3):
        here.append(pltpu.make_async_copy(sources[k], columns(k, 0), local.at[3 + k]))
    for copy in here:
        copy.start()
    meet(
        [c.device(0, 1), c.device(0, -1), c.device(1, 0), c.device(-1, 0)]
        + [c.device(0, 0, True), c.row_device(1), c.row_device(-1)]
    )
    parts = [
        SlabGather(c, table, tables, True, False),
        SlabGather(c, x, xs, True, True),
        SlabGather(c, dy, dys, False, True),
    ]
    for part in parts:
        part.start()
    basis_waits, basis_done, basis_far = [], [], []

    def basis_cross(k, dy_):
        if k < 2:
            ref = columns(k, dy_)
            src = sources[k] if dy_ == 0 else ref
            land = other_columns(k, dy_)
            basis_done.append(c.push(src, land, c.device(0, 0, True), land))

    for k in range(3):
        ref = columns(k, 0)
        basis_waits.append(
            (
                c.push(sources[k], ref, c.row_device(1), columns(k, -1)),
                c.push(sources[k], ref, c.row_device(-1), columns(k, 1)),
            )
        )
    for part in parts:
        part.start_own()
    for k in range(3):
        basis_cross(k, 0)
    for part in parts:
        part.first()
    for part in parts:
        part.second()
    for part in parts:
        part.third()
    ranks = gate.shape[0]
    stored = []

    def basis_load(k, dy_):
        at = pl.ds(pl.multiple_of(((c.row + dy_ + 4) % 4) * width, 128), width)
        src = sources[k] if dy_ == 0 else columns(k, dy_)
        copy = pltpu.make_async_copy(src, basis_held.at[k, :, at], basis_sems.at[k, dy_ % 4])
        copy.start()
        return copy

    def turn(k, dy_, load):
        load.wait()
        start = ((c.row + dy_ + 4) % 4) * width
        lanes = pl.ds(k * ranks, ranks)

        def step(i, carry):
            at = pl.ds(pl.multiple_of(start + i * 256, 256), 256)
            basis_turned[at, lanes] = basis_held[k, :, at].T
            return carry

        lax.fori_loop(0, width // 256, step, 0)
        at = pl.ds(pl.multiple_of(start, 256), width)
        copy = pltpu.make_async_copy(
            basis_turned.at[at, lanes], turned.at[at, lanes], turned_sems.at[k, dy_ % 4]
        )
        copy.start()
        stored.append(copy)

    own_loads = [basis_load(k, 0) for k in range(3)]
    for k in range(3):
        turn(k, 0, own_loads[k])
    half = ranks // 2
    waiting = []
    for step in range(4):
        for part in parts:
            part.ring(step)
        for args in waiting:
            turn(*args)
        waiting = []
        if step < 3:
            ahead, behind = basis_waits[step]
            low, high = pl.ds(0, half), pl.ds(half, half)
            ahead()
            ref = columns(step, -1, low)
            far = [c.push(ref, ref, c.row_device(1), columns(step, 2, low))]
            basis_cross(step, -1)
            behind()
            ref = columns(step, 1, high)
            far.append(c.push(ref, ref, c.row_device(-1), columns(step, 2, high)))
            basis_cross(step, 1)
            basis_far.append(far)
            waiting = [(step, d, basis_load(step, d)) for d in (-1, 1)]
    far_loads = []
    for k in range(3):
        for wait in basis_far[k]:
            wait()
        basis_cross(k, 2)
        far_loads.append(basis_load(k, 2))
    for k in (0, 2, 1, 3):
        for part in parts:
            part.end(k)
        if k < 3:
            turn(k, 2, far_loads[k])
    for part in parts:
        part.finish()
    for wait in basis_done:
        wait()
    for copy in here + stored:
        copy.wait()
    c.finish()


GATHER_COPIES = 32 + 32 + 31 + 20


def gather_inputs(x, dy, gate, up, down, table, n_ex):
    rows, width = gate.shape
    slabs = jax.ShapeDtypeStruct((n_ex,) + x.shape, BF)
    anywhere = pl.BlockSpec(memory_space=pl.ANY)
    return pl.pallas_call(
        gather_kernel,
        out_shape=[
            slabs,
            slabs,
            jax.ShapeDtypeStruct((n_ex,) + table.shape, FL),
            jax.ShapeDtypeStruct((2, rows, 4 * width), BF),
            jax.ShapeDtypeStruct((rows, 4 * width), BF),
            jax.ShapeDtypeStruct((2, rows, 4 * width), BF),
            jax.ShapeDtypeStruct((4 * width, 3 * rows), BF),
        ],
        in_specs=[anywhere] * 6,
        out_specs=[anywhere] * 7,
        scratch_shapes=[
            pltpu.VMEM((3, rows, 4 * width), BF),
            pltpu.VMEM((4 * width, 3 * rows), BF),
            pltpu.SemaphoreType.DMA((GATHER_COPIES,)),
            pltpu.SemaphoreType.DMA((GATHER_COPIES,)),
            pltpu.SemaphoreType.DMA((6,)),
            pltpu.SemaphoreType.DMA((3, 4)),
            pltpu.SemaphoreType.DMA((3, 4)),
        ],
        name="gather_inputs",
        compiler_params=pltpu.CompilerParams(
            collective_id=0, has_side_effects=True, vmem_limit_bytes=60 * MIB
        ),
    )(x, dy, gate, up, down, table)


def project_kernel(x, dy, turned, out):
    ranks = out.shape[1]
    ups = dot(x[...], turned[:, : 2 * ranks], 1, 0)
    downs = dot(dy[...], turned[:, 2 * ranks :], 1, 0)
    out[0] = ups[:, :ranks].T.astype(BF)
    out[1] = ups[:, ranks:].T.astype(BF)
    out[2] = downs.T.astype(BF)


def project(x, dy, turned):
    tokens, width = x.shape
    ranks = turned.shape[1] // 3
    step = 256
    some = pl.BlockSpec((step, width), lambda g: (g, 0))
    return pl.pallas_call(
        project_kernel,
        grid=(tokens // step,),
        out_shape=jax.ShapeDtypeStruct((3, ranks, tokens), BF),
        in_specs=[some, some, pl.BlockSpec(turned.shape, lambda g: (0, 0))],
        out_specs=pl.BlockSpec((3, ranks, step), lambda g: (0, 0, g)),
        name="project",
        compiler_params=pltpu.CompilerParams(vmem_limit_bytes=60 * MIB),
    )(x, dy, turned)


def home_kernel(
    rows, x, dy, bases, other,
    out, d_gate, d_up, d_down,
    paired, xb, db, bb, terms, far_in, near_in, turned, full, got, skipped, passed, kept, last,
    send, recv, loads,
):
    c = Copies(send, recv)
    width = d_gate.shape[1]
    near = (1, -1, 2)
    targets = [c.device(0, d) for d in near] + [c.device(d, 0) for d in near]
    targets += [c.device(0, 0, True), c.row_device(1), c.row_device(-1)]
    greet(targets)
    order = (2, 1, -1, 0)

    def load_rows(n):
        at = pl.ds(pl.multiple_of(((c.row + order[n] + 4) % 4) * width, 128), width)
        slot = n % 2
        copies = [
            pltpu.make_async_copy(x.at[:, at], xb.at[slot], loads.at[2 * slot]),
            pltpu.make_async_copy(dy.at[:, at], db.at[slot], loads.at[2 * slot + 1]),
        ]
        for copy in copies:
            copy.start()
        return copies

    def load_bases(n):
        at = pl.ds(n * width, width)
        slot = n % 2
        copies = [
            pltpu.make_async_copy(
                bases.at[:, :, at], bb.at[slot, 0], loads.at[4 + 2 * slot]
            ),
            pltpu.make_async_copy(other.at[:, :, at], bb.at[slot, 1], loads.at[5 + 2 * slot]),
        ]
        for copy in copies:
            copy.start()
        return copies

    flying = [load_rows(0), load_rows(1)]
    basis_flying = [load_bases(0), load_bases(1)]
    low, high = pl.ds(0, 64), pl.ds(64, 64)
    near_waits = [[], []]
    far_waits = [[], []]
    for n in range(4):
        for copy in flying[n]:
            copy.wait()
        slot = n % 2

        def columns(k, carry):
            at = pl.ds(pl.multiple_of(k * 256, 256), 256)
            ups = dot(rows[0:2].reshape(256, -1), xb[slot, :, at], 1, 0)
            downs = dot(rows[2], db[slot, :, at], 1, 0)
            if n < 3:
                terms[n, 0, :, at] = ups[:128].astype(BF)
                terms[n, 1, :, at] = ups[128:].astype(BF)
                terms[n, 2, :, at] = downs.astype(BF)
            else:
                d_gate[:, at] = ups[:128]
                d_up[:, at] = ups[128:]
                d_down[:, at] = downs
            return carry

        lax.fori_loop(0, width // 256, columns, 0)
        if n == 0:
            wait_for(targets)
            partner = c.push(rows.at[pl.ds(0, 2)], paired, c.device(0, 0, True), paired)
        if n < 2:
            flying.append(load_rows(n + 2))
        for k in range(3):
            if n == 0:
                land = far_in.at[0, k]
                far_waits[0].append(c.push(terms.at[0, k, low], land, c.row_device(1), land))
                land = far_in.at[1, k]
                far_waits[1].append(c.push(terms.at[0, k, high], land, c.row_device(-1), land))
            if n == 1:
                land = near_in.at[0, k, high]
                near_waits[0].append(c.push(terms.at[1, k, high], land, c.row_device(1), land))
            if n == 2:
                land = near_in.at[1, k, low]
                near_waits[1].append(c.push(terms.at[2, k, low], land, c.row_device(-1), land))
    partner()
    half_tokens = turned.shape[0]
    mine = pl.ds(pl.multiple_of(c.core * half_tokens, 128), half_tokens)
    for k in range(2):
        for n, source in enumerate((rows, paired)):
            at = pl.ds((2 * n + k) * 128, 128)
            turned[:, at] = source[k, :, mine].astype(FL).T.astype(BF)
    tok = full.shape[2]
    place = (c.z, c.x)
    got_waits = [{}, {}]
    cross_waits = []
    via_ahead, via_behind = (1, -1), (2, 0)

    def group(h, d, b):
        if h == 0:
            return ((c.z + b + 4) % 4) * 4 + (c.x + d + 4) % 4
        return ((c.z + d + 4) % 4) * 4 + (c.x + b + 4) % 4

    def along(h, d):
        return c.device(0, d) if h == 0 else c.device(d, 0)

    def cross_far(h):
        waits = []
        for d, which in ((1, via_ahead), (-1, via_behind)):
            for k, b in enumerate(which):
                land = skipped.at[h, d % 3 - 1, k]
                waits.append((d, b, k, c.push(full.at[h, group(h, 2, b)], land, along(h, d), land)))
        for d, which in ((1, via_behind), (-1, via_ahead)):
            for b in which:
                cross_push(h, d, b)
        return waits

    def cross_push(h, d, b):
        land = got.at[h, d % 3 - 1, b % 4]
        wait = c.push(full.at[h, group(h, d, b)], land, along(h, d), land)
        got_waits[h].setdefault(b, []).append(wait)

    def cross_near(h):
        for d, b, k, wait in cross_waits[h]:
            wait()
            slab = group(h, d, b)
            more = full[h, slab].astype(FL) + skipped[h, d % 3 - 1, k].astype(FL)
            full[h, slab] = more.astype(BF)
            cross_push(h, d, b)

    for n in range(4):
        for copy in basis_flying[n]:
            copy.wait()
        slot, h = n % 2, n // 2

        def token_columns(k, carry):
            at = pl.ds(pl.multiple_of(k * 256, 256), 256)
            to = pl.ds(pl.multiple_of((n % 2) * width + k * 256, 256), 256)
            both = jnp.concatenate(
                [bb[slot, s, k2, :, at] for s in range(2) for k2 in range(2)], axis=0
            )
            sums = dot(turned[...], both, 1, 0)
            for s in range(16):
                full[h, s, :, to] = sums[s * tok : (s + 1) * tok].astype(BF)
            return carry

        lax.fori_loop(0, width // 256, token_columns, 0)
        if n < 2:
            basis_flying.append(load_bases(n + 2))
        if n % 2 == 1:
            cross_waits.append(cross_far(h))
    for h in range(2):
        cross_near(h)
    for k in range(3):
        far_waits[0][k]()
        terms[1, k, low] = (terms[1, k, low].astype(FL) + far_in[0, k].astype(FL)).astype(BF)
        land = near_in.at[0, k, low]
        near_waits[0].append(c.push(terms.at[1, k, low], land, c.row_device(1), land))
        far_waits[1][k]()
        terms[2, k, high] = (terms[2, k, high].astype(FL) + far_in[1, k].astype(FL)).astype(BF)
        land = near_in.at[1, k, high]
        near_waits[1].append(c.push(terms.at[2, k, high], land, c.row_device(-1), land))
    last_waits = [[], []]
    for step, b in enumerate((1, -1, 2, 0)):
        for h in range(2):
            for wait in got_waits[h][b]:
                wait()
            slab = group(h, 0, b)
            target = c.device(b, 0) if h == 0 else c.device(0, b)
            total = full[h, slab].astype(FL)
            for side in range(2):
                total = total + got[h, side, b % 4].astype(FL)
            if b == 0:
                kept[h] = total
            else:
                passed[h, step] = total.astype(BF)
                land = last.at[h, step]
                last_waits[h].append(c.push(passed.at[h, step], land, target, land))
    for h in range(2):
        for wait in last_waits[h]:
            wait()
        total = kept[h]
        for step in range(3):
            total = total + last[h, step].astype(FL)
        out[:, h * 2 * width : (h + 1) * 2 * width] = total.astype(BF)
    for side in range(2):
        for wait in near_waits[side]:
            wait()
    for k, ref in enumerate((d_gate, d_up, d_down)):
        ref[...] = ref[...] + near_in[0, k].astype(FL) + near_in[1, k].astype(FL)
    c.finish()


HOME_COPIES = 1 + 18 + 24 + 6


def send_home(rows, x, dy, bases, other, tok):
    kinds, ranks, tokens = rows.shape
    full_width = x.shape[1]
    width = full_width // 4
    half = full_width // 2
    anywhere = pl.BlockSpec(memory_space=pl.ANY)
    vmem = pl.BlockSpec(memory_space=pltpu.VMEM)
    basis = jax.ShapeDtypeStruct((ranks, width), FL)
    return pl.pallas_call(
        home_kernel,
        out_shape=[jax.ShapeDtypeStruct((tok, full_width), BF), basis, basis, basis],
        in_specs=[vmem] + [anywhere] * 4,
        out_specs=[vmem] * 4,
        scratch_shapes=[
            pltpu.VMEM((2, ranks, tokens), BF),
            pltpu.VMEM((2, tokens, width), BF),
            pltpu.VMEM((2, tokens, width), BF),
            pltpu.VMEM((2, 2, 2, ranks, width), BF),
            pltpu.VMEM((3, kinds, ranks, width), BF),
            pltpu.VMEM((2, kinds, ranks // 2, width), BF),
            pltpu.VMEM((2, kinds, ranks, width), BF),
            pltpu.VMEM((tokens // 2, 4 * ranks), BF),
            pltpu.VMEM((2, 16, tok, half), BF),
            pltpu.VMEM((2, 2, 4, tok, half), BF),
            pltpu.VMEM((2, 2, 2, tok, half), BF),
            pltpu.VMEM((2, 3, tok, half), BF),
            pltpu.VMEM((2, tok, half), FL),
            pltpu.VMEM((2, 3, tok, half), BF),
            pltpu.SemaphoreType.DMA((HOME_COPIES,)),
            pltpu.SemaphoreType.DMA((HOME_COPIES,)),
            pltpu.SemaphoreType.DMA((8,)),
        ],
        name="send_home",
        compiler_params=pltpu.CompilerParams(
            collective_id=1, has_side_effects=True, vmem_limit_bytes=60 * MIB
        ),
    )(rows, x, dy, bases, other)


def slot_tables(route_ids, route_weight, cells):
    flat = route_ids.reshape(-1)
    pairs = flat.shape[0]
    at = jnp.arange(pairs, dtype=jnp.int32)
    earlier = (flat[:, None] == flat[None, :]) & (at[None, :] < at[:, None])
    slot = jnp.sum(earlier.astype(jnp.int32), axis=1)
    placed = (flat * 2 + slot)[:, None] == jnp.arange(cells, dtype=jnp.int32)[None, :]
    token = at // route_ids.shape[1] + 1
    cell_token = jnp.sum(jnp.where(placed, token[:, None], 0), axis=0)
    cell_weight = jnp.sum(
        jnp.where(placed, route_weight.reshape(-1)[:, None].astype(FL), 0.0), axis=0
    )
    return slot, cell_token, cell_weight


def body(
    tokens,
    grad_out,
    route_ids,
    route_weight,
    cluster_of,
    gate_basis,
    up_basis,
    down_basis,
    gate_factor,
    up_factor,
    down_factor,
):
    n_dp = lax.axis_size("dp")
    n_ex = lax.axis_size("expert")
    tok_rows, width = tokens.shape
    local = gate_factor.shape[0]
    lane_rows = local * 2
    cells = n_ex * lane_rows
    clusters, rank, part_width = gate_basis.shape
    plane_tokens = n_ex * tok_rows
    all_rank = n_ex * rank

    slot, cell_token, cell_weight = slot_tables(route_ids, route_weight, cells)
    table = jnp.concatenate([cell_token.astype(FL), cell_weight]).reshape(4, 128)
    flat = (clusters * rank, part_width)
    x_all, dy_all, tables, gate_up, _, other, turned = gather_inputs(
        tokens,
        grad_out,
        gate_basis.reshape(flat),
        up_basis.reshape(flat),
        down_basis.reshape(flat),
        table,
        n_ex,
    )
    x_all = x_all.reshape(plane_tokens, width)
    dy_all = dy_all.reshape(plane_tokens, width)
    tables = tables.reshape(n_ex, 2, n_ex, local, 2)
    tables = tables.transpose(1, 2, 3, 0, 4).reshape(2, n_ex, n_ex * lane_rows)
    block = (jnp.arange(n_ex * lane_rows, dtype=jnp.int32) // 2) % n_ex
    named = tables[0].astype(jnp.int32)
    slots = jnp.where(named > 0, named - 1 + tok_rows * block[None, :], -1)
    weights = tables[1]
    cluster = cluster_of.reshape(n_ex, local)[:, 0]

    rows = project(x_all, dy_all, turned)
    member = cluster[:, None] == jnp.arange(clusters, dtype=jnp.int32)[None, :]
    home, dots, kept_rows, kept_units = middle(
        member.astype(FL), rows, slots, weights, gate_factor, up_factor, down_factor, n_dp
    )
    summed = combine(cluster, home, slots, weights, clusters, plane_tokens)

    z, x, core = plane_place()
    flat = route_ids.reshape(-1)
    lane = jnp.arange(128, dtype=jnp.int32)
    wanted = jnp.arange(4, dtype=jnp.int32)
    wanted = (wanted // 2) * 64 + slab_of(z, x, core) * 2 + wanted % 2
    own = wanted[:, None, None] == lane[None, None, :]
    dots = jnp.sum(jnp.where(own, dots.reshape(1, n_ex * 2, 128), 0.0), axis=2)
    hit = (flat % 2 * 2 + slot)[:, None, None] == jnp.arange(4, dtype=jnp.int32)[None, :, None]
    hit = hit & ((flat // 2)[:, None, None] == jnp.arange(n_ex * 2, dtype=jnp.int32))
    scores = jnp.sum(jnp.where(hit, dots[None], 0.0), axis=(1, 2))
    grad_route = scores.reshape(route_ids.shape) / route_weight.astype(FL)
    passing = send_home(summed, x_all, dy_all, gate_up, other, tok_rows)
    d_gate_factor, d_up_factor, d_down_factor, grad_tokens, *terms = factor_grads(
        kept_rows, kept_units, passing
    )
    shape = gate_basis.shape
    return (
        grad_tokens,
        grad_route,
        terms[0].reshape(shape),
        terms[1].reshape(shape),
        terms[2].reshape(shape),
        d_gate_factor,
        d_up_factor,
        d_down_factor,
    )


def solution(mesh):
    rows = P(("dp", "expert"), None)
    basis = P(None, "expert", "dp")
    factor = P("expert", None, "dp")
    low = P("expert", "dp", None)
    in_specs = (rows, rows, rows, rows, P(), basis, basis, basis, factor, factor, low)
    out_specs = (rows, rows, basis, basis, basis, factor, factor, low)
    return jax.shard_map(body, mesh=mesh, in_specs=in_specs, out_specs=out_specs, check_vma=False)
```
